32 devices in a mesh: batch: 8 (over z, x), section: 4 (over y, core).
Axes of the slice: x: 2, y: 2, z: 4, core: 2. Of those that a mesh axis runs over, the one named last changes fastest.
Arguments:
- stem_input: float32 [64, 576, 1024], P(('batch', 'section')), may hold values from -6 to 6
- image_class: int32 [64], P(('batch', 'section')), may hold values 0 or 1
- owner: int32 [64], P('batch'), may hold values from 0 to 3, as said below
- conv_in_weight: bfloat16 [1024, 256], replicated, may hold values from -0.1875 to 0.1875
- first_gain: float32 [256], replicated, may hold values from 0.5 to 1.5
- first_bias: float32 [256], replicated, may hold values from -1.75 to 1.75
- conv_mid_weight: bfloat16 [9, 256, 256], replicated, may hold values from -0.125 to 0.125
- second_gain: float32 [256], replicated, may hold values from 0.5 to 1.5
- second_bias: float32 [256], replicated, may hold values from -1.75 to 1.75
- conv_out_weight: bfloat16 [256, 1024], replicated, may hold values from -0.375 to 0.375
- third_gain: float32 [1024], replicated, may hold values from 0.5 to 1.5
- third_bias: float32 [1024], replicated, may hold values from -1.75 to 1.75
- embed_weight: bfloat16 [1024, 768], replicated, may hold values from -0.1875 to 0.1875
- embed_bias: float32 [768], replicated, may hold values from -3 to 3
- position_table: bfloat16 [576, 768], replicated, may hold values from -3 to 3
- attn_gain: float32 [768], replicated, may hold values from 0.5 to 1.5
- attn_bias: float32 [768], replicated, may hold values from -1.75 to 1.75
- joint_weight: bfloat16 [768, 2304], replicated, may hold values from -0.21875 to 0.21875
- query_bias: float32 [768], replicated, may hold values from -3 to 3
- value_bias: float32 [768], replicated, may hold values from -3 to 3
- mix_weight: bfloat16 [768, 768], replicated, may hold values from -0.875 to 0.875
- mix_bias: float32 [768], replicated, may hold values from -1.75 to 1.75
- mlp_gain: float32 [768], replicated, may hold values from 0.5 to 1.5
- mlp_bias: float32 [768], replicated, may hold values from -1.75 to 1.75
- expand_weight: bfloat16 [768, 3072], replicated, may hold values from -0.21875 to 0.21875
- expand_bias: float32 [3072], replicated, may hold values from -3 to 3
- shrink_weight: bfloat16 [3072, 768], replicated, may hold values from -0.109375 to 0.109375
- shrink_bias: float32 [768], replicated, may hold values from -1.75 to 1.75
- cotangent: bfloat16 [32, 4, 576, 768], P(('batch', 'section')), may hold values from -6 to 6
Outputs:
- block_output: bfloat16 [32, 4, 576, 768], P(('batch', 'section'))
- input_grad: float32 [64, 576, 1024], P(('batch', 'section'))
- grad_conv_in: float32 [262144], P(('batch', 'section'))
- grad_first_gain: float32 [256], replicated
- grad_first_bias: float32 [256], replicated
- grad_conv_mid: float32 [589824], P(('batch', 'section'))
- grad_second_gain: float32 [256], replicated
- grad_second_bias: float32 [256], replicated
- grad_conv_out: float32 [262144], P(('batch', 'section'))
- grad_third_gain: float32 [1024], replicated
- grad_third_bias: float32 [1024], replicated
- grad_embed_weight: float32 [786432], P(('batch', 'section'))
- grad_embed_bias: float32 [768], replicated
- grad_position_table: float32 [442368], P(('batch', 'section'))
- grad_attn_gain: float32 [768], replicated
- grad_attn_bias: float32 [768], replicated
- grad_joint_weight: float32 [1769472], P(('batch', 'section'))
- grad_query_bias: float32 [768], replicated
- grad_value_bias: float32 [768], replicated
- grad_mix_weight: float32 [589824], P(('batch', 'section'))
- grad_mix_bias: float32 [768], replicated
- grad_mlp_gain: float32 [768], replicated
- grad_mlp_bias: float32 [768], replicated
- grad_expand_weight: float32 [2359296], P(('batch', 'section'))
- grad_expand_bias: float32 [3072], replicated
- grad_shrink_weight: float32 [2359296], P(('batch', 'section'))
- grad_shrink_bias: float32 [768], replicated
The draws below stay inside these ranges and needn't reach their ends.
Inputs may be any that keep to these rules, and one draw needn't show every extreme that they name: `image_class`: 1 marks an image of 24 x 24 patches, 0 one of 14 x 14 patches in the grid's top-left corner; the other cells are padding. `owner`: entry b * 4 * 2 + s * 2 + j is the section index that runs the block of image j of section index s at batch index b. Within one batch index every section index is named exactly 2 times, and one section index names the same section index at most 1 times, exactly 1 times for some pair.
All inputs are finite; a program needn't handle non-finite values. No bound on the sum of `image_class` on one device may be relied on, other than what follows from the above.
Results may differ from the reference program's by a relative error of at most 0.017.
The reference program's roundings to bfloat16 on the way count: a program that leaves them out, or rounds other values in their place, can miss the bound.
Values may be sent and summed in bfloat16 or wider, within the bound.
No kernel may reach another device: no remote copies, remote signals or barrier semaphores. Data moves between devices by JAX's collectives and lax.ppermute only.
A program may use at most 320 MiB of HBM per device.

```python
import jax
import jax.numpy as jnp
from jax import lax

C_IN = 1024
C_MID = 256
D = 768
HEADS = 12
HEAD_DIM = 64
FF = 3072
GROUPS = 32
SIDE = 24
SIDE_SMALL = 14
IMG_DEV = 2
CELLS = 576
CAP = 1
SLOTS = 4
IMAGES = 64
N_SECTION = 4
DEVICES = 32


def draw_owner(key, part):
    key = jax.random.fold_in(key, 7)
    groups = IMAGES // (N_SECTION * IMG_DEV)

    def one_group(index):
        inner = jax.random.fold_in(key, index)
        order = jax.random.permutation(jax.random.fold_in(inner, 1), N_SECTION).astype(jnp.int32)
        offset = jax.random.permutation(jax.random.fold_in(inner, 2), N_SECTION).astype(jnp.int32)
        entries = jnp.arange(N_SECTION * IMG_DEV, dtype=jnp.int32)
        source = entries // IMG_DEV
        local_index = entries % IMG_DEV
        return order[(source + offset[local_index % N_SECTION]) % N_SECTION]
    return jax.vmap(one_group)(jnp.arange(groups, dtype=jnp.int32)).reshape(-1).astype(jnp.int32)


def with_ends(values, own_key, low, largest):
    shape = values.shape
    spot = [jax.random.randint(jax.random.fold_in(own_key, axis), (), 0, shape[axis]) for axis in range(len(shape))]
    values = values.at[tuple(spot)].set(low)
    longest = shape.index(max(shape))
    spot[longest] = (spot[longest] + 1) % shape[longest]
    return values.at[tuple(spot)].set(largest)


def steps_of(own_key, shape, cuts, least, top_value):
    loudness = 1.0
    for position, blocks in cuts:
        draws = jax.random.uniform(jax.random.fold_in(jax.random.fold_in(own_key, 6), position), (blocks,), jnp.float32, least / len(cuts), top_value / len(cuts))
        loudness = loudness * jnp.repeat(jnp.exp(draws), shape[position] // blocks).reshape((-1,) + (1,) * (len(shape) - 1 - position))
    return loudness


def scatter_about(own_key, shape, scale, most, cuts=(), held_as=jnp.bfloat16):
    loudness = steps_of(own_key, shape, cuts, -0.22, 0.18) if cuts else 1.0
    drawn = jax.random.normal(own_key, shape, jnp.float32) * scale * loudness
    return jnp.minimum(jnp.maximum(drawn, -most), most).astype(held_as)


def setup_inputs(seed: int = 0) -> dict:
    keys = jax.random.split(jax.random.key(seed), 30)
    stem_input = scatter_about(keys[0], (IMAGES, CELLS, C_IN), 1.0, 6.0, ((0, 32),), jnp.float32)
    image_class = with_ends((jax.random.randint(keys[1], (IMAGES,), 0, 2) < 1).astype(jnp.int32), jax.random.fold_in(keys[1], 1), 0, 1)
    owner = draw_owner(jax.random.fold_in(keys[29], 71), 0)
    conv_in_weight = scatter_about(keys[3], (C_IN, C_MID), C_IN ** -0.5, 0.1875)
    first_gain = jnp.clip(1.0 + 0.1 * jax.random.normal(keys[4], (C_MID,), jnp.float32), 0.5, 1.5)
    first_bias = scatter_about(keys[5], (C_MID,), 0.3, 1.75, (), jnp.float32)
    conv_mid_weight = scatter_about(keys[6], (9, C_MID, C_MID), (9 * C_MID) ** -0.5, 0.125)
    second_gain = jnp.clip(1.0 + 0.1 * jax.random.normal(keys[7], (C_MID,), jnp.float32), 0.5, 1.5)
    second_bias = scatter_about(keys[8], (C_MID,), 0.3, 1.75, (), jnp.float32)
    conv_out_weight = scatter_about(keys[9], (C_MID, C_IN), C_MID ** -0.5, 0.375)
    third_gain = jnp.clip(1.0 + 0.1 * jax.random.normal(keys[10], (C_IN,), jnp.float32), 0.5, 1.5)
    third_bias = scatter_about(keys[11], (C_IN,), 0.3, 1.75, (), jnp.float32)
    embed_weight = scatter_about(keys[12], (C_IN, D), C_IN ** -0.5, 0.1875)
    embed_bias = scatter_about(keys[13], (D,), 0.5, 3.0, (), jnp.float32)
    position_table = scatter_about(keys[14], (CELLS, D), 0.5, 3.0)
    attn_gain = jnp.clip(1.0 + 0.1 * jax.random.normal(keys[15], (D,), jnp.float32), 0.5, 1.5)
    attn_bias = scatter_about(keys[16], (D,), 0.3, 1.75, (), jnp.float32)
    joint_weight = scatter_about(keys[17], (D, 3 * D), D ** -0.5, 0.21875)
    query_bias = scatter_about(keys[18], (D,), 0.5, 3.0, (), jnp.float32)
    value_bias = scatter_about(keys[19], (D,), 0.5, 3.0, (), jnp.float32)
    mix_weight = scatter_about(keys[20], (D, D), (D // 16) ** -0.5, 0.875)
    mix_bias = scatter_about(keys[21], (D,), 0.3, 1.75, (), jnp.float32)
    mlp_gain = jnp.clip(1.0 + 0.1 * jax.random.normal(keys[22], (D,), jnp.float32), 0.5, 1.5)
    mlp_bias = scatter_about(keys[23], (D,), 0.3, 1.75, (), jnp.float32)
    expand_weight = scatter_about(keys[24], (D, FF), D ** -0.5, 0.21875)
    expand_bias = scatter_about(keys[25], (FF,), 0.5, 3.0, (), jnp.float32)
    shrink_weight = scatter_about(keys[26], (FF, D), FF ** -0.5, 0.109375)
    shrink_bias = scatter_about(keys[27], (D,), 0.3, 1.75, (), jnp.float32)
    cotangent = scatter_about(keys[28], (DEVICES, SLOTS, CELLS, D), 1.0, 6.0, ((0, 32),))
    return {"stem_input": stem_input, "image_class": image_class, "owner": owner, "conv_in_weight": conv_in_weight, "first_gain": first_gain, "first_bias": first_bias, "conv_mid_weight": conv_mid_weight, "second_gain": second_gain, "second_bias": second_bias, "conv_out_weight": conv_out_weight, "third_gain": third_gain, "third_bias": third_bias, "embed_weight": embed_weight, "embed_bias": embed_bias, "position_table": position_table, "attn_gain": attn_gain, "attn_bias": attn_bias, "joint_weight": joint_weight, "query_bias": query_bias, "value_bias": value_bias, "mix_weight": mix_weight, "mix_bias": mix_bias, "mlp_gain": mlp_gain, "mlp_bias": mlp_bias, "expand_weight": expand_weight, "expand_bias": expand_bias, "shrink_weight": shrink_weight, "shrink_bias": shrink_bias, "cotangent": cotangent}


highest = lax.Precision.HIGHEST

@jax.custom_vjp
def low(v):
    return lax.optimization_barrier(v.astype(jnp.bfloat16)).astype(jnp.float32)

@jax.custom_vjp
def low_back(v):
    return v

def low_keep(v):
    return (low(v), None)

def low_pass(kept, grad):
    return (grad,)

def back_keep(v):
    return (v, None)

def back_low(kept, grad):
    return (low(grad),)
low.defvjp(low_keep, low_pass)
low_back.defvjp(back_keep, back_low)

def cell_validity(image_class):
    grid_cells = jnp.arange(SIDE * SIDE, dtype=jnp.int32)
    corner = (grid_cells // SIDE < SIDE_SMALL) & (grid_cells % SIDE < SIDE_SMALL)
    return jnp.where((image_class[:, None] == 1) | corner[None, :], 1.0, 0.0).astype(jnp.float32)

def standardize(weight):
    lead_axes = tuple(range(weight.ndim - 1))
    centred = weight - lax.optimization_barrier(jnp.mean(weight, axis=lead_axes, keepdims=True))
    spread = lax.optimization_barrier(jnp.mean(centred * centred, axis=lead_axes, keepdims=True))
    return centred * lax.rsqrt(spread + 1e-05)

def group_norm(values, gain, bias, validity):
    images, grid_cells, channels = values.shape
    per_group = channels // GROUPS
    grouped = values.reshape(images, grid_cells, GROUPS, per_group)
    weights = validity[:, :, None, None]
    total = lax.optimization_barrier(jnp.sum(weights, axis=(1, 3), keepdims=True)) * per_group
    centre = lax.optimization_barrier(jnp.sum(grouped * weights, axis=(1, 3), keepdims=True)) / total
    centred = (grouped - centre) * weights
    spread = lax.optimization_barrier(jnp.sum(centred * centred, axis=(1, 3), keepdims=True)) / total
    normed = ((grouped - centre) * lax.rsqrt(spread + 1e-05)).reshape(images, grid_cells, channels)
    return normed * gain + bias

def layer_norm(values, gain, bias):
    centre = lax.optimization_barrier(jnp.mean(values, axis=-1, keepdims=True))
    centred = values - centre
    spread = lax.optimization_barrier(jnp.mean(centred * centred, axis=-1, keepdims=True))
    return centred * lax.rsqrt(spread + 1e-06) * gain + bias

def neighbours(values):
    images, grid_cells, channels = values.shape
    grid = values.reshape(images, SIDE, SIDE, channels)
    padded = jnp.pad(grid, ((0, 0), (1, 1), (1, 1), (0, 0)))
    pieces = [padded[:, row_shift:row_shift + SIDE, col_shift:col_shift + SIDE, :] for row_shift in range(3) for col_shift in range(3)]
    return jnp.concatenate(pieces, axis=-1).reshape(images, grid_cells, 9 * channels)

def apply_rows(values, weight):
    images, grid_cells, inner = values.shape
    flat_rows = values.reshape(images * grid_cells, inner)
    return jnp.dot(flat_rows, weight, precision=highest, preferred_element_type=jnp.float32).reshape(images, grid_cells, weight.shape[1])

def gelu_exact(values):
    return jax.nn.gelu(values, approximate=False)

def attend(packed):
    query, key_rows, value_rows, validity = packed
    grid_cells = query.shape[0]
    query_heads = query.reshape(grid_cells, HEADS, HEAD_DIM)
    key_heads = key_rows.reshape(grid_cells, HEADS, HEAD_DIM)
    value_heads = value_rows.reshape(grid_cells, HEADS, HEAD_DIM)
    scores = jnp.einsum('qhd,khd->hqk', query_heads, key_heads, precision=highest) * HEAD_DIM ** (-0.5)
    scores = low_back(scores)
    scores = jnp.where(validity[None, None, :] > 0, scores, -1000000000.0)
    top = lax.optimization_barrier(jnp.max(scores, axis=-1, keepdims=True))
    weights = jnp.exp(scores - top)
    probs = low(weights / lax.optimization_barrier(jnp.sum(weights, axis=-1, keepdims=True)))
    mixed = jnp.einsum('hqk,khd->qhd', probs, value_heads, precision=highest)
    return mixed.reshape(grid_cells, HEADS * HEAD_DIM)

def forward(stem_input, validity, params):
    conv_in, first_gain, first_bias, conv_mid, second_gain, second_bias, conv_out, third_gain, third_bias, embed_weight, embed_bias, position_table, attn_gain, attn_bias, joint_weight, query_bias, value_bias, mix_weight, mix_bias, mlp_gain, mlp_bias, expand_weight, expand_bias, shrink_weight, shrink_bias = params
    keep_cells = validity[:, :, None]
    inputs = stem_input * keep_cells
    first = low_back(apply_rows(low(inputs), low(standardize(conv_in))))
    act_one = low(gelu_exact(group_norm(first, first_gain, first_bias, validity)) * keep_cells)
    mid_std = low(standardize(conv_mid)).reshape(9 * C_MID, C_MID)
    second = low_back(apply_rows(neighbours(act_one), mid_std))
    act_two = low(gelu_exact(group_norm(second, second_gain, second_bias, validity)) * keep_cells)
    third = low_back(apply_rows(act_two, low(standardize(conv_out))))
    stem = low(gelu_exact(inputs + group_norm(third, third_gain, third_bias, validity)) * keep_cells)
    tokens = (apply_rows(stem, embed_weight) + embed_bias + position_table[None]) * keep_cells
    tokens = low_back(low(tokens))
    normed = low(layer_norm(tokens, attn_gain, attn_bias))
    joint = low_back(apply_rows(normed, joint_weight))
    query = low(joint[:, :, :D] + query_bias)
    key_rows = low(joint[:, :, D:2 * D])
    value_rows = low(joint[:, :, 2 * D:] + value_bias)
    mixed = lax.map(jax.checkpoint(attend), (query, key_rows, value_rows, validity))
    mixed = low(low_back(mixed))
    resid = tokens + low_back(apply_rows(mixed, mix_weight)) + mix_bias
    normed_two = low(layer_norm(resid, mlp_gain, mlp_bias))
    hidden = low(gelu_exact(low_back(apply_rows(normed_two, expand_weight)) + expand_bias))
    return (resid + low_back(apply_rows(hidden, shrink_weight)) + shrink_bias) * keep_cells

def placement_of(owner):
    source_owner = owner.reshape(-1, IMG_DEV)
    local_index = jnp.arange(IMG_DEV, dtype=jnp.int32)
    earlier = local_index[None, :] < local_index[:, None]
    same_dest = source_owner[:, :, None] == source_owner[:, None, :]
    rank = lax.optimization_barrier(jnp.sum(same_dest & earlier[None], axis=2)).astype(jnp.int32).reshape(-1)
    image_index = jnp.arange(owner.shape[0], dtype=jnp.int32)
    device = image_index // (N_SECTION * IMG_DEV) * N_SECTION + owner
    source = image_index // IMG_DEV % N_SECTION
    return (device.astype(jnp.int32), (source * CAP + rank).astype(jnp.int32))

def reference(stem_input, image_class, owner, conv_in_weight, first_gain, first_bias, conv_mid_weight, second_gain, second_bias, conv_out_weight, third_gain, third_bias, embed_weight, embed_bias, position_table, attn_gain, attn_bias, joint_weight, query_bias, value_bias, mix_weight, mix_bias, mlp_gain, mlp_bias, expand_weight, expand_bias, shrink_weight, shrink_bias, cotangent):
    validity = cell_validity(image_class)
    params = tuple((item.astype(jnp.float32) for item in (conv_in_weight, first_gain, first_bias, conv_mid_weight, second_gain, second_bias, conv_out_weight, third_gain, third_bias, embed_weight, embed_bias, position_table, attn_gain, attn_bias, joint_weight, query_bias, value_bias, mix_weight, mix_bias, mlp_gain, mlp_bias, expand_weight, expand_bias, shrink_weight, shrink_bias)))

    def run(inputs, weights):
        return forward(inputs, validity, weights)
    block_rows, pullback = jax.vjp(run, stem_input, params)
    device, slot = placement_of(owner)
    grad_inputs, grads = pullback(cotangent[device, slot].astype(jnp.float32))
    block_output = jnp.zeros(cotangent.shape, jnp.bfloat16).at[device, slot].set(block_rows.astype(jnp.bfloat16))
    return (block_output, grad_inputs, grads[0].reshape(-1), grads[1], grads[2], grads[3].reshape(-1), grads[4], grads[5], grads[6].reshape(-1), grads[7], grads[8], grads[9].reshape(-1), grads[10], grads[11].reshape(-1), grads[12], grads[13], grads[14].reshape(-1), grads[15], grads[16], grads[17].reshape(-1), grads[18], grads[19], grads[20], grads[21].reshape(-1), grads[22], grads[23].reshape(-1), grads[24])
```

```python
import jax
import jax.numpy as jnp
from jax import lax
from jax.experimental import pallas as pl
from jax.experimental.pallas import tpu as pltpu
from jax.sharding import PartitionSpec as P

HEADS = 12
GROUPS = 32
SIDE = 24
SIDE_SMALL = 14
LANES = 128
MIB = 1024 * 1024
BOTH = ("batch", "section")

f32 = jnp.float32
bf16 = jnp.bfloat16


def dot_nn(left, right):
    return jnp.dot(left, right, preferred_element_type=f32)


def dot_tn(left, right):
    return lax.dot_general(left, right, (((0,), (0,)), ((), ())), preferred_element_type=f32)


def dot_nt(left, right):
    return lax.dot_general(left, right, (((1,), (1,)), ((), ())), preferred_element_type=f32)


def fold(values):
    rows, columns = values.shape
    return jnp.sum(values.reshape(rows // 8, 8, columns), axis=0)


def total(values):
    return jnp.sum(values, axis=0, keepdims=True)


def spread_lanes(mask, columns):
    return jnp.concatenate([mask] * (columns // LANES), axis=1)


def cdf_pdf(values):
    bell = jnp.exp(-0.5 * (values * values))
    t = 1.0 / (1.0 + 0.23164189 * jnp.abs(values))
    tail = (
        ((((0.5307027145 * t - 0.7265760135) * t + 0.7107068705) * t - 0.142248368) * t + 0.127414796)
        * t
        * bell
    )
    return jnp.where(values < 0.0, tail, 1.0 - tail), bell * 0.3989422804014327


def group_total(row, per_group):
    channels = row.shape[1]
    rows = jnp.broadcast_to(row, (8, channels))
    lane = lax.broadcasted_iota(jnp.int32, (8, LANES), 1)
    parts = []
    for k in range(channels // LANES):
        part = rows[:, k * LANES : (k + 1) * LANES]
        step = 1
        while step < per_group:
            up = pltpu.roll(part, LANES - step, 1)
            down = pltpu.roll(part, step, 1)
            part = part + jnp.where((lane & step) == 0, up, down)
            step *= 2
        parts.append(part)
    return jnp.concatenate(parts, axis=1)[0:1]


def cell_grid(cells):
    cell = lax.broadcasted_iota(jnp.int32, (cells, LANES), 0).astype(f32)
    row = jnp.floor((cell + 0.5) * (1.0 / SIDE))
    return row, cell - row * SIDE


def validity_mask(image_class, cells):
    row, column = cell_grid(cells)
    corner = jnp.where((row < SIDE_SMALL) & (column < SIDE_SMALL), 1.0, 0.0)
    return jnp.where(image_class == 1, 1.0, corner)


def valid_count(image_class):
    return jnp.where(image_class == 1, float(SIDE * SIDE), float(SIDE_SMALL * SIDE_SMALL))


def rows_at(index, size):
    return pl.ds(pl.multiple_of(index * size, size), size)


def fill_columns(grid_value, padded, columns, sign):
    cells, channels = grid_value.shape
    _, column = cell_grid(cells)
    has_left = spread_lanes(jnp.where(column > 0.5, 1.0, 0.0), channels)
    has_right = spread_lanes(jnp.where(column < SIDE - 1.5, 1.0, 0.0), channels)
    zeros = jnp.zeros((SIDE, channels), f32)
    shifted = (
        pltpu.roll(grid_value, 1, 0) * has_left,
        grid_value,
        pltpu.roll(grid_value, cells - 1, 0) * has_right,
    )
    for k in range(3):
        padded[k, 0:SIDE, :] = zeros
        padded[k, SIDE + cells : 2 * SIDE + cells, :] = zeros
        padded[k, SIDE : SIDE + cells, :] = shifted[k]
    for row_shift in range(3):
        for column_shift in range(3):
            tap = row_shift * 3 + column_shift
            down = row_shift if sign > 0 else 2 - row_shift
            across = column_shift if sign > 0 else 2 - column_shift
            columns[:, tap * channels : (tap + 1) * channels] = padded[
                across, down * SIDE : down * SIDE + cells, :
            ].astype(bf16)


def standardized(weight):
    rows = weight.shape[0]
    centred = weight - total(weight) * (1.0 / rows)
    spread = total(centred * centred) * (1.0 / rows)
    scale = lax.rsqrt(spread + 1e-05)
    return centred * scale, scale


def standardize_back(weight, grad):
    rows = weight.shape[0]
    normal, scale = standardized(weight)
    grad_mean = total(grad) * (1.0 / rows)
    inner = total(grad * normal) * (1.0 / rows)
    return scale * (grad - grad_mean - normal * inner)


def stem_forward_kernel(
    class_ref,
    x_ref,
    w_in_ref,
    w_mid_ref,
    w_out_ref,
    gain1_ref,
    bias1_ref,
    gain2_ref,
    bias2_ref,
    gain3_ref,
    bias3_ref,
    embed_ref,
    embed_bias_ref,
    position_ref,
    std_in_ref,
    std_mid_ref,
    std_out_ref,
    first_ref,
    second_ref,
    third_ref,
    stat1_ref,
    stat2_ref,
    stat3_ref,
    stem_ref,
    tokens_ref,
    mask,
    padded,
    columns,
    act_two,
):
    image = pl.program_id(0)
    cells = x_ref.shape[1]
    channels = x_ref.shape[2]
    middle = w_in_ref.shape[1]

    @pl.when(image == 0)
    def _():
        std_in_ref[...] = standardized(w_in_ref[...].astype(f32))[0].astype(bf16)
        std_mid_ref[...] = standardized(w_mid_ref[...].astype(f32))[0].astype(bf16)
        std_out_ref[...] = standardized(w_out_ref[...].astype(f32))[0].astype(bf16)

    image_class = class_ref[image]
    mask[...] = validity_mask(image_class, cells)
    count = valid_count(image_class)
    chunk = 96
    steps = cells // chunk

    def stats(values_ref, stat_ref, sums):
        width = values_ref.shape[2]
        per_group = width // GROUPS
        inverse = 1.0 / (count * per_group)
        centre = group_total(total(sums), per_group) * inverse

        def one(step, carry):
            rows = rows_at(step, chunk)
            centred = (values_ref[0, rows, :] - centre) * spread_lanes(mask[rows, :], width)
            return carry + fold(centred * centred)

        squares = lax.fori_loop(0, steps, one, jnp.zeros((8, width), f32))
        scale = lax.rsqrt(group_total(total(squares), per_group) * inverse + 1e-05)
        stat_ref[0, 0:1, :] = centre
        stat_ref[0, 1:2, :] = scale
        return centre, scale

    def first_step(step, carry):
        rows = rows_at(step, chunk)
        low = (x_ref[0, rows, :] * spread_lanes(mask[rows, :], channels)).astype(bf16)
        values = dot_nn(low, std_in_ref[...])
        first_ref[0, rows, :] = values
        return carry + fold(values)

    sums = lax.fori_loop(0, steps, first_step, jnp.zeros((8, middle), f32))
    centre, scale = stats(first_ref, stat1_ref, sums)
    gain = scale * gain1_ref[...]
    normed = (first_ref[0] - centre) * gain + bias1_ref[...]
    act = normed * cdf_pdf(normed)[0] * spread_lanes(mask[...], middle)
    fill_columns(act, padded, columns, 1)

    def second_step(step, carry):
        rows = rows_at(step, chunk)
        values = dot_nn(columns[rows, :], std_mid_ref[...])
        second_ref[0, rows, :] = values
        return carry + fold(values * spread_lanes(mask[rows, :], middle))

    sums = lax.fori_loop(0, steps, second_step, jnp.zeros((8, middle), f32))
    centre, scale = stats(second_ref, stat2_ref, sums)
    gain = scale * gain2_ref[...]
    normed = (second_ref[0] - centre) * gain + bias2_ref[...]
    act_two[...] = (normed * cdf_pdf(normed)[0] * spread_lanes(mask[...], middle)).astype(bf16)

    def third_step(step, carry):
        rows = rows_at(step, chunk)
        values = dot_nn(act_two[rows, :], std_out_ref[...])
        third_ref[0, rows, :] = values
        return carry + fold(values)

    sums = lax.fori_loop(0, steps, third_step, jnp.zeros((8, channels), f32))
    centre, scale = stats(third_ref, stat3_ref, sums)
    gain = scale * gain3_ref[...]

    @pl.loop(0, steps)
    def _(step):
        rows = rows_at(step, chunk)
        keep = mask[rows, :]
        keep_wide = spread_lanes(keep, channels)
        argument = (
            x_ref[0, rows, :] * keep_wide + (third_ref[0, rows, :] - centre) * gain + bias3_ref[...]
        )
        stem = (argument * cdf_pdf(argument)[0] * keep_wide).astype(bf16)
        stem_ref[0, rows, :] = stem
        values = dot_nn(stem, embed_ref[...]) + embed_bias_ref[...] + position_ref[rows, :].astype(f32)
        tokens_ref[0, rows, :] = (values * spread_lanes(keep, values.shape[1])).astype(bf16)


def whole(shape):
    return pl.BlockSpec(shape, lambda *_: (0,) * len(shape))


def per_image(shape):
    return pl.BlockSpec((1,) + shape, lambda image, *_: (image,) + (0,) * len(shape))


def stem_forward(image_class, x, w_in, w_mid, w_out, norms, embed, embed_bias, position):
    images, cells, channels = x.shape
    middle = w_in.shape[1]
    width = embed.shape[1]
    row = lambda size: whole((1, size))
    return pl.pallas_call(
        stem_forward_kernel,
        out_shape=(
            jax.ShapeDtypeStruct((channels, middle), bf16),
            jax.ShapeDtypeStruct((9 * middle, middle), bf16),
            jax.ShapeDtypeStruct((middle, channels), bf16),
            jax.ShapeDtypeStruct((images, cells, middle), f32),
            jax.ShapeDtypeStruct((images, cells, middle), f32),
            jax.ShapeDtypeStruct((images, cells, channels), f32),
            jax.ShapeDtypeStruct((images, 8, middle), f32),
            jax.ShapeDtypeStruct((images, 8, middle), f32),
            jax.ShapeDtypeStruct((images, 8, channels), f32),
            jax.ShapeDtypeStruct((images, cells, channels), bf16),
            jax.ShapeDtypeStruct((images, cells, width), bf16),
        ),
        grid_spec=pltpu.PrefetchScalarGridSpec(
            num_scalar_prefetch=1,
            grid=(images,),
            in_specs=[
                per_image((cells, channels)),
                whole((channels, middle)),
                whole((9 * middle, middle)),
                whole((middle, channels)),
                row(middle),
                row(middle),
                row(middle),
                row(middle),
                row(channels),
                row(channels),
                whole((channels, width)),
                row(width),
                whole((cells, width)),
            ],
            out_specs=[
                whole((channels, middle)),
                whole((9 * middle, middle)),
                whole((middle, channels)),
                per_image((cells, middle)),
                per_image((cells, middle)),
                per_image((cells, channels)),
                per_image((8, middle)),
                per_image((8, middle)),
                per_image((8, channels)),
                per_image((cells, channels)),
                per_image((cells, width)),
            ],
            scratch_shapes=[
                pltpu.VMEM((cells, LANES), f32),
                pltpu.VMEM((3, cells + 2 * SIDE, middle), f32),
                pltpu.VMEM((cells, 9 * middle), bf16),
                pltpu.VMEM((cells, middle), bf16),
            ],
        ),
        compiler_params=pltpu.CompilerParams(vmem_limit_bytes=58 * MIB),
        name="stem_forward",
    )(image_class, x, w_in, w_mid, w_out, *norms, embed, embed_bias, position)


def row_norm(values):
    centre = jnp.mean(values, axis=-1, keepdims=True)
    centred = values - centre
    scale = lax.rsqrt(jnp.mean(centred * centred, axis=-1, keepdims=True) + 1e-06)
    return centred * scale, scale


def attend_forward_kernel(
    class_ref,
    tokens_ref,
    gain1_ref,
    bias1_ref,
    joint_ref,
    query_bias_ref,
    value_bias_ref,
    mix_ref,
    mix_bias_ref,
    gain2_ref,
    bias2_ref,
    normed_ref,
    query_ref,
    key_ref,
    value_ref,
    log_total_ref,
    mixed_ref,
    resid_ref,
    normed_two_ref,
):
    image = pl.program_id(0)
    cells, width = tokens_ref.shape[1:]
    chunk = 96
    steps = cells // chunk
    scale = (width // HEADS) ** -0.5

    @pl.loop(0, steps)
    def _(step):
        rows = rows_at(step, chunk)
        normal, _ = row_norm(tokens_ref[0, rows, :].astype(f32))
        normed_ref[0, rows, :] = (normal * gain1_ref[...] + bias1_ref[...]).astype(bf16)

    block = 256
    blocks = width // block

    @pl.loop(0, blocks)
    def _(step):
        here = rows_at(step, block)
        later = pl.ds(pl.multiple_of(width + step * block, block), block)
        last = pl.ds(pl.multiple_of(2 * width + step * block, block), block)
        normed = normed_ref[0]
        query = dot_nn(normed, joint_ref[:, here]) + query_bias_ref[:, here]
        query_ref[0, :, here] = query.astype(bf16)
        key_ref[0, :, here] = dot_nn(normed, joint_ref[:, later]).astype(bf16)
        value = dot_nn(normed, joint_ref[:, last]) + value_bias_ref[:, here]
        value_ref[0, :, here] = value.astype(bf16)

    _, column = cell_grid(cells)
    image_class = class_ref[image]
    cell = lax.broadcasted_iota(jnp.int32, (8, cells), 1).astype(f32)
    cell_row = jnp.floor((cell + 0.5) * (1.0 / SIDE))
    cell_column = cell - cell_row * SIDE
    outside = jnp.where((cell_row < SIDE_SMALL) & (cell_column < SIDE_SMALL), 0.0, -1000000000.0)
    key_bias = jnp.where(image_class == 1, 0.0, outside)[0:1]
    upper = lax.broadcasted_iota(jnp.int32, (cells, LANES), 1) >= LANES // 2

    @pl.loop(0, width // LANES)
    def _(pair):
        lanes = rows_at(pair, LANES)
        query = query_ref[0, :, lanes] * bf16(scale)
        key = key_ref[0, :, lanes]
        value = value_ref[0, :, lanes]
        outs = []
        for half in range(2):
            mine = upper if half else jnp.logical_not(upper)
            scores = dot_nt(jnp.where(mine, query, bf16(0)), key) + key_bias
            top = jnp.max(scores, axis=-1, keepdims=True)
            weights = jnp.exp(scores - top)
            weight_sum = jnp.sum(weights, axis=-1, keepdims=True)
            probs = (weights * (1.0 / weight_sum)).astype(bf16)
            outs.append(dot_nn(probs, value))
            log_total = jnp.broadcast_to(top + jnp.log(weight_sum), (cells, LANES))
            log_total_ref[0, 2 * pair + half] = log_total.T[0:8]
        mixed_ref[0, :, lanes] = jnp.where(upper, outs[1], outs[0]).astype(bf16)

    @pl.loop(0, steps)
    def _(step):
        rows = rows_at(step, chunk)
        resid = (
            tokens_ref[0, rows, :].astype(f32)
            + dot_nn(mixed_ref[0, rows, :], mix_ref[...])
            + mix_bias_ref[...]
        )
        resid_ref[0, rows, :] = resid
        normal, _ = row_norm(resid)
        normed_two_ref[0, rows, :] = (normal * gain2_ref[...] + bias2_ref[...]).astype(bf16)


def attend_forward(
    image_class, tokens, gain1, bias1, joint, query_bias, value_bias, mix, mix_bias, gain2, bias2
):
    images, cells, width = tokens.shape
    row = whole((1, width))
    low = jax.ShapeDtypeStruct((images, cells, width), bf16)
    low_spec = per_image((cells, width))
    return pl.pallas_call(
        attend_forward_kernel,
        out_shape=(
            low,
            low,
            low,
            low,
            jax.ShapeDtypeStruct((images, HEADS, 8, cells), f32),
            low,
            jax.ShapeDtypeStruct((images, cells, width), f32),
            low,
        ),
        grid_spec=pltpu.PrefetchScalarGridSpec(
            num_scalar_prefetch=1,
            grid=(images,),
            in_specs=[
                low_spec,
                row,
                row,
                whole((width, 3 * width)),
                row,
                row,
                whole((width, width)),
                row,
                row,
                row,
            ],
            out_specs=[
                low_spec,
                low_spec,
                low_spec,
                low_spec,
                per_image((HEADS, 8, cells)),
                low_spec,
                low_spec,
                low_spec,
            ],
        ),
        compiler_params=pltpu.CompilerParams(vmem_limit_bytes=58 * MIB),
        name="attend_forward",
    )(image_class, tokens, gain1, bias1, joint, query_bias, value_bias, mix, mix_bias, gain2, bias2)


def feed_kernel(
    class_ref,
    mine_ref,
    normed_ref,
    resid_ref,
    cotangent_ref,
    expand_ref,
    expand_bias_ref,
    shrink_ref,
    shrink_bias_ref,
    output_ref,
    grad_normed_ref,
    grad_shrink_ref,
    grad_expand_ref,
    grad_expand_bias_ref,
    grad_shrink_bias_ref,
    sent,
    result,
    hidden,
    grad_pre,
    normed_turned,
):
    step = pl.program_id(0)
    images, cells, width = normed_ref.shape
    part = cells // 2

    @pl.when(step == 0)
    def _():
        sums = jnp.zeros((8, width), f32)
        for image in range(images):
            keep = spread_lanes(validity_mask(class_ref[image], cells), width)
            grad = cotangent_ref[mine_ref[image]].astype(f32) * keep
            sent[image * cells : (image + 1) * cells, :] = grad.astype(bf16)
            sums = sums + fold(grad)
            result[image * cells : (image + 1) * cells, :] = resid_ref[image] + shrink_bias_ref[...]
            normed_turned[:, image * cells : (image + 1) * cells] = normed_ref[image].T
        grad_shrink_bias_ref[...] = sums
        grad_normed_ref[...] = jnp.zeros_like(grad_normed_ref)

    bias_sums = jnp.zeros((8, expand_ref.shape[1]), f32)
    for image in range(images):
        for piece in range(cells // part):
            local = slice(piece * part, (piece + 1) * part)
            rows = slice(image * cells + piece * part, image * cells + (piece + 1) * part)
            pre = dot_nn(normed_ref[image, local, :], expand_ref[...]) + expand_bias_ref[...]
            back = dot_nt(sent[rows, :], shrink_ref[...])
            cdf, pdf = cdf_pdf(pre)
            low = (pre * cdf).astype(bf16)
            hidden[rows, :] = low
            grad = back * (cdf + pre * pdf)
            bias_sums = bias_sums + fold(grad)
            grad_low = grad.astype(bf16)
            grad_pre[rows, :] = grad_low
            result[rows, :] += dot_nn(low, shrink_ref[...])
            grad_normed_ref[image, local, :] += dot_nt(grad_low, expand_ref[...])
    grad_expand_bias_ref[...] = bias_sums
    grad_shrink_ref[...] = dot_tn(hidden[...], sent[...]).astype(bf16)
    grad_expand_ref[...] = dot_nn(normed_turned[...], grad_pre[...]).astype(bf16)

    @pl.when(step == pl.num_programs(0) - 1)
    def _():
        output_ref[...] = jnp.zeros_like(output_ref)
        for image in range(images):
            keep = spread_lanes(validity_mask(class_ref[image], cells), width)
            rows = result[image * cells : (image + 1) * cells, :] * keep
            output_ref[mine_ref[image]] = rows.astype(bf16)


def feed(image_class, mine, normed, resid, cotangent, expand, expand_bias, shrink, shrink_bias):
    images, cells, width = normed.shape
    inner = expand.shape[1]
    slots = cotangent.shape[0]
    block = 512
    return pl.pallas_call(
        feed_kernel,
        out_shape=(
            jax.ShapeDtypeStruct((slots, cells, width), bf16),
            jax.ShapeDtypeStruct((images, cells, width), f32),
            jax.ShapeDtypeStruct((inner, width), bf16),
            jax.ShapeDtypeStruct((width, inner), bf16),
            jax.ShapeDtypeStruct((8, inner), f32),
            jax.ShapeDtypeStruct((8, width), f32),
        ),
        grid_spec=pltpu.PrefetchScalarGridSpec(
            num_scalar_prefetch=2,
            grid=(inner // block,),
            in_specs=[
                whole((images, cells, width)),
                whole((images, cells, width)),
                whole((slots, cells, width)),
                pl.BlockSpec((width, block), lambda step, *_: (0, step)),
                pl.BlockSpec((1, block), lambda step, *_: (0, step)),
                pl.BlockSpec((block, width), lambda step, *_: (step, 0)),
                whole((1, width)),
            ],
            out_specs=[
                whole((slots, cells, width)),
                whole((images, cells, width)),
                pl.BlockSpec((block, width), lambda step, *_: (step, 0)),
                pl.BlockSpec((width, block), lambda step, *_: (0, step)),
                pl.BlockSpec((8, block), lambda step, *_: (0, step)),
                whole((8, width)),
            ],
            scratch_shapes=[
                pltpu.VMEM((images * cells, width), bf16),
                pltpu.VMEM((images * cells, width), f32),
                pltpu.VMEM((images * cells, block), bf16),
                pltpu.VMEM((images * cells, block), bf16),
                pltpu.VMEM((width, images * cells), bf16),
            ],
        ),
        compiler_params=pltpu.CompilerParams(vmem_limit_bytes=60 * MIB),
        name="feed",
    )(image_class, mine, normed, resid, cotangent, expand, expand_bias, shrink, shrink_bias)


def row_norm_back(grad, normal, scale, gain):
    inner = grad * gain
    mean = jnp.mean(inner, axis=-1, keepdims=True)
    cross = jnp.mean(inner * normal, axis=-1, keepdims=True)
    return scale * (inner - mean - normal * cross)


def attend_backward_kernel(
    class_ref,
    mine_ref,
    tokens_ref,
    normed_ref,
    query_ref,
    key_ref,
    value_ref,
    log_total_ref,
    mixed_ref,
    resid_ref,
    cotangent_ref,
    grad_normed_two_ref,
    gain1_ref,
    joint_ref,
    mix_ref,
    gain2_ref,
    grad_tokens_ref,
    grad_joint_weight_ref,
    grad_mix_ref,
    sums_ref,
    mask,
    grad_resid,
    resid_low,
    grad_mixed,
    grad_joint,
    joint_total,
    mix_total,
):
    image = pl.program_id(0)
    last = pl.num_programs(0) - 1
    cells, width = tokens_ref.shape[1:]
    chunk = 96
    steps = cells // chunk
    scale = (width // HEADS) ** -0.5
    mask[...] = validity_mask(class_ref[image], cells)

    @pl.when(image == 0)
    def _():
        sums_ref[...] = jnp.zeros_like(sums_ref)
        joint_total[...] = jnp.zeros_like(joint_total)
        mix_total[...] = jnp.zeros_like(mix_total)

    @pl.loop(0, steps)
    def _(step):
        rows = rows_at(step, chunk)
        normal, row_scale = row_norm(resid_ref[0, rows, :])
        grad = grad_normed_two_ref[0, rows, :]
        sums_ref[0] += fold(grad * normal)
        sums_ref[1] += fold(grad)
        keep = spread_lanes(mask[rows, :], width)
        whole_grad = cotangent_ref[0, rows, :].astype(f32) * keep + row_norm_back(
            grad, normal, row_scale, gain2_ref[...]
        )
        sums_ref[2] += fold(whole_grad)
        grad_resid[rows, :] = whole_grad
        low = whole_grad.astype(bf16)
        resid_low[rows, :] = low
        grad_mixed[rows, :] = dot_nt(low, mix_ref[...]).astype(bf16)

    mix_total[...] += dot_tn(mixed_ref[0], resid_low[...])

    upper = lax.broadcasted_iota(jnp.int32, (cells, LANES), 1) >= LANES // 2
    key_bias = (mask[...] - 1.0) * 1000000000.0
    bias_wide = jnp.concatenate([key_bias] * 5, axis=1)[:, :cells]

    @pl.loop(0, width // LANES)
    def _(pair):
        lanes = rows_at(pair, LANES)
        query = query_ref[0, :, lanes] * bf16(scale)
        key = key_ref[0, :, lanes]
        value = value_ref[0, :, lanes]
        grad_out = grad_mixed[:, lanes]
        grads = []
        for half in range(2):
            mine = upper if half else jnp.logical_not(upper)
            scores = dot_nt(jnp.where(mine, key, bf16(0)), query)
            log_total = log_total_ref[0, 2 * pair + half, 0:1, :]
            probs = jnp.exp(scores + bias_wide - log_total)
            grad_probs = dot_nt(jnp.where(mine, value, bf16(0)), grad_out)
            weighted = probs * grad_probs
            grad_scores = (weighted - probs * total(weighted)).astype(bf16)
            grad_value = dot_nn(probs.astype(bf16), grad_out)
            grad_key = dot_nn(grad_scores, query)
            grad_query = dot_tn(grad_scores, key) * scale
            grads.append((grad_query, grad_key, grad_value))
        for k in range(3):
            grad = jnp.where(upper, grads[1][k], grads[0][k])
            if k != 1:
                sums_ref[3 + k // 2, :, lanes] += fold(grad)
            where = pl.ds(pl.multiple_of(k * width + pair * LANES, LANES), LANES)
            grad_joint[:, where] = grad.astype(bf16)

    block = 256

    @pl.loop(0, 3 * width // block)
    def _(step):
        here = rows_at(step, block)
        joint_total[:, here] += dot_tn(normed_ref[0], grad_joint[:, here])

    @pl.loop(0, steps)
    def _(step):
        rows = rows_at(step, chunk)
        normal, row_scale = row_norm(tokens_ref[0, rows, :].astype(f32))
        grad = dot_nt(grad_joint[rows, :], joint_ref[...])
        sums_ref[5] += fold(grad * normal)
        sums_ref[6] += fold(grad)
        back = row_norm_back(grad, normal, row_scale, gain1_ref[...])
        grad_tokens_ref[0, rows, :] = (grad_resid[rows, :] + back).astype(bf16)

    @pl.when(image == last)
    def _():
        grad_joint_weight_ref[...] = joint_total[...].astype(bf16)
        grad_mix_ref[...] = mix_total[...].astype(bf16)


def attend_backward(
    image_class,
    mine,
    tokens,
    normed,
    query,
    key,
    value,
    log_total,
    mixed,
    resid,
    cotangent,
    grad_normed_two,
    gain1,
    joint,
    mix,
    gain2,
):
    images, cells, width = tokens.shape
    row = whole((1, width))
    rows = per_image((cells, width))
    return pl.pallas_call(
        attend_backward_kernel,
        out_shape=(
            jax.ShapeDtypeStruct((images, cells, width), bf16),
            jax.ShapeDtypeStruct((width, 3 * width), bf16),
            jax.ShapeDtypeStruct((width, width), bf16),
            jax.ShapeDtypeStruct((7, 8, width), f32),
        ),
        grid_spec=pltpu.PrefetchScalarGridSpec(
            num_scalar_prefetch=2,
            grid=(images,),
            in_specs=[
                rows,
                rows,
                rows,
                rows,
                rows,
                per_image((HEADS, 8, cells)),
                rows,
                rows,
                pl.BlockSpec((1, cells, width), lambda image, classes, mine: (mine[image], 0, 0)),
                rows,
                row,
                whole((width, 3 * width)),
                whole((width, width)),
                row,
            ],
            out_specs=[
                rows,
                whole((width, 3 * width)),
                whole((width, width)),
                whole((7, 8, width)),
            ],
            scratch_shapes=[
                pltpu.VMEM((cells, LANES), f32),
                pltpu.VMEM((cells, width), f32),
                pltpu.VMEM((cells, width), bf16),
                pltpu.VMEM((cells, width), bf16),
                pltpu.VMEM((cells, 3 * width), bf16),
                pltpu.VMEM((width, 3 * width), f32),
                pltpu.VMEM((width, width), f32),
            ],
        ),
        compiler_params=pltpu.CompilerParams(vmem_limit_bytes=62 * MIB),
        name="attend_backward",
    )(
        image_class,
        mine,
        tokens,
        normed,
        query,
        key,
        value,
        log_total,
        mixed,
        resid,
        cotangent,
        grad_normed_two,
        gain1,
        joint,
        mix,
        gain2,
    )


def stem_backward_kernel(
    class_ref,
    grad_tokens_ref,
    x_ref,
    first_ref,
    second_ref,
    third_ref,
    stat1_ref,
    stat2_ref,
    stat3_ref,
    stem_ref,
    std_in_ref,
    std_mid_ref,
    std_out_ref,
    w_in_ref,
    w_mid_ref,
    w_out_ref,
    gain1_ref,
    bias1_ref,
    gain2_ref,
    bias2_ref,
    gain3_ref,
    bias3_ref,
    embed_ref,
    input_grad_ref,
    grad_embed_ref,
    grad_position_ref,
    grad_in_ref,
    grad_mid_ref,
    grad_out_ref,
    sums_embed_ref,
    sums1_ref,
    sums2_ref,
    sums3_ref,
    mask,
    grad_third,
    act,
    grad_grid,
    grad_first,
    padded,
    columns,
    embed_total,
    in_total,
    mid_total,
    out_total,
):
    image = pl.program_id(0)
    last = pl.num_programs(0) - 1
    cells, channels = x_ref.shape[1:]
    width = embed_ref.shape[1]
    middle = first_ref.shape[2]
    chunk = 96
    steps = cells // chunk
    image_class = class_ref[image]
    mask[...] = validity_mask(image_class, cells)
    count = valid_count(image_class)

    @pl.when(image == 0)
    def _():
        for ref in (
            grad_position_ref,
            sums_embed_ref,
            sums1_ref,
            sums2_ref,
            sums3_ref,
            embed_total,
            in_total,
            mid_total,
            out_total,
        ):
            ref[...] = jnp.zeros_like(ref)

    @pl.loop(0, steps)
    def _(step):
        rows = rows_at(step, chunk)
        grad = grad_tokens_ref[0, rows, :].astype(f32) * spread_lanes(mask[rows, :], width)
        grad_position_ref[rows, :] += grad
        sums_embed_ref[...] += fold(grad)

    embed_total[...] += dot_tn(stem_ref[0], grad_tokens_ref[0])

    def norm_of(stat_ref):
        return stat_ref[0, 0:1, :], stat_ref[0, 1:2, :]

    def means(sums, gain, per_group):
        inverse = 1.0 / (count * per_group)
        return (
            group_total(total(sums[0]) * gain, per_group) * inverse,
            group_total(total(sums[1]) * gain, per_group) * inverse,
        )

    centre, scale = norm_of(stat3_ref)
    gain = gain3_ref[...]

    def third_step(step, carry):
        rows = rows_at(step, chunk)
        keep = spread_lanes(mask[rows, :], channels)
        grad = dot_nt(grad_tokens_ref[0, rows, :], embed_ref[...]) * keep
        normal = (third_ref[0, rows, :] - centre) * scale
        argument = x_ref[0, rows, :] * keep + normal * gain + bias3_ref[...]
        cdf, pdf = cdf_pdf(argument)
        grad = grad * (cdf + argument * pdf)
        input_grad_ref[0, rows, :] = grad
        return carry[0] + fold(grad * normal), carry[1] + fold(grad)

    zeros = jnp.zeros((8, channels), f32)
    with_normal, plain = lax.fori_loop(0, steps, third_step, (zeros, zeros))
    sums3_ref[0] += with_normal
    sums3_ref[1] += plain
    mean, cross = means((plain, with_normal), gain, channels // GROUPS)
    outer = scale * gain
    mean = mean * scale
    cross = cross * scale

    @pl.loop(0, steps)
    def _(step):
        rows = rows_at(step, chunk)
        keep = spread_lanes(mask[rows, :], channels)
        normal = (third_ref[0, rows, :] - centre) * scale
        grad = (input_grad_ref[0, rows, :] * outer - mean - normal * cross) * keep
        grad_third[rows, :] = grad.astype(bf16)

    def middle_norm(values_ref, stat_ref, gain_ref, bias_ref, sums_ref, grad_of):
        centre, scale = norm_of(stat_ref)
        gain = gain_ref[...]
        keep = spread_lanes(mask[...], middle)
        normal = (values_ref[0] - centre) * scale
        argument = normal * gain + bias_ref[...]
        cdf, pdf = cdf_pdf(argument)
        act[...] = (argument * cdf * keep).astype(bf16)
        grad = grad_of() * keep * (cdf + argument * pdf)
        plain, with_normal = fold(grad), fold(grad * normal)
        sums_ref[0] += with_normal
        sums_ref[1] += plain
        mean, cross = means((plain, with_normal), gain, middle // GROUPS)
        return (grad * (scale * gain) - mean * scale - normal * (cross * scale)) * keep

    grad_second = middle_norm(
        second_ref,
        stat2_ref,
        gain2_ref,
        bias2_ref,
        sums2_ref,
        lambda: dot_nt(grad_third[...], std_out_ref[...]),
    )
    out_total[...] += dot_tn(act[...], grad_third[...])
    fill_columns(grad_second, padded, columns, -1)

    def spread_back():
        grad = jnp.zeros((cells, middle), f32)
        for tap in range(9):
            part = slice(tap * middle, (tap + 1) * middle)
            grad = grad + dot_nt(columns[:, part], std_mid_ref[part, :])
        return grad

    grad = middle_norm(first_ref, stat1_ref, gain1_ref, bias1_ref, sums1_ref, spread_back)
    grad_first[...] = grad.astype(bf16)
    mid_total[...] += dot_tn(act[...], columns[...])

    grad_grid[...] = grad_first[...].T

    @pl.loop(0, steps)
    def _(step):
        rows = rows_at(step, chunk)
        keep = spread_lanes(mask[rows, :], channels)
        back = dot_nt(grad_first[rows, :], std_in_ref[...])
        input_grad_ref[0, rows, :] = (input_grad_ref[0, rows, :] + back) * keep

    low = (x_ref[0] * spread_lanes(mask[...], channels)).astype(bf16)
    in_total[...] += dot_nn(grad_grid[...], low)

    @pl.when(image == last)
    def _():
        grad_embed_ref[...] = embed_total[...].astype(bf16)
        grad_out_ref[...] = standardize_back(w_out_ref[...].astype(f32), out_total[...]).astype(bf16)
        grad_in_ref[...] = standardize_back(w_in_ref[...].astype(f32), in_total[...].T).astype(bf16)
        rows = 9 * middle
        normal, scale = standardized(w_mid_ref[...].astype(f32))
        grads = [mid_total[:, tap * middle : (tap + 1) * middle] for tap in range(9)]
        grad_mean = sum(total(g) for g in grads) * (1.0 / rows)
        inner = sum(
            total(g * normal[tap * middle : (tap + 1) * middle]) for tap, g in enumerate(grads)
        ) * (1.0 / rows)
        for tap, g in enumerate(grads):
            part = slice(tap * middle, (tap + 1) * middle)
            grad_mid_ref[part, :] = (scale * (g - grad_mean - normal[part] * inner)).astype(bf16)


def stem_backward(
    image_class, grad_tokens, x, kept, stem, stds, weights, norms, embed
):
    images, cells, channels = x.shape
    middle = weights[0].shape[1]
    width = embed.shape[1]
    row = lambda size: whole((1, size))
    return pl.pallas_call(
        stem_backward_kernel,
        out_shape=(
            jax.ShapeDtypeStruct((images, cells, channels), f32),
            jax.ShapeDtypeStruct((channels, width), bf16),
            jax.ShapeDtypeStruct((cells, width), f32),
            jax.ShapeDtypeStruct((channels, middle), bf16),
            jax.ShapeDtypeStruct((9 * middle, middle), bf16),
            jax.ShapeDtypeStruct((middle, channels), bf16),
            jax.ShapeDtypeStruct((8, width), f32),
            jax.ShapeDtypeStruct((2, 8, middle), f32),
            jax.ShapeDtypeStruct((2, 8, middle), f32),
            jax.ShapeDtypeStruct((2, 8, channels), f32),
        ),
        grid_spec=pltpu.PrefetchScalarGridSpec(
            num_scalar_prefetch=1,
            grid=(images,),
            in_specs=[
                per_image((cells, width)),
                per_image((cells, channels)),
                per_image((cells, middle)),
                per_image((cells, middle)),
                per_image((cells, channels)),
                per_image((8, middle)),
                per_image((8, middle)),
                per_image((8, channels)),
                per_image((cells, channels)),
                whole((channels, middle)),
                whole((9 * middle, middle)),
                whole((middle, channels)),
                whole((channels, middle)),
                whole((9 * middle, middle)),
                whole((middle, channels)),
                row(middle),
                row(middle),
                row(middle),
                row(middle),
                row(channels),
                row(channels),
                whole((channels, width)),
            ],
            out_specs=[
                per_image((cells, channels)),
                whole((channels, width)),
                whole((cells, width)),
                whole((channels, middle)),
                whole((9 * middle, middle)),
                whole((middle, channels)),
                whole((8, width)),
                whole((2, 8, middle)),
                whole((2, 8, middle)),
                whole((2, 8, channels)),
            ],
            scratch_shapes=[
                pltpu.VMEM((cells, LANES), f32),
                pltpu.VMEM((cells, channels), bf16),
                pltpu.VMEM((cells, middle), bf16),
                pltpu.VMEM((middle, cells), bf16),
                pltpu.VMEM((cells, middle), bf16),
                pltpu.VMEM((3, cells + 2 * SIDE, middle), f32),
                pltpu.VMEM((cells, 9 * middle), bf16),
                pltpu.VMEM((channels, width), f32),
                pltpu.VMEM((middle, channels), f32),
                pltpu.VMEM((middle, 9 * middle), f32),
                pltpu.VMEM((middle, channels), f32),
            ],
        ),
        compiler_params=pltpu.CompilerParams(vmem_limit_bytes=62 * MIB),
        name="stem_backward",
    )(image_class, grad_tokens, x, *kept, stem, *stds, *weights, *norms, embed)


def local_step(
    image_class,
    mine,
    stem_input,
    conv_in_weight,
    conv_mid_weight,
    conv_out_weight,
    norms,
    embed_weight,
    embed_bias,
    position_table,
    attn_gain,
    attn_bias,
    joint_weight,
    query_bias,
    value_bias,
    mix_weight,
    mix_bias,
    mlp_gain,
    mlp_bias,
    expand_weight,
    expand_bias,
    shrink_weight,
    shrink_bias,
    received,
    after_feed=lambda *parts: parts,
):
    line = lambda vector: vector.reshape(1, -1)
    norms = tuple(line(item) for item in norms)
    weights = (conv_in_weight, conv_mid_weight.reshape(-1, conv_mid_weight.shape[-1]), conv_out_weight)
    std_in, std_mid, std_out, first, second, third, stat1, stat2, stat3, stem, tokens = stem_forward(
        image_class, stem_input, *weights, norms, embed_weight, line(embed_bias), position_table
    )
    normed, query, key, value, log_total, mixed, resid, normed_two = attend_forward(
        image_class,
        tokens,
        line(attn_gain),
        line(attn_bias),
        joint_weight,
        line(query_bias),
        line(value_bias),
        mix_weight,
        line(mix_bias),
        line(mlp_gain),
        line(mlp_bias),
    )
    outgoing, grad_normed_two, grad_shrink, grad_expand, sum_expand_bias, sum_shrink_bias = feed(
        image_class,
        mine,
        normed_two,
        resid,
        received,
        expand_weight,
        line(expand_bias),
        shrink_weight,
        line(shrink_bias),
    )
    grad_tokens, grad_joint, grad_mix, sums_block = attend_backward(
        image_class,
        mine,
        tokens,
        normed,
        query,
        key,
        value,
        log_total,
        mixed,
        resid,
        received,
        grad_normed_two,
        line(attn_gain),
        joint_weight,
        mix_weight,
        line(mlp_gain),
    )
    (
        input_grad,
        grad_embed,
        grad_position,
        grad_in,
        grad_mid,
        grad_out,
        sums_embed,
        sums1,
        sums2,
        sums3,
    ) = stem_backward(
        image_class,
        grad_tokens,
        stem_input,
        (first, second, third, stat1, stat2, stat3),
        stem,
        (std_in, std_mid, std_out),
        weights,
        norms,
        embed_weight,
    )
    matrices = (
        grad_in,
        grad_mid,
        grad_out,
        grad_embed,
        grad_position,
        grad_joint,
        grad_mix,
        grad_expand,
        grad_shrink,
    )
    vectors = (
        sums1[0],
        sums1[1],
        sums2[0],
        sums2[1],
        sums3[0],
        sums3[1],
        sums_embed,
        sums_block[5],
        sums_block[6],
        sums_block[3],
        sums_block[4],
        sums_block[2],
        sums_block[0],
        sums_block[1],
        sum_expand_bias,
        sum_shrink_bias,
    )
    return outgoing, input_grad, matrices, vectors


def shards(
    stem_input,
    image_class,
    owner,
    conv_in_weight,
    first_gain,
    first_bias,
    conv_mid_weight,
    second_gain,
    second_bias,
    conv_out_weight,
    third_gain,
    third_bias,
    embed_weight,
    embed_bias,
    position_table,
    attn_gain,
    attn_bias,
    joint_weight,
    query_bias,
    value_bias,
    mix_weight,
    mix_bias,
    mlp_gain,
    mlp_bias,
    expand_weight,
    expand_bias,
    shrink_weight,
    shrink_bias,
    cotangent,
):
    sections = lax.axis_size("section")
    devices = sections * lax.axis_size("batch")
    images = stem_input.shape[0]
    section_index = lax.axis_index("section")
    mine = lax.dynamic_index_in_dim(owner.reshape(sections, images), section_index, 0, keepdims=False)
    received = lax.all_to_all(cotangent[0], "section", split_axis=0, concat_axis=0, tiled=True)
    outgoing, input_grad, matrices, vectors = local_step(
        image_class,
        mine,
        stem_input,
        conv_in_weight,
        conv_mid_weight,
        conv_out_weight,
        (first_gain, first_bias, second_gain, second_bias, third_gain, third_bias),
        embed_weight,
        embed_bias,
        position_table,
        attn_gain,
        attn_bias,
        joint_weight,
        query_bias,
        value_bias,
        mix_weight,
        mix_bias,
        mlp_gain,
        mlp_bias,
        expand_weight,
        expand_bias,
        shrink_weight,
        shrink_bias,
        received,
    )
    block_output = lax.all_to_all(outgoing, "section", split_axis=0, concat_axis=0, tiled=True)[None]

    def scatter(matrix):
        parts = matrix.astype(bf16).reshape(devices, -1)
        size = parts.shape[1]
        padded = -(-size // LANES) * LANES
        if padded != size:
            parts = jnp.pad(parts, ((0, 0), (0, padded - size)))
        parts = parts.reshape(devices, -1, LANES)
        own = lax.psum_scatter(parts, BOTH, scatter_dimension=0, tiled=True)
        return own.astype(f32).reshape(-1)[:size]

    matrices = tuple(scatter(matrix) for matrix in matrices)
    sizes = [vector.shape[1] for vector in vectors]
    packed = lax.psum(jnp.concatenate([jnp.sum(vector, axis=0) for vector in vectors]), BOTH)
    small = []
    start = 0
    for size in sizes:
        small.append(packed[start : start + size])
        start += size
    return (
        block_output,
        input_grad,
        matrices[0],
        small[0],
        small[1],
        matrices[1],
        small[2],
        small[3],
        matrices[2],
        small[4],
        small[5],
        matrices[3],
        small[6],
        matrices[4],
        small[7],
        small[8],
        matrices[5],
        small[9],
        small[10],
        matrices[6],
        small[11],
        small[12],
        small[13],
        matrices[7],
        small[14],
        matrices[8],
        small[15],
    )


def solution(mesh):
    split = P(BOTH)
    images = P(BOTH, None, None)
    slots = P(BOTH, None, None, None)
    full = P()
    in_specs = (images, split, P("batch")) + (full,) * 25 + (slots,)
    out_specs = (
        slots,
        images,
        split,
        full,
        full,
        split,
        full,
        full,
        split,
        full,
        full,
        split,
        full,
        split,
        full,
        full,
        split,
        full,
        full,
        split,
        full,
        full,
        full,
        split,
        full,
        split,
        full,
    )
    return jax.shard_map(shards, mesh=mesh, in_specs=in_specs, out_specs=out_specs, check_vma=False)
```

```python
import jax
import jax.numpy as jnp
from jax import lax
from jax.experimental import pallas as pl
from jax.experimental.pallas import tpu as pltpu
from jax.sharding import PartitionSpec as P

HEADS = 12
GROUPS = 32
SIDE = 24
SIDE_SMALL = 14
LANES = 128
MIB = 1024 * 1024
BOTH = ("batch", "section")

f32 = jnp.float32
bf16 = jnp.bfloat16


def dot_nn(left, right):
    return jnp.dot(left, right, preferred_element_type=f32)


def dot_tn(left, right):
    return lax.dot_general(left, right, (((0,), (0,)), ((), ())), preferred_element_type=f32)


def dot_nt(left, right):
    return lax.dot_general(left, right, (((1,), (1,)), ((), ())), preferred_element_type=f32)


def fold(values):
    rows, columns = values.shape
    return jnp.sum(values.reshape(rows // 8, 8, columns), axis=0)


def total(values):
    return jnp.sum(values, axis=0, keepdims=True)


def line(ref):
    return ref[...].reshape(1, -1)


def spread_lanes(mask, columns):
    return jnp.concatenate([mask] * (columns // LANES), axis=1)


def cdf_pdf(values):
    bell = jnp.exp(-0.5 * (values * values))
    t = 1.0 / (1.0 + 0.23164189 * jnp.abs(values))
    tail = (
        ((((0.5307027145 * t - 0.7265760135) * t + 0.7107068705) * t - 0.142248368) * t + 0.127414796)
        * t
        * bell
    )
    return jnp.where(values < 0.0, tail, 1.0 - tail), bell * 0.3989422804014327


def group_total(row, per_group):
    channels = row.shape[1]
    rows = jnp.broadcast_to(row, (8, channels))
    lane = lax.broadcasted_iota(jnp.int32, (8, LANES), 1)
    parts = []
    for k in range(channels // LANES):
        part = rows[:, k * LANES : (k + 1) * LANES]
        step = 1
        while step < per_group:
            up = pltpu.roll(part, LANES - step, 1)
            down = pltpu.roll(part, step, 1)
            part = part + jnp.where((lane & step) == 0, up, down)
            step *= 2
        parts.append(part)
    return jnp.concatenate(parts, axis=1)[0:1]


def cell_grid(cells):
    cell = lax.broadcasted_iota(jnp.int32, (cells, LANES), 0).astype(f32)
    row = jnp.floor((cell + 0.5) * (1.0 / SIDE))
    return row, cell - row * SIDE


def validity_mask(image_class, cells):
    row, column = cell_grid(cells)
    corner = jnp.where((row < SIDE_SMALL) & (column < SIDE_SMALL), 1.0, 0.0)
    return jnp.where(image_class == 1, 1.0, corner)


def valid_count(image_class):
    return jnp.where(image_class == 1, float(SIDE * SIDE), float(SIDE_SMALL * SIDE_SMALL))


def rows_at(index, size):
    return pl.ds(pl.multiple_of(index * size, size), size)


def fill_columns(grid_value, padded, columns, sign):
    cells, channels = grid_value.shape
    _, column = cell_grid(cells)
    has_left = spread_lanes(jnp.where(column > 0.5, 1.0, 0.0), channels)
    has_right = spread_lanes(jnp.where(column < SIDE - 1.5, 1.0, 0.0), channels)
    zeros = jnp.zeros((SIDE, channels), f32)
    shifted = (
        pltpu.roll(grid_value, 1, 0) * has_left,
        grid_value,
        pltpu.roll(grid_value, cells - 1, 0) * has_right,
    )
    for k in range(3):
        padded[k, 0:SIDE, :] = zeros
        padded[k, SIDE + cells : 2 * SIDE + cells, :] = zeros
        padded[k, SIDE : SIDE + cells, :] = shifted[k]
    for row_shift in range(3):
        for column_shift in range(3):
            tap = row_shift * 3 + column_shift
            down = row_shift if sign > 0 else 2 - row_shift
            across = column_shift if sign > 0 else 2 - column_shift
            columns[:, tap * channels : (tap + 1) * channels] = padded[
                across, down * SIDE : down * SIDE + cells, :
            ].astype(bf16)


def standardized(weight):
    rows = weight.shape[0]
    centred = weight - total(weight) * (1.0 / rows)
    spread = total(centred * centred) * (1.0 / rows)
    scale = lax.rsqrt(spread + 1e-05)
    return centred * scale, scale


def standardize_back(weight, grad):
    rows = weight.shape[0]
    normal, scale = standardized(weight)
    grad_mean = total(grad) * (1.0 / rows)
    inner = total(grad * normal) * (1.0 / rows)
    return scale * (grad - grad_mean - normal * inner)


PAIRS = 16
VECTORS = 3


def store_split(ref, start, values):
    high = values.astype(bf16)
    low = (values - high.astype(f32)).astype(bf16)
    shape = (VECTORS, 8, values.shape[-1])
    ref[start : start + VECTORS] = high.astype(f32).reshape(shape).astype(bf16)
    ref[start + VECTORS : start + 2 * VECTORS] = low.astype(f32).reshape(shape).astype(bf16)


def load_split(ref, start):
    high = ref[start : start + VECTORS].astype(f32)
    low = ref[start + VECTORS : start + 2 * VECTORS].astype(f32)
    rows = high + low
    return rows.reshape(VECTORS * 8, rows.shape[-1])


def sections_of(values):
    rows, columns = values.shape
    return values.reshape(rows // 8, 8, columns).astype(bf16)


def stem_forward_kernel(
    class_ref,
    x_ref,
    w_in_ref,
    w_mid_ref,
    w_out_ref,
    gain1_ref,
    bias1_ref,
    gain2_ref,
    bias2_ref,
    gain3_ref,
    bias3_ref,
    embed_ref,
    embed_bias_ref,
    position_ref,
    std_in_ref,
    std_mid_ref,
    std_out_ref,
    first_ref,
    second_ref,
    third_ref,
    stat1_ref,
    stat2_ref,
    stat3_ref,
    stem_ref,
    tokens_ref,
    mask,
    padded,
    columns,
    act_two,
):
    image = pl.program_id(0)
    cells = x_ref.shape[1]
    channels = x_ref.shape[2]
    middle = w_in_ref.shape[1]

    @pl.when(image == 0)
    def _():
        std_in_ref[...] = standardized(w_in_ref[...].astype(f32))[0].astype(bf16)
        std_mid_ref[...] = standardized(w_mid_ref[...].astype(f32))[0].astype(bf16)
        std_out_ref[...] = standardized(w_out_ref[...].astype(f32))[0].astype(bf16)

    image_class = class_ref[image]
    mask[...] = validity_mask(image_class, cells)
    count = valid_count(image_class)
    chunk = 96
    steps = cells // chunk

    def stats(values_ref, stat_ref, sums):
        width = values_ref.shape[2]
        per_group = width // GROUPS
        inverse = 1.0 / (count * per_group)
        centre = group_total(total(sums), per_group) * inverse

        def one(step, carry):
            rows = rows_at(step, chunk)
            centred = (values_ref[0, rows, :] - centre) * spread_lanes(mask[rows, :], width)
            return carry + fold(centred * centred)

        squares = lax.fori_loop(0, steps, one, jnp.zeros((8, width), f32))
        scale = lax.rsqrt(group_total(total(squares), per_group) * inverse + 1e-05)
        stat_ref[0, 0:1, :] = centre
        stat_ref[0, 1:2, :] = scale
        return centre, scale

    def first_step(step, carry):
        rows = rows_at(step, chunk)
        low = (x_ref[0, rows, :] * spread_lanes(mask[rows, :], channels)).astype(bf16)
        values = dot_nn(low, std_in_ref[...])
        first_ref[0, rows, :] = values
        return carry + fold(values)

    sums = lax.fori_loop(0, steps, first_step, jnp.zeros((8, middle), f32))
    centre, scale = stats(first_ref, stat1_ref, sums)
    gain = scale * line(gain1_ref)
    normed = (first_ref[0] - centre) * gain + line(bias1_ref)
    act = normed * cdf_pdf(normed)[0] * spread_lanes(mask[...], middle)
    fill_columns(act, padded, columns, 1)

    def second_step(step, carry):
        rows = rows_at(step, chunk)
        values = dot_nn(columns[rows, :], std_mid_ref[...])
        second_ref[0, rows, :] = values
        return carry + fold(values * spread_lanes(mask[rows, :], middle))

    sums = lax.fori_loop(0, steps, second_step, jnp.zeros((8, middle), f32))
    centre, scale = stats(second_ref, stat2_ref, sums)
    gain = scale * line(gain2_ref)
    normed = (second_ref[0] - centre) * gain + line(bias2_ref)
    act_two[...] = (normed * cdf_pdf(normed)[0] * spread_lanes(mask[...], middle)).astype(bf16)

    def third_step(step, carry):
        rows = rows_at(step, chunk)
        values = dot_nn(act_two[rows, :], std_out_ref[...])
        third_ref[0, rows, :] = values
        return carry + fold(values)

    sums = lax.fori_loop(0, steps, third_step, jnp.zeros((8, channels), f32))
    centre, scale = stats(third_ref, stat3_ref, sums)
    gain = scale * line(gain3_ref)

    @pl.loop(0, steps)
    def _(step):
        rows = rows_at(step, chunk)
        keep = mask[rows, :]
        keep_wide = spread_lanes(keep, channels)
        argument = (
            x_ref[0, rows, :] * keep_wide + (third_ref[0, rows, :] - centre) * gain + line(bias3_ref)
        )
        stem = (argument * cdf_pdf(argument)[0] * keep_wide).astype(bf16)
        stem_ref[0, rows, :] = stem
        values = dot_nn(stem, embed_ref[...]) + line(embed_bias_ref) + position_ref[rows, :].astype(f32)
        tokens_ref[0, rows, :] = (values * spread_lanes(keep, values.shape[1])).astype(bf16)


def cost(flops, moved):
    return pl.CostEstimate(flops=flops, bytes_accessed=moved, transcendentals=0)


def whole(shape):
    return pl.BlockSpec(shape, lambda *_: (0,) * len(shape))


def per_image(shape):
    return pl.BlockSpec((1,) + shape, lambda image, *_: (image,) + (0,) * len(shape))


def stem_forward(image_class, x, w_in, w_mid, w_out, norms, embed, embed_bias, position):
    images, cells, channels = x.shape
    middle = w_in.shape[1]
    width = embed.shape[1]
    row = lambda size: whole((size,))
    return pl.pallas_call(
        stem_forward_kernel,
        out_shape=(
            jax.ShapeDtypeStruct((channels, middle), bf16),
            jax.ShapeDtypeStruct((9 * middle, middle), bf16),
            jax.ShapeDtypeStruct((middle, channels), bf16),
            jax.ShapeDtypeStruct((images, cells, middle), f32),
            jax.ShapeDtypeStruct((images, cells, middle), f32),
            jax.ShapeDtypeStruct((images, cells, channels), f32),
            jax.ShapeDtypeStruct((images, 8, middle), f32),
            jax.ShapeDtypeStruct((images, 8, middle), f32),
            jax.ShapeDtypeStruct((images, 8, channels), f32),
            jax.ShapeDtypeStruct((images, cells, channels), bf16),
            jax.ShapeDtypeStruct((images, cells, width), bf16),
        ),
        grid_spec=pltpu.PrefetchScalarGridSpec(
            num_scalar_prefetch=1,
            grid=(images,),
            in_specs=[
                per_image((cells, channels)),
                whole((channels, middle)),
                whole((9 * middle, middle)),
                whole((middle, channels)),
                row(middle),
                row(middle),
                row(middle),
                row(middle),
                row(channels),
                row(channels),
                whole((channels, width)),
                row(width),
                whole((cells, width)),
            ],
            out_specs=[
                whole((channels, middle)),
                whole((9 * middle, middle)),
                whole((middle, channels)),
                per_image((cells, middle)),
                per_image((cells, middle)),
                per_image((cells, channels)),
                per_image((8, middle)),
                per_image((8, middle)),
                per_image((8, channels)),
                per_image((cells, channels)),
                per_image((cells, width)),
            ],
            scratch_shapes=[
                pltpu.VMEM((cells, LANES), f32),
                pltpu.VMEM((3, cells + 2 * SIDE, middle), f32),
                pltpu.VMEM((cells, 9 * middle), bf16),
                pltpu.VMEM((cells, middle), bf16),
            ],
        ),
        compiler_params=pltpu.CompilerParams(vmem_limit_bytes=62 * MIB),
        cost_estimate=cost(25_000_000_000, 30 * MIB),
        name="stem_forward",
    )(image_class, x, w_in, w_mid, w_out, *norms, embed, embed_bias, position)


def row_norm(values):
    centre = jnp.mean(values, axis=-1, keepdims=True)
    centred = values - centre
    scale = lax.rsqrt(jnp.mean(centred * centred, axis=-1, keepdims=True) + 1e-06)
    return centred * scale, scale


def attend_forward_kernel(
    class_ref,
    tokens_ref,
    gain1_ref,
    bias1_ref,
    joint_ref,
    query_bias_ref,
    value_bias_ref,
    mix_ref,
    mix_bias_ref,
    gain2_ref,
    bias2_ref,
    normed_ref,
    query_ref,
    key_ref,
    value_ref,
    log_total_ref,
    mixed_ref,
    resid_ref,
    normed_two_ref,
):
    image = pl.program_id(0)
    cells, width = tokens_ref.shape[1:]
    chunk = 96
    steps = cells // chunk
    scale = (width // HEADS) ** -0.5

    @pl.loop(0, steps)
    def _(step):
        rows = rows_at(step, chunk)
        normal, _ = row_norm(tokens_ref[0, rows, :].astype(f32))
        normed_ref[0, rows, :] = (normal * line(gain1_ref) + line(bias1_ref)).astype(bf16)

    block = 256
    query_bias = line(query_bias_ref)
    value_bias = line(value_bias_ref)
    for start in range(0, width, block):
        here = slice(start, start + block)
        later = slice(width + start, width + start + block)
        last = slice(2 * width + start, 2 * width + start + block)
        normed = normed_ref[0]
        query = dot_nn(normed, joint_ref[:, here]) + query_bias[:, here]
        query_ref[0, :, here] = query.astype(bf16)
        key_ref[0, :, here] = dot_nn(normed, joint_ref[:, later]).astype(bf16)
        value = dot_nn(normed, joint_ref[:, last]) + value_bias[:, here]
        value_ref[0, :, here] = value.astype(bf16)

    _, column = cell_grid(cells)
    image_class = class_ref[image]
    cell = lax.broadcasted_iota(jnp.int32, (8, cells), 1).astype(f32)
    cell_row = jnp.floor((cell + 0.5) * (1.0 / SIDE))
    cell_column = cell - cell_row * SIDE
    outside = jnp.where((cell_row < SIDE_SMALL) & (cell_column < SIDE_SMALL), 0.0, -1000000000.0)
    key_bias = jnp.where(image_class == 1, 0.0, outside)[0:1]
    upper = lax.broadcasted_iota(jnp.int32, (cells, LANES), 1) >= LANES // 2

    @pl.loop(0, width // LANES)
    def _(pair):
        lanes = rows_at(pair, LANES)
        query = query_ref[0, :, lanes] * bf16(scale)
        key = key_ref[0, :, lanes]
        value = value_ref[0, :, lanes]
        outs = []
        for half in range(2):
            mine = upper if half else jnp.logical_not(upper)
            scores = dot_nt(jnp.where(mine, query, bf16(0)), key) + key_bias
            top = jnp.max(scores, axis=-1, keepdims=True)
            weights = jnp.exp(scores - top)
            weight_sum = jnp.sum(weights, axis=-1, keepdims=True)
            probs = (weights * (1.0 / weight_sum)).astype(bf16)
            outs.append(dot_nn(probs, value))
            log_total = jnp.broadcast_to(top + jnp.log(weight_sum), (cells, LANES))
            log_total_ref[0, 2 * pair + half] = log_total.T[0:8]
        mixed_ref[0, :, lanes] = jnp.where(upper, outs[1], outs[0]).astype(bf16)

    @pl.loop(0, steps)
    def _(step):
        rows = rows_at(step, chunk)
        resid = (
            tokens_ref[0, rows, :].astype(f32)
            + dot_nn(mixed_ref[0, rows, :], mix_ref[...])
            + line(mix_bias_ref)
        )
        resid_ref[0, rows, :] = resid
        normal, _ = row_norm(resid)
        normed_two_ref[0, rows, :] = (normal * line(gain2_ref) + line(bias2_ref)).astype(bf16)


def attend_forward(
    image_class, tokens, gain1, bias1, joint, query_bias, value_bias, mix, mix_bias, gain2, bias2
):
    images, cells, width = tokens.shape
    row = whole((width,))
    low = jax.ShapeDtypeStruct((images, cells, width), bf16)
    low_spec = per_image((cells, width))
    return pl.pallas_call(
        attend_forward_kernel,
        out_shape=(
            low,
            low,
            low,
            low,
            jax.ShapeDtypeStruct((images, HEADS, 8, cells), f32),
            low,
            jax.ShapeDtypeStruct((images, cells, width), f32),
            low,
        ),
        grid_spec=pltpu.PrefetchScalarGridSpec(
            num_scalar_prefetch=1,
            grid=(images,),
            in_specs=[
                low_spec,
                row,
                row,
                whole((width, 3 * width)),
                row,
                row,
                whole((width, width)),
                row,
                row,
                row,
            ],
            out_specs=[
                low_spec,
                low_spec,
                low_spec,
                low_spec,
                per_image((HEADS, 8, cells)),
                low_spec,
                low_spec,
                low_spec,
            ],
        ),
        compiler_params=pltpu.CompilerParams(vmem_limit_bytes=62 * MIB),
        cost_estimate=cost(35_000_000_000, 30 * MIB),
        name="attend_forward",
    )(image_class, tokens, gain1, bias1, joint, query_bias, value_bias, mix, mix_bias, gain2, bias2)


def feed_kernel(
    class_ref,
    mine_ref,
    core_ref,
    normed_ref,
    resid_ref,
    cotangent_ref,
    expand_ref,
    expand_bias_ref,
    shrink_ref,
    shrink_bias_ref,
    output_ref,
    grad_normed_ref,
    shrink_mine_ref,
    shrink_other_ref,
    expand_mine_ref,
    expand_other_ref,
    grad_expand_bias_ref,
    grad_shrink_bias_ref,
    sent,
    result,
    hidden,
    grad_pre,
    normed_turned,
    shrink_total,
    expand_total,
    biases,
):
    step = pl.program_id(0)
    images, cells, width = normed_ref.shape
    block = expand_ref.shape[1]
    part = cells // 2

    @pl.when(step == 0)
    def _():
        sums = jnp.zeros((8, width), f32)
        for image in range(images):
            keep = spread_lanes(validity_mask(class_ref[image], cells), width)
            grad = cotangent_ref[mine_ref[image]].astype(f32) * keep
            sent[image * cells : (image + 1) * cells, :] = grad.astype(bf16)
            sums = sums + fold(grad)
            result[image * cells : (image + 1) * cells, :] = resid_ref[image] + line(shrink_bias_ref)
            normed_turned[:, image * cells : (image + 1) * cells] = normed_ref[image].T
        grad_shrink_bias_ref[...] = sums
        grad_normed_ref[...] = jnp.zeros_like(grad_normed_ref)
        every = line(expand_bias_ref)
        for k in range(biases.shape[0]):
            biases[k : k + 1, :] = every[:, k * block : (k + 1) * block]

    bias_sums = jnp.zeros((8, expand_ref.shape[1]), f32)
    for image in range(images):
        for piece in range(cells // part):
            local = slice(piece * part, (piece + 1) * part)
            rows = slice(image * cells + piece * part, image * cells + (piece + 1) * part)
            pre = dot_nn(normed_ref[image, local, :], expand_ref[...]) + biases[pl.ds(step, 1), :]
            back = dot_nt(sent[rows, :], shrink_ref[...])
            cdf, pdf = cdf_pdf(pre)
            low = (pre * cdf).astype(bf16)
            hidden[rows, :] = low
            grad = back * (cdf + pre * pdf)
            bias_sums = bias_sums + fold(grad)
            grad_low = grad.astype(bf16)
            grad_pre[rows, :] = grad_low
            result[rows, :] += dot_nn(low, shrink_ref[...])
            grad_normed_ref[image, local, :] += dot_nt(grad_low, expand_ref[...])
    grad_expand_bias_ref[...] = bias_sums
    shrink_total[...] = dot_tn(hidden[...], sent[...])
    expand_total[...] = dot_nn(normed_turned[...], grad_pre[...])
    core = core_ref[0]
    size = shrink_mine_ref.shape[1] * 8
    for pair in range(shrink_mine_ref.shape[0]):
        at = pl.multiple_of((2 * pair + core) * size, 8)
        shrink_mine_ref[pair] = sections_of(shrink_total[pl.ds(at, size), :])
        at = pl.multiple_of((2 * pair + 1 - core) * size, 8)
        shrink_other_ref[pair] = sections_of(shrink_total[pl.ds(at, size), :])
    size = expand_mine_ref.shape[1] * 8
    for pair in range(PAIRS):
        at = pl.multiple_of((2 * pair + core) * size, 8)
        expand_mine_ref[pair] = sections_of(expand_total[pl.ds(at, size), :])
        at = pl.multiple_of((2 * pair + 1 - core) * size, 8)
        expand_other_ref[pair] = sections_of(expand_total[pl.ds(at, size), :])

    @pl.when(step == pl.num_programs(0) - 1)
    def _():
        output_ref[...] = jnp.zeros_like(output_ref)
        for image in range(images):
            keep = spread_lanes(validity_mask(class_ref[image], cells), width)
            rows = result[image * cells : (image + 1) * cells, :] * keep
            output_ref[mine_ref[image]] = rows.astype(bf16)


def feed(image_class, mine, core, normed, resid, cotangent, expand, expand_bias, shrink, shrink_bias):
    images, cells, width = normed.shape
    inner = expand.shape[1]
    slots = cotangent.shape[0]
    block = width // 2
    rows = images * cells
    shrink_size = inner // (2 * PAIRS)
    pairs = block // (2 * shrink_size)
    expand_size = width // (2 * PAIRS)
    shrink_half = jax.ShapeDtypeStruct((PAIRS, shrink_size // 8, 8, width), bf16)
    expand_half = jax.ShapeDtypeStruct((PAIRS, expand_size // 8 * (inner // width), 8, width), bf16)
    shrink_spec = pl.BlockSpec((pairs, shrink_size // 8, 8, width), lambda step, *_: (step, 0, 0, 0))
    expand_spec = pl.BlockSpec(
        (PAIRS, expand_size // 8, 8, block), lambda step, *_: (0, step // 2, 0, step % 2)
    )
    return pl.pallas_call(
        feed_kernel,
        out_shape=(
            jax.ShapeDtypeStruct((slots, cells, width), bf16),
            jax.ShapeDtypeStruct((images, cells, width), f32),
            shrink_half,
            shrink_half,
            expand_half,
            expand_half,
            jax.ShapeDtypeStruct((8, inner), f32),
            jax.ShapeDtypeStruct((8, width), f32),
        ),
        grid_spec=pltpu.PrefetchScalarGridSpec(
            num_scalar_prefetch=3,
            grid=(inner // block,),
            in_specs=[
                whole((images, cells, width)),
                whole((images, cells, width)),
                whole((slots, cells, width)),
                pl.BlockSpec((width, block), lambda step, *_: (0, step)),
                whole((inner,)),
                pl.BlockSpec((block, width), lambda step, *_: (step, 0)),
                whole((width,)),
            ],
            out_specs=[
                whole((slots, cells, width)),
                whole((images, cells, width)),
                shrink_spec,
                shrink_spec,
                expand_spec,
                expand_spec,
                pl.BlockSpec((8, block), lambda step, *_: (0, step)),
                whole((8, width)),
            ],
            scratch_shapes=[
                pltpu.VMEM((rows, width), bf16),
                pltpu.VMEM((rows, width), f32),
                pltpu.VMEM((rows, block), bf16),
                pltpu.VMEM((rows, block), bf16),
                pltpu.VMEM((width, rows), bf16),
                pltpu.VMEM((block, width), f32),
                pltpu.VMEM((width, block), f32),
                pltpu.VMEM((inner // block, block), f32),
            ],
        ),
        compiler_params=pltpu.CompilerParams(vmem_limit_bytes=62 * MIB),
        cost_estimate=cost(12 * rows * width * inner, 40 * MIB),
        name="feed",
    )(image_class, mine, core, normed, resid, cotangent, expand, expand_bias, shrink, shrink_bias)


def row_norm_back(grad, normal, scale, gain):
    inner = grad * gain
    mean = jnp.mean(inner, axis=-1, keepdims=True)
    cross = jnp.mean(inner * normal, axis=-1, keepdims=True)
    return scale * (inner - mean - normal * cross)


def mix_backward_kernel(
    class_ref,
    mine_ref,
    resid_ref,
    cotangent_ref,
    grad_normed_two_ref,
    mix_ref,
    gain2_ref,
    grad_resid_ref,
    grad_mixed_ref,
    sums_ref,
    mask,
):
    image = pl.program_id(0)
    cells, width = resid_ref.shape[1:]
    chunk = 96
    mask[...] = validity_mask(class_ref[image], cells)

    @pl.when(image == 0)
    def _():
        sums_ref[...] = jnp.zeros_like(sums_ref)

    @pl.loop(0, cells // chunk)
    def _(step):
        rows = rows_at(step, chunk)
        normal, row_scale = row_norm(resid_ref[0, rows, :])
        grad = grad_normed_two_ref[0, rows, :]
        sums_ref[0] += fold(grad * normal)
        sums_ref[1] += fold(grad)
        keep = spread_lanes(mask[rows, :], width)
        grad = cotangent_ref[0, rows, :].astype(f32) * keep + row_norm_back(
            grad, normal, row_scale, line(gain2_ref)
        )
        sums_ref[2] += fold(grad)
        grad_resid_ref[0, rows, :] = grad
        grad_mixed_ref[0, rows, :] = dot_nt(grad.astype(bf16), mix_ref[...]).astype(bf16)


def mix_backward(image_class, mine, resid, cotangent, grad_normed_two, mix, gain2):
    images, cells, width = resid.shape
    rows = per_image((cells, width))
    return pl.pallas_call(
        mix_backward_kernel,
        out_shape=(
            jax.ShapeDtypeStruct((images, cells, width), f32),
            jax.ShapeDtypeStruct((images, cells, width), bf16),
            jax.ShapeDtypeStruct((3, 8, width), f32),
        ),
        grid_spec=pltpu.PrefetchScalarGridSpec(
            num_scalar_prefetch=2,
            grid=(images,),
            in_specs=[
                rows,
                pl.BlockSpec((1, cells, width), lambda image, classes, mine: (mine[image], 0, 0)),
                rows,
                whole((width, width)),
                whole((width,)),
            ],
            out_specs=[rows, rows, whole((3, 8, width))],
            scratch_shapes=[pltpu.VMEM((cells, LANES), f32)],
        ),
        compiler_params=pltpu.CompilerParams(vmem_limit_bytes=62 * MIB),
        cost_estimate=cost(2 * images * cells * width * width, 20 * MIB),
        name="mix_backward",
    )(image_class, mine, resid, cotangent, grad_normed_two, mix, gain2)


def attend_backward_kernel(
    class_ref,
    query_ref,
    key_ref,
    value_ref,
    log_total_ref,
    grad_mixed_ref,
    feed_expand_ref,
    feed_shrink_ref,
    mix_sums_ref,
    grad_joint_ref,
    vectors_ref,
    sums_ref,
):
    image = pl.program_id(0)
    cells, width = query_ref.shape[1:]
    scale = (width // HEADS) ** -0.5

    @pl.when(image == 0)
    def _():
        sums_ref[...] = jnp.zeros_like(sums_ref)
        vectors_ref[...] = jnp.zeros_like(vectors_ref)
        for k in range(feed_expand_ref.shape[1] // width):
            vectors_ref[k : k + 1, :] = total(feed_expand_ref[:, k * width : (k + 1) * width])
        vectors_ref[4:5, :] = total(feed_shrink_ref[...])
        for k in range(3):
            vectors_ref[5 + k : 6 + k, :] = total(mix_sums_ref[k])

    upper = lax.broadcasted_iota(jnp.int32, (cells, LANES), 1) >= LANES // 2
    key_bias = (validity_mask(class_ref[image], cells) - 1.0) * 1000000000.0
    bias_wide = jnp.concatenate([key_bias] * 5, axis=1)[:, :cells]

    @pl.loop(0, width // LANES)
    def _(pair):
        lanes = rows_at(pair, LANES)
        query = query_ref[0, :, lanes] * bf16(scale)
        key = key_ref[0, :, lanes]
        value = value_ref[0, :, lanes]
        grad_out = grad_mixed_ref[0, :, lanes]
        grads = []
        for half in range(2):
            mine = upper if half else jnp.logical_not(upper)
            scores = dot_nt(jnp.where(mine, key, bf16(0)), query)
            log_total = log_total_ref[0, 2 * pair + half, 0:1, :]
            probs = jnp.exp(scores + bias_wide - log_total)
            grad_probs = dot_nt(jnp.where(mine, value, bf16(0)), grad_out)
            weighted = probs * grad_probs
            grad_scores = (weighted - probs * total(weighted)).astype(bf16)
            grad_value = dot_nn(probs.astype(bf16), grad_out)
            grad_key = dot_nn(grad_scores, query)
            grad_query = dot_tn(grad_scores, key) * scale
            grads.append((grad_query, grad_key, grad_value))
        for k in range(3):
            grad = jnp.where(upper, grads[1][k], grads[0][k])
            if k != 1:
                sums_ref[k // 2, :, lanes] += fold(grad)
            where = pl.ds(pl.multiple_of(k * width + pair * LANES, LANES), LANES)
            grad_joint_ref[0, :, where] = grad.astype(bf16)

    @pl.when(image == pl.num_programs(0) - 1)
    def _():
        for k in range(2):
            vectors_ref[8 + k : 9 + k, :] = total(sums_ref[k])


def attend_backward(
    image_class, query, key, value, log_total, grad_mixed, sums_expand, sums_shrink, sums_mix
):
    images, cells, width = query.shape
    rows = per_image((cells, width))
    return pl.pallas_call(
        attend_backward_kernel,
        out_shape=(
            jax.ShapeDtypeStruct((images, cells, 3 * width), bf16),
            jax.ShapeDtypeStruct((16, width), f32),
        ),
        grid_spec=pltpu.PrefetchScalarGridSpec(
            num_scalar_prefetch=1,
            grid=(images,),
            in_specs=[
                rows,
                rows,
                rows,
                per_image((HEADS, 8, cells)),
                rows,
                whole(sums_expand.shape),
                whole(sums_shrink.shape),
                whole(sums_mix.shape),
            ],
            out_specs=[per_image((cells, 3 * width)), whole((16, width))],
            scratch_shapes=[pltpu.VMEM((2, 8, width), f32)],
        ),
        compiler_params=pltpu.CompilerParams(vmem_limit_bytes=62 * MIB),
        cost_estimate=cost(40 * images * cells * cells * width, 12 * MIB),
        name="attend_backward",
    )(image_class, query, key, value, log_total, grad_mixed, sums_expand, sums_shrink, sums_mix)


def joint_backward_kernel(
    core_ref,
    tokens_ref,
    normed_ref,
    mixed_ref,
    grad_resid_ref,
    grad_joint_ref,
    gain1_ref,
    joint_ref,
    grad_tokens_ref,
    mine_ref,
    other_ref,
    sums,
    resid_low,
    joint_total,
    mix_total,
):
    image = pl.program_id(0)
    last = pl.num_programs(0) - 1
    cells, width = tokens_ref.shape[1:]
    chunk = 96
    block = 256

    @pl.when(image == 0)
    def _():
        sums[...] = jnp.zeros_like(sums)
        joint_total[...] = jnp.zeros_like(joint_total)
        mix_total[...] = jnp.zeros_like(mix_total)

    @pl.loop(0, 3 * width // block)
    def _(step):
        here = rows_at(step, block)
        joint_total[:, here] += dot_tn(normed_ref[0], grad_joint_ref[0, :, here])

    @pl.loop(0, cells // chunk)
    def _(step):
        rows = rows_at(step, chunk)
        normal, row_scale = row_norm(tokens_ref[0, rows, :].astype(f32))
        grad = dot_nt(grad_joint_ref[0, rows, :], joint_ref[...])
        sums[0] += fold(grad * normal)
        sums[1] += fold(grad)
        back = row_norm_back(grad, normal, row_scale, line(gain1_ref))
        grad_resid = grad_resid_ref[0, rows, :]
        resid_low[rows, :] = grad_resid.astype(bf16)
        grad_tokens_ref[0, rows, :] = (grad_resid + back).astype(bf16)

    mix_total[...] += dot_tn(mixed_ref[0], resid_low[...])

    @pl.when(image == last)
    def _():
        core = core_ref[0]
        size = width // (2 * PAIRS)
        parts = size // 8
        for pair in range(PAIRS):
            for ref, side in ((mine_ref, core), (other_ref, 1 - core)):
                at = pl.ds(pl.multiple_of((2 * pair + side) * size, 8), size)
                for k in range(3):
                    ref[pair, k * parts : (k + 1) * parts] = sections_of(
                        joint_total[at, k * width : (k + 1) * width]
                    )
                ref[pair, 3 * parts : 4 * parts] = sections_of(mix_total[at, :])


def joint_backward(
    core, tokens, normed, mixed, grad_resid, grad_joint, gain1, joint
):
    images, cells, width = tokens.shape
    rows = per_image((cells, width))
    size = width // (2 * PAIRS)
    half = (PAIRS, 4 * size // 8, 8, width)
    return pl.pallas_call(
        joint_backward_kernel,
        out_shape=(
            jax.ShapeDtypeStruct((images, cells, width), bf16),
            jax.ShapeDtypeStruct(half, bf16),
            jax.ShapeDtypeStruct(half, bf16),
            jax.ShapeDtypeStruct((2, 8, width), f32),
        ),
        grid_spec=pltpu.PrefetchScalarGridSpec(
            num_scalar_prefetch=1,
            grid=(images,),
            in_specs=[
                rows,
                rows,
                rows,
                rows,
                per_image((cells, 3 * width)),
                whole((width,)),
                whole((width, 3 * width)),
            ],
            out_specs=[rows, whole(half), whole(half), whole((2, 8, width))],
            scratch_shapes=[
                pltpu.VMEM((cells, width), bf16),
                pltpu.VMEM((width, 3 * width), f32),
                pltpu.VMEM((width, width), f32),
            ],
        ),
        compiler_params=pltpu.CompilerParams(vmem_limit_bytes=62 * MIB),
        cost_estimate=cost(14 * images * cells * width * width, 25 * MIB),
        name="joint_backward",
    )(
        core,
        tokens,
        normed,
        mixed,
        grad_resid,
        grad_joint,
        gain1,
        joint,
    )


def norm_means(sums, gain, per_group, count):
    inverse = 1.0 / (count * per_group)
    return [group_total(total(item) * gain, per_group) * inverse for item in sums]


def embed_backward_kernel(
    class_ref,
    core_ref,
    grad_tokens_ref,
    x_ref,
    third_ref,
    stat3_ref,
    stem_ref,
    gain3_ref,
    bias3_ref,
    embed_ref,
    grad_inner_ref,
    grad_third_ref,
    mine_ref,
    other_ref,
    sums_embed_ref,
    sums3_ref,
    mask,
    embed_total,
    grad_position,
    position_total,
):
    image = pl.program_id(0)
    last = pl.num_programs(0) - 1
    cells, channels = x_ref.shape[1:]
    width = embed_ref.shape[1]
    chunk = 96
    steps = cells // chunk
    image_class = class_ref[image]
    mask[...] = validity_mask(image_class, cells)
    count = valid_count(image_class)

    @pl.when(image == 0)
    def _():
        for ref in (grad_position, sums_embed_ref, sums3_ref, embed_total):
            ref[...] = jnp.zeros_like(ref)

    @pl.loop(0, steps)
    def _(step):
        rows = rows_at(step, chunk)
        grad = grad_tokens_ref[0, rows, :].astype(f32) * spread_lanes(mask[rows, :], width)
        grad_position[rows, :] += grad
        sums_embed_ref[...] += fold(grad)

    embed_total[...] += dot_tn(stem_ref[0], grad_tokens_ref[0])
    centre, scale = stat3_ref[0, 0:1, :], stat3_ref[0, 1:2, :]
    gain = line(gain3_ref)

    def third_step(step, carry):
        rows = rows_at(step, chunk)
        keep = spread_lanes(mask[rows, :], channels)
        grad = dot_nt(grad_tokens_ref[0, rows, :], embed_ref[...]) * keep
        normal = (third_ref[0, rows, :] - centre) * scale
        argument = x_ref[0, rows, :] * keep + normal * gain + line(bias3_ref)
        cdf, pdf = cdf_pdf(argument)
        grad = grad * (cdf + argument * pdf)
        grad_inner_ref[0, rows, :] = grad
        return carry[0] + fold(grad * normal), carry[1] + fold(grad)

    zeros = jnp.zeros((8, channels), f32)
    with_normal, plain = lax.fori_loop(0, steps, third_step, (zeros, zeros))
    sums3_ref[0] += with_normal
    sums3_ref[1] += plain
    mean, cross = norm_means((plain, with_normal), gain, channels // GROUPS, count)
    outer = scale * gain
    mean = mean * scale
    cross = cross * scale

    @pl.loop(0, steps)
    def _(step):
        rows = rows_at(step, chunk)
        keep = spread_lanes(mask[rows, :], channels)
        normal = (third_ref[0, rows, :] - centre) * scale
        grad = (grad_inner_ref[0, rows, :] * outer - mean - normal * cross) * keep
        grad_third_ref[0, rows, :] = grad.astype(bf16)

    @pl.when(image == last)
    def _():
        core = core_ref[0]
        position_rows = cells // (2 * PAIRS)
        position_total[...] = jnp.zeros_like(position_total)
        for block in range(2 * PAIRS):
            position_total[block, 0:position_rows, :] = grad_position[
                block * position_rows : (block + 1) * position_rows, :
            ]
        size = channels // (2 * PAIRS)
        for pair in range(PAIRS):
            for ref, side in ((mine_ref, core), (other_ref, 1 - core)):
                block = 2 * pair + side
                at = pl.ds(pl.multiple_of(block * size, 8), size)
                ref[pair, 0 : size // 8] = sections_of(embed_total[at, :])
                ref[pair, size // 8 :] = sections_of(position_total[block])


def embed_backward(image_class, core, grad_tokens, x, third, stat3, stem, gain3, bias3, embed):
    images, cells, channels = x.shape
    width = embed.shape[1]
    position_rows = -(-cells // (2 * PAIRS) // 8) * 8
    half = (PAIRS, (channels // (2 * PAIRS) + position_rows) // 8, 8, width)
    return pl.pallas_call(
        embed_backward_kernel,
        out_shape=(
            jax.ShapeDtypeStruct((images, cells, channels), f32),
            jax.ShapeDtypeStruct((images, cells, channels), bf16),
            jax.ShapeDtypeStruct(half, bf16),
            jax.ShapeDtypeStruct(half, bf16),
            jax.ShapeDtypeStruct((8, width), f32),
            jax.ShapeDtypeStruct((2, 8, channels), f32),
        ),
        grid_spec=pltpu.PrefetchScalarGridSpec(
            num_scalar_prefetch=2,
            grid=(images,),
            in_specs=[
                per_image((cells, width)),
                per_image((cells, channels)),
                per_image((cells, channels)),
                per_image((8, channels)),
                per_image((cells, channels)),
                whole((channels,)),
                whole((channels,)),
                whole((channels, width)),
            ],
            out_specs=[
                per_image((cells, channels)),
                per_image((cells, channels)),
                whole(half),
                whole(half),
                whole((8, width)),
                whole((2, 8, channels)),
            ],
            scratch_shapes=[
                pltpu.VMEM((cells, LANES), f32),
                pltpu.VMEM((channels, width), f32),
                pltpu.VMEM((cells, width), f32),
                pltpu.VMEM((2 * PAIRS, position_rows, width), f32),
            ],
        ),
        compiler_params=pltpu.CompilerParams(vmem_limit_bytes=62 * MIB),
        cost_estimate=cost(20_000_000_000, 30 * MIB),
        name="embed_backward",
    )(image_class, core, grad_tokens, x, third, stat3, stem, gain3, bias3, embed)


def convs_backward_kernel(
    class_ref,
    core_ref,
    grad_third_ref,
    x_ref,
    first_ref,
    second_ref,
    stat1_ref,
    stat2_ref,
    std_in_ref,
    std_mid_ref,
    std_out_ref,
    w_in_ref,
    w_mid_ref,
    w_out_ref,
    gain1_ref,
    bias1_ref,
    gain2_ref,
    bias2_ref,
    sums_embed_ref,
    sums3_ref,
    sums_attn_ref,
    grad_first_ref,
    mine_ref,
    other_ref,
    vectors,
    sums1,
    sums2,
    mask,
    act,
    padded,
    columns,
    in_total,
    mid_total,
    out_total,
    mid_done,
    in_done,
):
    image = pl.program_id(0)
    last = pl.num_programs(0) - 1
    cells, channels = x_ref.shape[1:]
    width = sums_embed_ref.shape[1]
    middle = first_ref.shape[2]
    image_class = class_ref[image]
    mask[...] = validity_mask(image_class, cells)
    count = valid_count(image_class)

    @pl.when(image == 0)
    def _():
        for ref in (sums1, sums2, in_total, mid_total, out_total):
            ref[...] = jnp.zeros_like(ref)

    def middle_norm(values_ref, stat_ref, gain_ref, bias_ref, sums_ref, grad_of):
        centre, scale = stat_ref[0, 0:1, :], stat_ref[0, 1:2, :]
        gain = line(gain_ref)
        keep = spread_lanes(mask[...], middle)
        normal = (values_ref[0] - centre) * scale
        argument = normal * gain + line(bias_ref)
        cdf, pdf = cdf_pdf(argument)
        act[...] = (argument * cdf * keep).astype(bf16)
        grad = grad_of() * keep * (cdf + argument * pdf)
        plain, with_normal = fold(grad), fold(grad * normal)
        sums_ref[0] += with_normal
        sums_ref[1] += plain
        mean, cross = norm_means((plain, with_normal), gain, middle // GROUPS, count)
        return (grad * (scale * gain) - mean * scale - normal * (cross * scale)) * keep

    grad_second = middle_norm(
        second_ref,
        stat2_ref,
        gain2_ref,
        bias2_ref,
        sums2,
        lambda: dot_nt(grad_third_ref[0], std_out_ref[...]),
    )
    out_total[...] += dot_tn(act[...], grad_third_ref[0])
    fill_columns(grad_second, padded, columns, -1)

    def spread_back():
        grad = jnp.zeros((cells, middle), f32)
        for tap in range(9):
            part = slice(tap * middle, (tap + 1) * middle)
            grad = grad + dot_nt(columns[:, part], std_mid_ref[part, :])
        return grad

    grad = middle_norm(first_ref, stat1_ref, gain1_ref, bias1_ref, sums1, spread_back)
    grad_low = grad.astype(bf16)
    grad_first_ref[0] = grad_low
    mid_total[...] += dot_tn(act[...], columns[...])
    low = (x_ref[0] * spread_lanes(mask[...], channels)).astype(bf16)
    in_total[...] += dot_tn(grad_low, low)

    @pl.when(image == last)
    def _():
        core = core_ref[0]
        out_total[...] = standardize_back(w_out_ref[...].astype(f32), out_total[...])
        in_done[...] = standardize_back(w_in_ref[...].astype(f32), in_total[...].T)
        rows = 9 * middle
        normal, scale = standardized(w_mid_ref[...].astype(f32))
        grads = [mid_total[:, tap * middle : (tap + 1) * middle] for tap in range(9)]
        grad_mean = sum(total(g) for g in grads) * (1.0 / rows)
        inner = sum(
            total(g * normal[tap * middle : (tap + 1) * middle]) for tap, g in enumerate(grads)
        ) * (1.0 / rows)
        for tap, g in enumerate(grads):
            part = slice(tap * middle, (tap + 1) * middle)
            mid_done[part, :] = scale * (g - grad_mean - normal[part] * inner)
        in_size = channels // (2 * PAIRS)
        mid_size = rows // (2 * PAIRS)
        out_size = middle // (2 * PAIRS)
        in_parts = in_size // 8
        mid_parts = mid_size // 8
        for pair in range(PAIRS):
            for ref, side in ((mine_ref, core), (other_ref, 1 - core)):
                block = 2 * pair + side
                at = pl.ds(pl.multiple_of(block * in_size, 8), in_size)
                ref[pair, 0:in_parts] = sections_of(in_done[at, :])
                at = pl.ds(pl.multiple_of(block * mid_size, 8), mid_size)
                ref[pair, in_parts : in_parts + mid_parts] = sections_of(mid_done[at, :])
                at = pl.ds(pl.multiple_of(block * out_size, 8), out_size)
                for k in range(channels // middle):
                    ref[pair, in_parts + mid_parts + k] = out_total[
                        at, k * middle : (k + 1) * middle
                    ].astype(bf16)
        vectors[...] = jnp.zeros_like(vectors)
        row = 0
        for item in (
            total(sums_embed_ref[...]),
            total(sums_attn_ref[0]),
            total(sums_attn_ref[1]),
            total(sums1[0]),
            total(sums1[1]),
            total(sums2[0]),
            total(sums2[1]),
            total(sums3_ref[0]),
            total(sums3_ref[1]),
        ):
            for start in range(0, item.shape[1], middle):
                vectors[row : row + 1, :] = item[:, start : start + middle]
                row += 1
        mine_ref[PAIRS] = jnp.zeros(mine_ref.shape[1:], bf16)
        store_split(mine_ref.at[PAIRS], 0, vectors[...])
        other_ref[PAIRS] = mine_ref[PAIRS]


def convs_backward(
    image_class,
    core,
    grad_third,
    x,
    first,
    second,
    stat1,
    stat2,
    stds,
    weights,
    norms,
    sums_embed,
    sums3,
    sums_attn,
):
    images, cells, channels = x.shape
    middle = first.shape[2]
    width = sums_embed.shape[1]
    row = lambda size: whole((size,))
    conv_rows = channels // (2 * PAIRS) + 9 * middle // (2 * PAIRS) + middle // (2 * PAIRS) * (channels // middle)
    half = (PAIRS + 1, conv_rows // 8, 8, middle)
    return pl.pallas_call(
        convs_backward_kernel,
        out_shape=(
            jax.ShapeDtypeStruct((images, cells, middle), bf16),
            jax.ShapeDtypeStruct(half, bf16),
            jax.ShapeDtypeStruct(half, bf16),
        ),
        grid_spec=pltpu.PrefetchScalarGridSpec(
            num_scalar_prefetch=2,
            grid=(images,),
            in_specs=[
                per_image((cells, channels)),
                per_image((cells, channels)),
                per_image((cells, middle)),
                per_image((cells, middle)),
                per_image((8, middle)),
                per_image((8, middle)),
                whole((channels, middle)),
                whole((9 * middle, middle)),
                whole((middle, channels)),
                whole((channels, middle)),
                whole((9 * middle, middle)),
                whole((middle, channels)),
                row(middle),
                row(middle),
                row(middle),
                row(middle),
                whole((8, width)),
                whole((2, 8, channels)),
                whole((2, 8, width)),
            ],
            out_specs=[
                per_image((cells, middle)),
                whole(half),
                whole(half),
            ],
            scratch_shapes=[
                pltpu.VMEM((VECTORS * 8, middle), f32),
                pltpu.VMEM((2, 8, middle), f32),
                pltpu.VMEM((2, 8, middle), f32),
                pltpu.VMEM((cells, LANES), f32),
                pltpu.VMEM((cells, middle), bf16),
                pltpu.VMEM((3, cells + 2 * SIDE, middle), f32),
                pltpu.VMEM((cells, 9 * middle), bf16),
                pltpu.VMEM((middle, channels), f32),
                pltpu.VMEM((middle, 9 * middle), f32),
                pltpu.VMEM((middle, channels), f32),
                pltpu.VMEM((9 * middle, middle), f32),
                pltpu.VMEM((channels, middle), f32),
            ],
        ),
        compiler_params=pltpu.CompilerParams(vmem_limit_bytes=62 * MIB),
        cost_estimate=cost(20_000_000_000, 20 * MIB),
        name="convs_backward",
    )(
        image_class,
        core,
        grad_third,
        x,
        first,
        second,
        stat1,
        stat2,
        *stds,
        *weights,
        *norms[:4],
        sums_embed,
        sums3,
        sums_attn,
    )


def input_backward_kernel(class_ref, grad_inner_ref, grad_first_ref, std_in_ref, input_grad_ref):
    cells, channels = grad_inner_ref.shape[1:]
    keep = spread_lanes(validity_mask(class_ref[pl.program_id(0)], cells), channels)
    back = dot_nt(grad_first_ref[0], std_in_ref[...])
    input_grad_ref[0] = (grad_inner_ref[0] + back) * keep


def input_backward(image_class, grad_inner, grad_first, std_in):
    images, cells, channels = grad_inner.shape
    middle = grad_first.shape[2]
    return pl.pallas_call(
        input_backward_kernel,
        out_shape=jax.ShapeDtypeStruct((images, cells, channels), f32),
        grid_spec=pltpu.PrefetchScalarGridSpec(
            num_scalar_prefetch=1,
            grid=(images,),
            in_specs=[
                per_image((cells, channels)),
                per_image((cells, middle)),
                whole((channels, middle)),
            ],
            out_specs=per_image((cells, channels)),
        ),
        compiler_params=pltpu.CompilerParams(vmem_limit_bytes=62 * MIB),
        cost_estimate=cost(2 * images * cells * channels * middle, 12 * MIB),
        name="input_backward",
    )(image_class, grad_inner, grad_first, std_in)


def combine_core_kernel(plane_ref, *refs, arrays, extra):
    mines, others, outs = refs[:arrays], refs[arrays : 2 * arrays], refs[2 * arrays :]
    start = 0
    for mine, other in zip(mines, others):
        size = mine.shape[1]
        for z in range(mine.shape[0] // 4):
            for q in range(4):
                at = 4 * z + lax.bitwise_xor(plane_ref[0], q)
                summed = mine[at].astype(f32) + other[at].astype(f32)
                outs[q][z, start : start + size] = summed.astype(bf16)
        start += size
    if extra:
        vectors = load_split(mines[0].at[PAIRS], 0) + load_split(others[0].at[PAIRS], 0)
        for out in outs:
            out[PAIRS // 4] = jnp.zeros(out.shape[1:], bf16)
            store_split(out.at[PAIRS // 4], 0, vectors)


def combine_core(plane, mines, others, extra):
    arrays = len(mines)
    depth = PAIRS // 4
    steps = 1 if extra else depth
    out_shape = (sum(item.shape[1] for item in mines),) + mines[0].shape[2:]
    in_spec = lambda item: pl.BlockSpec(
        (item.shape[0] // steps,) + item.shape[1:], lambda step, *_: (step, 0, 0, 0)
    )
    out_spec = pl.BlockSpec(((depth + extra) // steps,) + out_shape, lambda step, *_: (step, 0, 0, 0))
    size = sum(item.size for item in mines)
    return pl.pallas_call(
        lambda *refs: combine_core_kernel(*refs, arrays=arrays, extra=extra),
        out_shape=[jax.ShapeDtypeStruct((depth + extra,) + out_shape, bf16)] * 4,
        grid_spec=pltpu.PrefetchScalarGridSpec(
            num_scalar_prefetch=1,
            grid=(steps,),
            in_specs=[in_spec(item) for item in mines] * 2,
            out_specs=[out_spec] * 4,
        ),
        compiler_params=pltpu.CompilerParams(vmem_limit_bytes=62 * MIB),
        cost_estimate=cost(size, 6 * size),
        name="combine_core",
    )(plane, *mines, *others)


def four(values):
    return (values[0] + values[1]) + (values[2] + values[3])


def combine_plane_kernel(depth_ref, *refs, extra):
    parts, outs = refs[:4], refs[4:]
    size = parts[0].shape[1]
    for q in range(4):
        at = lax.bitwise_xor(depth_ref[0], q)
        outs[q][0:size] = four([part[at].astype(f32) for part in parts]).astype(bf16)
    if extra:
        vectors = four([load_split(part.at[PAIRS // 4], 0) for part in parts])
        for out in outs:
            store_split(out, size, vectors)


def combine_plane(depth, parts, extra):
    shape = (parts[0].shape[1] + 2 * VECTORS * extra,) + parts[0].shape[2:]
    size = 4 * parts[0].size
    return pl.pallas_call(
        lambda *refs: combine_plane_kernel(*refs, extra=extra),
        out_shape=[jax.ShapeDtypeStruct(shape, bf16)] * 4,
        grid_spec=pltpu.PrefetchScalarGridSpec(
            num_scalar_prefetch=1,
            grid=(1,),
            in_specs=[whole(item.shape) for item in parts],
            out_specs=[whole(shape)] * 4,
        ),
        compiler_params=pltpu.CompilerParams(vmem_limit_bytes=62 * MIB),
        cost_estimate=cost(size, 3 * size),
        name="combine_plane",
    )(depth, *parts)


def store_lines(outs, vectors, lines):
    for out, pieces in zip(outs, lines):
        out[...] = jnp.concatenate(
            [vectors[row : row + 1, 0:size] for row, size in pieces], axis=1
        ).reshape(-1)


def line_shapes(lines):
    return [jax.ShapeDtypeStruct((sum(size for _, size in pieces),), f32) for pieces in lines]


def combine_depth_kernel(*refs, places, lines):
    parts, outs = refs[:4], refs[4:]
    count = len(places)
    summed = four([part[0:count].astype(f32) for part in parts])
    for section, (out, row, column, columns, rows) in enumerate(places):
        stride = columns // LANES
        for lane in range(summed.shape[2] // LANES):
            start = row * stride + column // LANES + lane
            outs[out][pl.ds(start, rows, stride=stride), :] = summed[
                section, 0:rows, lane * LANES : (lane + 1) * LANES
            ]
    if lines:
        vectors = four([load_split(part, count) for part in parts])
        store_lines(outs[len(outs) - len(lines) :], vectors, lines)


def combine_depth(parts, places, sizes, lines):
    shapes = [jax.ShapeDtypeStruct((size // LANES, LANES), f32) for size in sizes] + line_shapes(lines)
    size = 4 * parts[0].size
    outs = pl.pallas_call(
        lambda *refs: combine_depth_kernel(*refs, places=places, lines=lines),
        out_shape=shapes,
        grid=(1,),
        in_specs=[whole(item.shape) for item in parts],
        out_specs=[whole(item.shape) for item in shapes],
        compiler_params=pltpu.CompilerParams(vmem_limit_bytes=62 * MIB),
        cost_estimate=cost(size, 3 * size),
        name="combine_depth",
    )(*parts)
    return [item.reshape(-1) for item in outs[: len(sizes)]], list(outs[len(sizes) :])


def sum_vectors_kernel(gathered_ref, *outs, lines):
    store_lines(outs, jnp.sum(gathered_ref[...], axis=0), lines)


def sum_vectors(gathered, lines):
    shapes = line_shapes(lines)
    return pl.pallas_call(
        lambda *refs: sum_vectors_kernel(*refs, lines=lines),
        out_shape=shapes,
        grid=(1,),
        in_specs=[whole(gathered.shape)],
        out_specs=[whole(item.shape) for item in shapes],
        compiler_params=pltpu.CompilerParams(vmem_limit_bytes=62 * MIB),
        name="sum_vectors",
    )(gathered)


def permuted(item, distance, devices):
    return lax.ppermute(item, BOTH, [(k, k ^ distance) for k in range(devices)])


class Sums:
    def __init__(self, index, devices):
        self.devices = devices
        self.plane = ((index // 2) % 4).astype(jnp.int32).reshape(1)
        self.depth = (index // 8).astype(jnp.int32).reshape(1)

    def spread(self, parts, unit):
        return [parts[0]] + [permuted(parts[q], q * unit, self.devices) for q in (1, 2, 3)]

    def start_core(self, mines, others):
        return mines, [permuted(item, 1, self.devices) for item in others]

    def end_core(self, started, extra=0):
        return combine_core(self.plane, *started, extra)

    def start_plane(self, parts):
        return self.spread(parts, 2)

    def end_plane(self, started, extra=0):
        return combine_plane(self.depth, started, extra)

    def start_depth(self, parts):
        return self.spread(parts, 8)


def after(value, *others):
    return lax.optimization_barrier((value,) + others)[0]


def ahead(value, others):
    leaves, tree = jax.tree.flatten(others)
    held = lax.optimization_barrier((value, *leaves))
    return jax.tree.unflatten(tree, held[1:])


def octets(out, rows, columns, width, offset=0):
    return [
        (out, 8 * part, start, columns, min(8, rows - 8 * part))
        for start in range(0, columns, width)
        for part in range(-(-rows // 8))
    ]


def scattered(mine, other, places, sizes, devices):
    blocks = jnp.stack([mine, other], axis=1).reshape((2 * PAIRS,) + mine.shape[1:])
    results = []
    for out, size in sizes:
        chosen = [k for k, place in enumerate(places) if place[0] == out]
        columns = places[chosen[0]][3]
        width = mine.shape[-1]
        rows = size // columns
        groups = columns // width
        values = blocks[:, chosen[0] : chosen[-1] + 1]
        values = values.reshape(2 * PAIRS, groups, -1, width)[:, :, :rows]
        values = jnp.moveaxis(values, 1, 2).reshape(devices, -1)
        length = values.shape[1]
        padded = -(-length // LANES) * LANES
        values = jnp.pad(values, ((0, 0), (0, padded - length))).reshape(devices, -1, LANES)
        own = lax.psum_scatter(values, BOTH, scatter_dimension=0, tiled=True)
        results.append(own.astype(f32).reshape(-1)[:length])
    return results


def shards(
    stem_input,
    image_class,
    owner,
    conv_in_weight,
    first_gain,
    first_bias,
    conv_mid_weight,
    second_gain,
    second_bias,
    conv_out_weight,
    third_gain,
    third_bias,
    embed_weight,
    embed_bias,
    position_table,
    attn_gain,
    attn_bias,
    joint_weight,
    query_bias,
    value_bias,
    mix_weight,
    mix_bias,
    mlp_gain,
    mlp_bias,
    expand_weight,
    expand_bias,
    shrink_weight,
    shrink_bias,
    cotangent,
):
    sections = lax.axis_size("section")
    devices = sections * lax.axis_size("batch")
    staged = (devices, sections) == (2 * PAIRS, 4)
    index = lax.axis_index(BOTH)
    images, cells, channels = stem_input.shape
    middle = conv_in_weight.shape[1]
    width = embed_weight.shape[1]
    inner = expand_weight.shape[1]
    section_index = lax.axis_index("section")
    mine = lax.dynamic_index_in_dim(owner.reshape(sections, images), section_index, 0, keepdims=False)
    core = ((index % 2) if staged else jnp.zeros((), jnp.int32)).astype(jnp.int32).reshape(1)
    received = lax.all_to_all(cotangent[0], "section", split_axis=0, concat_axis=0, tiled=True)
    norms = (first_gain, first_bias, second_gain, second_bias, third_gain, third_bias)
    weights = (conv_in_weight, conv_mid_weight.reshape(-1, middle), conv_out_weight)
    std_in, std_mid, std_out, first, second, third, stat1, stat2, stat3, stem, tokens = stem_forward(
        image_class, stem_input, *weights, norms, embed_weight, embed_bias, position_table
    )
    normed, query, key, value, log_total, mixed, resid, normed_two = attend_forward(
        image_class,
        tokens,
        attn_gain,
        attn_bias,
        joint_weight,
        query_bias,
        value_bias,
        mix_weight,
        mix_bias,
        mlp_gain,
        mlp_bias,
    )
    (
        outgoing,
        grad_normed_two,
        shrink_mine,
        shrink_other,
        expand_mine,
        expand_other,
        sums_expand,
        sums_shrink,
    ) = feed(
        image_class,
        mine,
        core,
        normed_two,
        resid,
        received,
        expand_weight,
        expand_bias,
        shrink_weight,
        shrink_bias,
    )
    sums = Sums(index, devices)
    if staged:
        feed_core = sums.start_core([shrink_mine, expand_mine], [shrink_other, expand_other])
    arrived = lax.all_to_all(outgoing, "section", split_axis=0, concat_axis=0, tiled=True)
    grad_resid, grad_mixed, sums_mix = mix_backward(
        image_class, mine, resid, received, grad_normed_two, mix_weight, mlp_gain
    )
    if staged:
        feed_core = ahead(grad_resid, feed_core)
        feed_plane = sums.start_plane(sums.end_core(feed_core))
        grad_mixed = after(grad_mixed, feed_plane[0])
    grad_joint, vectors_block = attend_backward(
        image_class, query, key, value, log_total, grad_mixed, sums_expand, sums_shrink, sums_mix
    )
    gathered = lax.all_gather(vectors_block, BOTH)
    grad_tokens, joint_mine, joint_other, sums_attn = joint_backward(
        core, tokens, normed, mixed, grad_resid, grad_joint, attn_gain, joint_weight
    )
    if staged:
        joint_core = sums.start_core([joint_mine], [joint_other])
        feed_plane, arrived = ahead(grad_tokens, (feed_plane, arrived))
        feed_depth = sums.start_depth(sums.end_plane(feed_plane))
        grad_tokens = after(grad_tokens, feed_depth[0], arrived)
    block_output = arrived[None]
    grad_inner, grad_third, embed_mine, embed_other, sums_embed, sums3 = embed_backward(
        image_class,
        core,
        grad_tokens,
        stem_input,
        third,
        stat3,
        stem,
        third_gain,
        third_bias,
        embed_weight,
    )
    if staged:
        embed_core = sums.start_core([embed_mine], [embed_other])
        joint_core, feed_depth = ahead(grad_third, (joint_core, feed_depth))
        joint_plane = sums.start_plane(sums.end_core(joint_core))
        grad_third = after(grad_third, joint_plane[0], *feed_depth)
    grad_first, conv_mine, conv_other = convs_backward(
        image_class,
        core,
        grad_third,
        stem_input,
        first,
        second,
        stat1,
        stat2,
        (std_in, std_mid, std_out),
        weights,
        norms,
        sums_embed,
        sums3,
        sums_attn,
    )
    if staged:
        embed_core, joint_plane = ahead(grad_first, (embed_core, joint_plane))
        conv_other = after(conv_other, *joint_plane)
        conv_core = sums.start_core([conv_mine], [conv_other])
        embed_plane = sums.start_plane(sums.end_core(embed_core))
        joint_depth = sums.start_depth(sums.end_plane(joint_plane))
        grad_first = after(grad_first, embed_plane[0], joint_depth[0])
    input_grad = input_backward(image_class, grad_inner, grad_first, std_in)

    parts = 2 * PAIRS
    shrink_places = octets(0, inner // parts, width, width)
    expand_places = octets(1, width // parts, inner, width)
    feed_sizes = [inner // parts * width] * 2
    joint_places = octets(0, width // parts, 3 * width, width) + octets(1, width // parts, width, width)
    joint_sizes = [3 * width * width // parts, width * width // parts]
    embed_places = octets(0, channels // parts, width, width) + octets(1, cells // parts, width, width)
    embed_sizes = [channels * width // parts, cells * width // parts]
    conv_places = (
        octets(0, channels // parts, middle, middle)
        + octets(1, 9 * middle // parts, middle, middle)
        + octets(2, middle // parts, channels, middle)
    )
    conv_sizes = [
        channels * middle // parts,
        9 * middle * middle // parts,
        middle * channels // parts,
    ]
    block_lines = [[(row, width) for row in range(inner // width)]] + [
        [(row, width)] for row in range(inner // width, inner // width + 6)
    ]
    stem_lines = []
    row = 0
    for size in [width] * 3 + [middle] * 4 + [channels] * 2:
        stem_lines.append([(row + k, middle) for k in range(size // middle)])
        row += size // middle
    block_vectors = sum_vectors(gathered.reshape((-1,) + vectors_block.shape), block_lines)
    if staged:
        conv_plane = sums.start_plane(sums.end_core(conv_core, 1))
        embed_depth = sums.start_depth(sums.end_plane(embed_plane))
        conv_depth = sums.start_depth(sums.end_plane(conv_plane, 1))
        (grad_shrink, grad_expand), _ = combine_depth(
            feed_depth, shrink_places + expand_places, feed_sizes, []
        )
        (grad_joint, grad_mix), _ = combine_depth(joint_depth, joint_places, joint_sizes, [])
        (grad_embed, grad_position), _ = combine_depth(embed_depth, embed_places, embed_sizes, [])
        (grad_in, grad_mid, grad_out), stem_vectors = combine_depth(
            conv_depth, conv_places, conv_sizes, stem_lines
        )
    else:
        (grad_shrink,) = scattered(
            shrink_mine, shrink_other, shrink_places, [(0, feed_sizes[0])], devices
        )
        (grad_expand,) = scattered(
            expand_mine, expand_other, expand_places, [(1, feed_sizes[1])], devices
        )
        grad_joint, grad_mix = scattered(
            joint_mine, joint_other, joint_places, list(enumerate(joint_sizes)), devices
        )
        grad_embed, grad_position = scattered(
            embed_mine, embed_other, embed_places, list(enumerate(embed_sizes)), devices
        )
        rows = conv_mine[PAIRS, :VECTORS].astype(f32) + conv_mine[PAIRS, VECTORS : 2 * VECTORS].astype(f32)
        rows = lax.psum(rows.reshape(-1, middle), BOTH)
        stem_vectors = [rows[pieces[0][0] : pieces[-1][0] + 1].reshape(-1) for pieces in stem_lines]
        conv_mine, conv_other = conv_mine[:PAIRS], conv_other[:PAIRS]
        grad_in, grad_mid, grad_out = scattered(
            conv_mine, conv_other, conv_places, list(enumerate(conv_sizes)), devices
        )
    (
        grad_expand_bias,
        grad_shrink_bias,
        grad_mlp_gain,
        grad_mlp_bias,
        grad_mix_bias,
        grad_query_bias,
        grad_value_bias,
    ) = block_vectors
    (
        grad_embed_bias,
        grad_attn_gain,
        grad_attn_bias,
        grad_first_gain,
        grad_first_bias,
        grad_second_gain,
        grad_second_bias,
        grad_third_gain,
        grad_third_bias,
    ) = stem_vectors
    return (
        block_output,
        input_grad,
        grad_in,
        grad_first_gain,
        grad_first_bias,
        grad_mid,
        grad_second_gain,
        grad_second_bias,
        grad_out,
        grad_third_gain,
        grad_third_bias,
        grad_embed,
        grad_embed_bias,
        grad_position,
        grad_attn_gain,
        grad_attn_bias,
        grad_joint,
        grad_query_bias,
        grad_value_bias,
        grad_mix,
        grad_mix_bias,
        grad_mlp_gain,
        grad_mlp_bias,
        grad_expand,
        grad_expand_bias,
        grad_shrink,
        grad_shrink_bias,
    )


def solution(mesh):
    split = P(BOTH)
    images = P(BOTH, None, None)
    slots = P(BOTH, None, None, None)
    full = P()
    in_specs = (images, split, P("batch")) + (full,) * 25 + (slots,)
    out_specs = (
        slots,
        images,
        split,
        full,
        full,
        split,
        full,
        full,
        split,
        full,
        full,
        split,
        full,
        split,
        full,
        full,
        split,
        full,
        full,
        split,
        full,
        full,
        full,
        split,
        full,
        split,
        full,
    )
    return jax.shard_map(shards, mesh=mesh, in_specs=in_specs, out_specs=out_specs, check_vma=False)
```

```python
import jax
import jax.numpy as jnp
from jax import lax
from jax.experimental import pallas as pl
from jax.experimental.pallas import tpu as pltpu
from jax.sharding import PartitionSpec as P

HEADS = 12
GROUPS = 32
SIDE = 24
SIDE_SMALL = 14
LANES = 128
MIB = 1024 * 1024
BOTH = ("batch", "section")

f32 = jnp.float32
bf16 = jnp.bfloat16


def dot_nn(left, right):
    return jnp.dot(left, right, preferred_element_type=f32)


def dot_tn(left, right):
    return lax.dot_general(left, right, (((0,), (0,)), ((), ())), preferred_element_type=f32)


def dot_nt(left, right):
    return lax.dot_general(left, right, (((1,), (1,)), ((), ())), preferred_element_type=f32)


def fold(values):
    rows, columns = values.shape
    return jnp.sum(values.reshape(rows // 8, 8, columns), axis=0)


def total(values):
    return jnp.sum(values, axis=0, keepdims=True)


def line(ref):
    return ref[...].reshape(1, -1)


def spread_lanes(mask, columns):
    return jnp.concatenate([mask] * (columns // LANES), axis=1)


def cdf_pdf(values):
    bell = jnp.exp(-0.5 * (values * values))
    t = 1.0 / (1.0 + 0.23164189 * jnp.abs(values))
    tail = (
        ((((0.5307027145 * t - 0.7265760135) * t + 0.7107068705) * t - 0.142248368) * t + 0.127414796)
        * t
        * bell
    )
    return jnp.where(values < 0.0, tail, 1.0 - tail), bell * 0.3989422804014327


def group_total(row, per_group):
    channels = row.shape[1]
    rows = jnp.broadcast_to(row, (8, channels))
    lane = lax.broadcasted_iota(jnp.int32, (8, LANES), 1)
    parts = []
    for k in range(channels // LANES):
        part = rows[:, k * LANES : (k + 1) * LANES]
        step = 1
        while step < per_group:
            up = pltpu.roll(part, LANES - step, 1)
            down = pltpu.roll(part, step, 1)
            part = part + jnp.where((lane & step) == 0, up, down)
            step *= 2
        parts.append(part)
    return jnp.concatenate(parts, axis=1)[0:1]


def cell_grid(cells):
    cell = lax.broadcasted_iota(jnp.int32, (cells, LANES), 0).astype(f32)
    row = jnp.floor((cell + 0.5) * (1.0 / SIDE))
    return row, cell - row * SIDE


def validity_mask(image_class, cells):
    row, column = cell_grid(cells)
    corner = jnp.where((row < SIDE_SMALL) & (column < SIDE_SMALL), 1.0, 0.0)
    return jnp.where(image_class == 1, 1.0, corner)


def valid_count(image_class):
    return jnp.where(image_class == 1, float(SIDE * SIDE), float(SIDE_SMALL * SIDE_SMALL))


def rows_at(index, size):
    return pl.ds(pl.multiple_of(index * size, size), size)


def fill_columns(grid_value, padded, columns, sign):
    cells, channels = grid_value.shape
    _, column = cell_grid(cells)
    has_left = spread_lanes(jnp.where(column > 0.5, 1.0, 0.0), channels)
    has_right = spread_lanes(jnp.where(column < SIDE - 1.5, 1.0, 0.0), channels)
    zeros = jnp.zeros((SIDE, channels), f32)
    shifted = (
        pltpu.roll(grid_value, 1, 0) * has_left,
        grid_value,
        pltpu.roll(grid_value, cells - 1, 0) * has_right,
    )
    for k in range(3):
        padded[k, 0:SIDE, :] = zeros
        padded[k, SIDE + cells : 2 * SIDE + cells, :] = zeros
        padded[k, SIDE : SIDE + cells, :] = shifted[k]
    for row_shift in range(3):
        for column_shift in range(3):
            tap = row_shift * 3 + column_shift
            down = row_shift if sign > 0 else 2 - row_shift
            across = column_shift if sign > 0 else 2 - column_shift
            columns[:, tap * channels : (tap + 1) * channels] = padded[
                across, down * SIDE : down * SIDE + cells, :
            ].astype(bf16)


def standardized(weight):
    rows = weight.shape[0]
    centred = weight - total(weight) * (1.0 / rows)
    spread = total(centred * centred) * (1.0 / rows)
    scale = lax.rsqrt(spread + 1e-05)
    return centred * scale, scale


def standardize_back(weight, grad):
    rows = weight.shape[0]
    normal, scale = standardized(weight)
    grad_mean = total(grad) * (1.0 / rows)
    inner = total(grad * normal) * (1.0 / rows)
    return scale * (grad - grad_mean - normal * inner)


PAIRS = 16
VECTORS = 3


def store_pairs(values, mine_ref, other_ref, core):
    pairs, parts = mine_ref.shape[:2]
    for pair in range(pairs):
        for ref, side in ((mine_ref, core), (other_ref, 1 - core)):
            at = pl.multiple_of((2 * pair + side) * parts * 8, 8)
            ref[pair] = sections_of(values[pl.ds(at, parts * 8), :])


def store_split(ref, start, values):
    high = values.astype(bf16)
    low = (values - high.astype(f32)).astype(bf16)
    shape = (VECTORS, 8, values.shape[-1])
    ref[start : start + VECTORS] = high.astype(f32).reshape(shape).astype(bf16)
    ref[start + VECTORS : start + 2 * VECTORS] = low.astype(f32).reshape(shape).astype(bf16)


def load_split(ref, start):
    high = ref[start : start + VECTORS].astype(f32)
    low = ref[start + VECTORS : start + 2 * VECTORS].astype(f32)
    rows = high + low
    return rows.reshape(VECTORS * 8, rows.shape[-1])


def sections_of(values):
    rows, columns = values.shape
    return values.reshape(rows // 8, 8, columns).astype(bf16)


def stem_forward_kernel(
    class_ref,
    x_ref,
    w_in_ref,
    w_mid_ref,
    w_out_ref,
    gain1_ref,
    bias1_ref,
    gain2_ref,
    bias2_ref,
    gain3_ref,
    bias3_ref,
    embed_ref,
    embed_bias_ref,
    position_ref,
    std_in_ref,
    std_mid_ref,
    std_out_ref,
    first_ref,
    second_ref,
    third_ref,
    stat1_ref,
    stat2_ref,
    stat3_ref,
    stem_ref,
    tokens_ref,
    mask,
    padded,
    columns,
    act_two,
):
    image = pl.program_id(0)
    cells = x_ref.shape[1]
    channels = x_ref.shape[2]
    middle = w_in_ref.shape[1]

    @pl.when(image == 0)
    def _():
        std_in_ref[...] = standardized(w_in_ref[...].astype(f32))[0].astype(bf16)
        std_mid_ref[...] = standardized(w_mid_ref[...].astype(f32))[0].astype(bf16)
        std_out_ref[...] = standardized(w_out_ref[...].astype(f32))[0].astype(bf16)

    image_class = class_ref[image]
    mask[...] = validity_mask(image_class, cells)
    count = valid_count(image_class)
    chunk = cells
    steps = cells // chunk

    def stats(values_ref, stat_ref, sums):
        width = values_ref.shape[2]
        per_group = width // GROUPS
        inverse = 1.0 / (count * per_group)
        centre = group_total(total(sums), per_group) * inverse

        def one(step, carry):
            rows = rows_at(step, chunk)
            centred = (values_ref[0, rows, :] - centre) * spread_lanes(mask[rows, :], width)
            return carry + fold(centred * centred)

        squares = lax.fori_loop(0, steps, one, jnp.zeros((8, width), f32))
        scale = lax.rsqrt(group_total(total(squares), per_group) * inverse + 1e-05)
        stat_ref[0, 0:1, :] = centre
        stat_ref[0, 1:2, :] = scale
        return centre, scale

    def first_step(step, carry):
        rows = rows_at(step, chunk)
        low = (x_ref[0, rows, :] * spread_lanes(mask[rows, :], channels)).astype(bf16)
        values = dot_nn(low, std_in_ref[...])
        first_ref[0, rows, :] = values
        return carry + fold(values)

    sums = lax.fori_loop(0, steps, first_step, jnp.zeros((8, middle), f32))
    centre, scale = stats(first_ref, stat1_ref, sums)
    gain = scale * line(gain1_ref)
    normed = (first_ref[0] - centre) * gain + line(bias1_ref)
    act = normed * cdf_pdf(normed)[0] * spread_lanes(mask[...], middle)
    fill_columns(act, padded, columns, 1)

    def second_step(step, carry):
        rows = rows_at(step, chunk)
        values = dot_nn(columns[rows, :], std_mid_ref[...])
        second_ref[0, rows, :] = values
        return carry + fold(values * spread_lanes(mask[rows, :], middle))

    sums = lax.fori_loop(0, steps, second_step, jnp.zeros((8, middle), f32))
    centre, scale = stats(second_ref, stat2_ref, sums)
    gain = scale * line(gain2_ref)
    normed = (second_ref[0] - centre) * gain + line(bias2_ref)
    act_two[...] = (normed * cdf_pdf(normed)[0] * spread_lanes(mask[...], middle)).astype(bf16)

    def third_step(step, carry):
        rows = rows_at(step, chunk)
        values = dot_nn(act_two[rows, :], std_out_ref[...])
        third_ref[0, rows, :] = values
        return carry + fold(values)

    sums = lax.fori_loop(0, steps, third_step, jnp.zeros((8, channels), f32))
    centre, scale = stats(third_ref, stat3_ref, sums)
    gain = scale * line(gain3_ref)

    @pl.loop(0, steps)
    def _(step):
        rows = rows_at(step, chunk)
        keep = mask[rows, :]
        keep_wide = spread_lanes(keep, channels)
        argument = (
            x_ref[0, rows, :] * keep_wide + (third_ref[0, rows, :] - centre) * gain + line(bias3_ref)
        )
        stem = (argument * cdf_pdf(argument)[0] * keep_wide).astype(bf16)
        stem_ref[0, rows, :] = stem
        values = dot_nn(stem, embed_ref[...]) + line(embed_bias_ref) + position_ref[rows, :].astype(f32)
        tokens_ref[0, rows, :] = (values * spread_lanes(keep, values.shape[1])).astype(bf16)


def cost(flops, moved):
    return pl.CostEstimate(flops=flops, bytes_accessed=moved, transcendentals=0)


def whole(shape):
    return pl.BlockSpec(shape, lambda *_: (0,) * len(shape))


def per_image(shape):
    return pl.BlockSpec((1,) + shape, lambda image, *_: (image,) + (0,) * len(shape))


def stem_forward(image_class, x, w_in, w_mid, w_out, norms, embed, embed_bias, position):
    images, cells, channels = x.shape
    middle = w_in.shape[1]
    width = embed.shape[1]
    row = lambda size: whole((size,))
    return pl.pallas_call(
        stem_forward_kernel,
        out_shape=(
            jax.ShapeDtypeStruct((channels, middle), bf16),
            jax.ShapeDtypeStruct((9 * middle, middle), bf16),
            jax.ShapeDtypeStruct((middle, channels), bf16),
            jax.ShapeDtypeStruct((images, cells, middle), f32),
            jax.ShapeDtypeStruct((images, cells, middle), f32),
            jax.ShapeDtypeStruct((images, cells, channels), f32),
            jax.ShapeDtypeStruct((images, 8, middle), f32),
            jax.ShapeDtypeStruct((images, 8, middle), f32),
            jax.ShapeDtypeStruct((images, 8, channels), f32),
            jax.ShapeDtypeStruct((images, cells, channels), bf16),
            jax.ShapeDtypeStruct((images, cells, width), bf16),
        ),
        grid_spec=pltpu.PrefetchScalarGridSpec(
            num_scalar_prefetch=1,
            grid=(images,),
            in_specs=[
                per_image((cells, channels)),
                whole((channels, middle)),
                whole((9 * middle, middle)),
                whole((middle, channels)),
                row(middle),
                row(middle),
                row(middle),
                row(middle),
                row(channels),
                row(channels),
                whole((channels, width)),
                row(width),
                whole((cells, width)),
            ],
            out_specs=[
                whole((channels, middle)),
                whole((9 * middle, middle)),
                whole((middle, channels)),
                per_image((cells, middle)),
                per_image((cells, middle)),
                per_image((cells, channels)),
                per_image((8, middle)),
                per_image((8, middle)),
                per_image((8, channels)),
                per_image((cells, channels)),
                per_image((cells, width)),
            ],
            scratch_shapes=[
                pltpu.VMEM((cells, LANES), f32),
                pltpu.VMEM((3, cells + 2 * SIDE, middle), f32),
                pltpu.VMEM((cells, 9 * middle), bf16),
                pltpu.VMEM((cells, middle), bf16),
            ],
        ),
        compiler_params=pltpu.CompilerParams(vmem_limit_bytes=62 * MIB),
        cost_estimate=cost(25_000_000_000, 30 * MIB),
        name="stem_forward",
    )(image_class, x, w_in, w_mid, w_out, *norms, embed, embed_bias, position)


def row_norm(values):
    centre = jnp.mean(values, axis=-1, keepdims=True)
    centred = values - centre
    scale = lax.rsqrt(jnp.mean(centred * centred, axis=-1, keepdims=True) + 1e-06)
    return centred * scale, scale


def attend_forward_kernel(
    class_ref,
    tokens_ref,
    gain1_ref,
    bias1_ref,
    joint_ref,
    query_bias_ref,
    value_bias_ref,
    mix_ref,
    mix_bias_ref,
    gain2_ref,
    bias2_ref,
    normed_ref,
    query_ref,
    key_ref,
    value_ref,
    log_total_ref,
    mixed_ref,
    resid_ref,
    normed_two_ref,
):
    image = pl.program_id(0)
    cells, width = tokens_ref.shape[1:]
    chunk = cells
    steps = cells // chunk
    scale = (width // HEADS) ** -0.5

    @pl.loop(0, steps)
    def _(step):
        rows = rows_at(step, chunk)
        normal, _ = row_norm(tokens_ref[0, rows, :].astype(f32))
        normed_ref[0, rows, :] = (normal * line(gain1_ref) + line(bias1_ref)).astype(bf16)

    block = 256
    query_bias = line(query_bias_ref)
    value_bias = line(value_bias_ref)
    for start in range(0, width, block):
        here = slice(start, start + block)
        later = slice(width + start, width + start + block)
        last = slice(2 * width + start, 2 * width + start + block)
        normed = normed_ref[0]
        query = dot_nn(normed, joint_ref[:, here]) + query_bias[:, here]
        query_ref[0, :, here] = query.astype(bf16)
        key_ref[0, :, here] = dot_nn(normed, joint_ref[:, later]).astype(bf16)
        value = dot_nn(normed, joint_ref[:, last]) + value_bias[:, here]
        value_ref[0, :, here] = value.astype(bf16)

    upper = lax.broadcasted_iota(jnp.int32, (cells, LANES), 1) >= LANES // 2
    key_bias = (validity_mask(class_ref[image], cells) - 1.0) * 1000000000.0
    key_bias = key_bias.astype(bf16)
    lane = lax.broadcasted_iota(jnp.int32, (cells, LANES), 1)

    @pl.loop(0, width // LANES, unroll=True)
    def _(pair):
        lanes = rows_at(pair, LANES)
        query = query_ref[0, :, lanes] * bf16(scale)
        key = key_ref[0, :, lanes]
        value = value_ref[0, :, lanes]
        outs = []
        for half in range(2):
            mine = upper if half else jnp.logical_not(upper)
            spare = lane == (0 if half else LANES // 2)
            scores = dot_nt(
                jnp.where(mine, key, jnp.where(spare, key_bias, bf16(0))),
                jnp.where(spare, bf16(1), query),
            )
            top = jnp.max(scores, axis=0, keepdims=True)
            weights = jnp.exp(scores - top)
            weight_sum = total(weights)
            probs = (weights * (1.0 / weight_sum)).astype(bf16)
            outs.append(dot_tn(probs, value))
            log_total_ref[0, 2 * pair + half] = jnp.broadcast_to(top + jnp.log(weight_sum), (8, cells))
        mixed_ref[0, :, lanes] = jnp.where(upper, outs[1], outs[0]).astype(bf16)

    @pl.loop(0, steps)
    def _(step):
        rows = rows_at(step, chunk)
        resid = (
            tokens_ref[0, rows, :].astype(f32)
            + dot_nn(mixed_ref[0, rows, :], mix_ref[...])
            + line(mix_bias_ref)
        )
        resid_ref[0, rows, :] = resid
        normal, _ = row_norm(resid)
        normed_two_ref[0, rows, :] = (normal * line(gain2_ref) + line(bias2_ref)).astype(bf16)


def attend_forward(
    image_class, tokens, gain1, bias1, joint, query_bias, value_bias, mix, mix_bias, gain2, bias2
):
    images, cells, width = tokens.shape
    row = whole((width,))
    low = jax.ShapeDtypeStruct((images, cells, width), bf16)
    low_spec = per_image((cells, width))
    return pl.pallas_call(
        attend_forward_kernel,
        out_shape=(
            low,
            low,
            low,
            low,
            jax.ShapeDtypeStruct((images, HEADS, 8, cells), f32),
            low,
            jax.ShapeDtypeStruct((images, cells, width), f32),
            low,
        ),
        grid_spec=pltpu.PrefetchScalarGridSpec(
            num_scalar_prefetch=1,
            grid=(images,),
            in_specs=[
                low_spec,
                row,
                row,
                whole((width, 3 * width)),
                row,
                row,
                whole((width, width)),
                row,
                row,
                row,
            ],
            out_specs=[
                low_spec,
                low_spec,
                low_spec,
                low_spec,
                per_image((HEADS, 8, cells)),
                low_spec,
                low_spec,
                low_spec,
            ],
        ),
        compiler_params=pltpu.CompilerParams(vmem_limit_bytes=62 * MIB),
        cost_estimate=cost(35_000_000_000, 30 * MIB),
        name="attend_forward",
    )(image_class, tokens, gain1, bias1, joint, query_bias, value_bias, mix, mix_bias, gain2, bias2)


def feed_kernel(
    class_ref,
    mine_ref,
    core_ref,
    normed_ref,
    cotangent0_ref,
    cotangent1_ref,
    expand_ref,
    expand_bias_ref,
    shrink_ref,
    shrink_bias_ref,
    gain2_ref,
    resid_ref,
    mix_ref,
    output_ref,
    grad_resid_ref,
    grad_mixed_ref,
    shrink_mine_ref,
    shrink_other_ref,
    expand_mine_ref,
    expand_other_ref,
    grad_expand_bias_ref,
    grad_shrink_bias_ref,
    sums_ref,
    sent,
    result,
    grad_normed,
    hidden,
    grad_pre,
    normed_turned,
    shrink_total,
    expand_total,
    biases,
    resid,
    mix,
    empty,
    in_sems,
    out_sems,
    empty_sems,
):
    step = pl.program_id(0)
    last = pl.num_programs(0) - 1
    images, cells, width = normed_ref.shape
    slots = output_ref.shape[0]
    block = expand_ref.shape[1]
    part = cells // 2
    loads = [
        pltpu.make_async_copy(resid_ref, resid, in_sems.at[0]),
        pltpu.make_async_copy(mix_ref, mix, in_sems.at[1]),
    ]

    def image_rows(image):
        return slice(image * cells, (image + 1) * cells)

    def each_empty(act):
        for slot in range(slots):
            taken = mine_ref[0] == slot
            for image in range(1, images):
                taken = taken | (mine_ref[image] == slot)

            @pl.when(jnp.logical_not(taken))
            def _():
                act(pltpu.make_async_copy(empty, output_ref.at[slot], empty_sems.at[slot]))

    @pl.when(step == 0)
    def _():
        empty[...] = jnp.zeros_like(empty)
        each_empty(lambda copy: copy.start())
        for copy in loads:
            copy.start()
        sums = jnp.zeros((8, width), f32)
        for image, ref in enumerate((cotangent0_ref, cotangent1_ref)):
            keep = spread_lanes(validity_mask(class_ref[image], cells), width)
            grad = ref[0].astype(f32) * keep
            sent[image_rows(image), :] = grad.astype(bf16)
            sums = sums + fold(grad)
            normed_turned[:, image_rows(image)] = normed_ref[image].T
        grad_shrink_bias_ref[...] = sums
        result[...] = jnp.zeros_like(result)
        grad_normed[...] = jnp.zeros_like(grad_normed)
        every = line(expand_bias_ref)
        for k in range(biases.shape[0]):
            biases[k : k + 1, :] = every[:, k * block : (k + 1) * block]

    bias_sums = jnp.zeros((8, block), f32)
    for image in range(images):
        for piece in range(cells // part):
            local = slice(piece * part, (piece + 1) * part)
            rows = slice(image * cells + piece * part, image * cells + (piece + 1) * part)
            pre = dot_nn(normed_ref[image, local, :], expand_ref[...]) + biases[pl.ds(step, 1), :]
            back = dot_nt(sent[rows, :], shrink_ref[...])
            cdf, pdf = cdf_pdf(pre)
            low = (pre * cdf).astype(bf16)
            hidden[rows, :] = low
            grad = back * (cdf + pre * pdf)
            bias_sums = bias_sums + fold(grad)
            grad_low = grad.astype(bf16)
            grad_pre[rows, :] = grad_low
            result[rows, :] += dot_nn(low, shrink_ref[...])
            grad_normed[rows, :] += dot_nt(grad_low, expand_ref[...])
    grad_expand_bias_ref[...] = bias_sums
    shrink_total[...] = dot_tn(hidden[...], sent[...])
    expand_total[...] = dot_nn(normed_turned[...], grad_pre[...])
    core = core_ref[0]
    store_pairs(shrink_total, shrink_mine_ref, shrink_other_ref, core)
    store_pairs(expand_total, expand_mine_ref, expand_other_ref, core)

    @pl.when(step == last)
    def _():
        for copy in loads:
            copy.wait()
        stores = []
        for image in range(images):
            rows = image_rows(image)
            keep = spread_lanes(validity_mask(class_ref[image], cells), width)
            out = (resid[image] + result[rows, :] + line(shrink_bias_ref)) * keep
            hidden[rows, :] = out.astype(bf16)
            stores.append(
                pltpu.make_async_copy(
                    hidden.at[pl.ds(image * cells, cells)],
                    output_ref.at[mine_ref[image]],
                    out_sems.at[3 * image],
                )
            )
            stores[-1].start()
        sums = [jnp.zeros((8, width), f32)] * 3
        for image in range(images):
            rows = image_rows(image)
            normal, row_scale = row_norm(resid[image])
            grad = grad_normed[rows, :]
            sums[0] = sums[0] + fold(grad * normal)
            sums[1] = sums[1] + fold(grad)
            grad = sent[rows, :].astype(f32) + row_norm_back(grad, normal, row_scale, line(gain2_ref))
            sums[2] = sums[2] + fold(grad)
            resid[image] = grad
            stores.append(
                pltpu.make_async_copy(resid.at[image], grad_resid_ref.at[image], out_sems.at[3 * image + 1])
            )
            stores[-1].start()
            grad_pre[rows, :] = dot_nt(grad.astype(bf16), mix[...]).astype(bf16)
            stores.append(
                pltpu.make_async_copy(
                    grad_pre.at[pl.ds(image * cells, cells)],
                    grad_mixed_ref.at[image],
                    out_sems.at[3 * image + 2],
                )
            )
            stores[-1].start()
        for k in range(3):
            sums_ref[k] = sums[k]
        each_empty(lambda copy: copy.wait())
        for copy in stores:
            copy.wait()


def feed(
    image_class, mine, core, normed, resid, cotangent, expand, expand_bias, shrink, shrink_bias, gain2, mix
):
    images, cells, width = normed.shape
    inner = expand.shape[1]
    slots = cotangent.shape[0]
    block = width
    rows = images * cells
    shrink_size = inner // (2 * PAIRS)
    pairs = block // (2 * shrink_size)
    expand_size = width // (2 * PAIRS)
    shrink_half = jax.ShapeDtypeStruct((PAIRS, shrink_size // 8, 8, width), bf16)
    expand_half = jax.ShapeDtypeStruct((PAIRS, expand_size // 8 * (inner // width), 8, width), bf16)
    shrink_spec = pl.BlockSpec((pairs, shrink_size // 8, 8, width), lambda step, *_: (step, 0, 0, 0))
    expand_spec = pl.BlockSpec((PAIRS, expand_size // 8, 8, block), lambda step, *_: (0, step, 0, 0))
    anywhere = pl.BlockSpec(memory_space=pl.ANY)
    return pl.pallas_call(
        feed_kernel,
        out_shape=(
            jax.ShapeDtypeStruct((slots, cells, width), bf16),
            jax.ShapeDtypeStruct((images, cells, width), f32),
            jax.ShapeDtypeStruct((images, cells, width), bf16),
            shrink_half,
            shrink_half,
            expand_half,
            expand_half,
            jax.ShapeDtypeStruct((8, inner), f32),
            jax.ShapeDtypeStruct((8, width), f32),
            jax.ShapeDtypeStruct((3, 8, width), f32),
        ),
        grid_spec=pltpu.PrefetchScalarGridSpec(
            num_scalar_prefetch=3,
            grid=(inner // block,),
            in_specs=[
                whole((images, cells, width)),
                pl.BlockSpec((1, cells, width), lambda step, classes, mine, core: (mine[0], 0, 0)),
                pl.BlockSpec((1, cells, width), lambda step, classes, mine, core: (mine[1], 0, 0)),
                pl.BlockSpec((width, block), lambda step, *_: (0, step)),
                whole((inner,)),
                pl.BlockSpec((block, width), lambda step, *_: (step, 0)),
                whole((width,)),
                whole((width,)),
                anywhere,
                anywhere,
            ],
            out_specs=[
                anywhere,
                anywhere,
                anywhere,
                shrink_spec,
                shrink_spec,
                expand_spec,
                expand_spec,
                pl.BlockSpec((8, block), lambda step, *_: (0, step)),
                whole((8, width)),
                whole((3, 8, width)),
            ],
            scratch_shapes=[
                pltpu.VMEM((rows, width), bf16),
                pltpu.VMEM((rows, width), f32),
                pltpu.VMEM((rows, width), f32),
                pltpu.VMEM((rows, block), bf16),
                pltpu.VMEM((rows, block), bf16),
                pltpu.VMEM((width, rows), bf16),
                pltpu.VMEM((block, width), f32),
                pltpu.VMEM((width, block), f32),
                pltpu.VMEM((inner // block, block), f32),
                pltpu.VMEM((images, cells, width), f32),
                pltpu.VMEM((width, width), bf16),
                pltpu.VMEM((cells, width), bf16),
                pltpu.SemaphoreType.DMA((2,)),
                pltpu.SemaphoreType.DMA((3 * images,)),
                pltpu.SemaphoreType.DMA((slots,)),
            ],
        ),
        compiler_params=pltpu.CompilerParams(vmem_limit_bytes=62 * MIB),
        cost_estimate=cost(14 * rows * width * inner, 40 * MIB),
        name="feed",
    )(
        image_class,
        mine,
        core,
        normed,
        cotangent,
        cotangent,
        expand,
        expand_bias,
        shrink,
        shrink_bias,
        gain2,
        resid,
        mix,
    )


def row_norm_back(grad, normal, scale, gain):
    inner = grad * gain
    mean = jnp.mean(inner, axis=-1, keepdims=True)
    cross = jnp.mean(inner * normal, axis=-1, keepdims=True)
    return scale * (inner - mean - normal * cross)


def attend_backward_kernel(
    class_ref,
    query_ref,
    key_ref,
    value_ref,
    log_total_ref,
    grad_mixed_ref,
    grad_joint_ref,
    sums_ref,
    *,
    image,
):
    cells, width = query_ref.shape[1:]
    scale = (width // HEADS) ** -0.5

    upper = lax.broadcasted_iota(jnp.int32, (cells, LANES), 1) >= LANES // 2
    key_bias = (validity_mask(class_ref[image], cells) - 1.0) * 1000000000.0
    key_bias = key_bias.astype(bf16)
    lane = lax.broadcasted_iota(jnp.int32, (cells, LANES), 1)

    @pl.loop(0, width // LANES, unroll=True)
    def _(pair):
        lanes = rows_at(pair, LANES)
        query = query_ref[0, :, lanes] * bf16(scale)
        key = key_ref[0, :, lanes]
        value = value_ref[0, :, lanes]
        grad_out = grad_mixed_ref[0, :, lanes]
        grads = []
        for half in range(2):
            mine = upper if half else jnp.logical_not(upper)
            spare = lane == (0 if half else LANES // 2)
            scores = dot_nt(
                jnp.where(mine, key, jnp.where(spare, key_bias, bf16(0))),
                jnp.where(spare, bf16(1), query),
            )
            log_total = log_total_ref[0, 2 * pair + half, 0:1, :]
            probs = jnp.exp(scores - log_total)
            grad_probs = dot_nt(jnp.where(mine, value, bf16(0)), grad_out)
            weighted = probs * grad_probs
            grad_scores = (weighted - probs * total(weighted)).astype(bf16)
            grad_value = dot_nn(probs.astype(bf16), grad_out)
            grad_key = dot_nn(grad_scores, query)
            grad_query = dot_tn(grad_scores, key) * scale
            grads.append((grad_query, grad_key, grad_value))
        for k in range(3):
            grad = jnp.where(upper, grads[1][k], grads[0][k])
            if k != 1:
                sums_ref[k // 2, :, lanes] = fold(grad)
            where = pl.ds(pl.multiple_of(k * width + pair * LANES, LANES), LANES)
            grad_joint_ref[0, :, where] = grad.astype(bf16)


def attend_backward(image, image_class, query, key, value, log_total, grad_mixed):
    images, cells, width = query.shape
    own = lambda shape: pl.BlockSpec((1,) + shape, lambda *_: (image,) + (0,) * len(shape))
    rows = own((cells, width))
    return pl.pallas_call(
        lambda *refs: attend_backward_kernel(*refs, image=image),
        out_shape=(
            jax.ShapeDtypeStruct((1, cells, 3 * width), bf16),
            jax.ShapeDtypeStruct((2, 8, width), f32),
        ),
        grid_spec=pltpu.PrefetchScalarGridSpec(
            num_scalar_prefetch=1,
            grid=(1,),
            in_specs=[rows, rows, rows, own((HEADS, 8, cells)), rows],
            out_specs=[whole((1, cells, 3 * width)), whole((2, 8, width))],
        ),
        compiler_params=pltpu.CompilerParams(vmem_limit_bytes=62 * MIB),
        cost_estimate=cost(40 * cells * cells * width, 6 * MIB),
        name="attend_backward",
    )(image_class, query, key, value, log_total, grad_mixed)


def joint_backward_kernel(
    core_ref,
    normed_ref,
    grad_joint0_ref,
    grad_joint1_ref,
    joint_ref,
    gain1_ref,
    tokens_ref,
    mixed_ref,
    grad_resid_ref,
    feed_expand_ref,
    feed_shrink_ref,
    mix_sums_ref,
    attend_sums0_ref,
    attend_sums1_ref,
    grad_tokens_ref,
    mine_ref,
    other_ref,
    sums_ref,
    vectors_ref,
    grad_joint,
    weight_total,
    grad_normed,
    tokens,
    mixed,
    grad_resid,
    sems,
):
    step = pl.program_id(0)
    last = pl.num_programs(0) - 1
    images, cells, width = normed_ref.shape
    rows = images * cells
    loads = [
        pltpu.make_async_copy(mixed_ref, mixed, sems.at[0]),
        pltpu.make_async_copy(grad_resid_ref, grad_resid, sems.at[1]),
        pltpu.make_async_copy(tokens_ref, tokens, sems.at[2]),
    ]

    @pl.when(step == 0)
    def _():
        for copy in loads:
            copy.start()
        grad_normed[...] = jnp.zeros_like(grad_normed)
        vectors_ref[...] = jnp.zeros_like(vectors_ref)
        for k in range(feed_expand_ref.shape[1] // width):
            vectors_ref[k : k + 1, :] = total(feed_expand_ref[:, k * width : (k + 1) * width])
        vectors_ref[4:5, :] = total(feed_shrink_ref[...])
        for k in range(3):
            vectors_ref[5 + k : 6 + k, :] = total(mix_sums_ref[k])
        for k in range(2):
            vectors_ref[8 + k : 9 + k, :] = total(attend_sums0_ref[k] + attend_sums1_ref[k])

    @pl.when(step < last)
    def _():
        grad_joint[0:cells, :] = grad_joint0_ref[0]
        grad_joint[cells:rows, :] = grad_joint1_ref[0]
        weight_total[...] = dot_tn(normed_ref[...].reshape(rows, width), grad_joint[...])
        grad_normed[...] += dot_nt(grad_joint[...], joint_ref[...])

    @pl.when(step == last)
    def _():
        for copy in loads:
            copy.wait()
        low = grad_resid[...].reshape(rows, width).astype(bf16)
        weight_total[...] = dot_tn(mixed[...].reshape(rows, width), low)
        sums = [jnp.zeros((8, width), f32)] * 2
        for image in range(images):
            at = slice(image * cells, (image + 1) * cells)
            normal, row_scale = row_norm(tokens[image].astype(f32))
            grad = grad_normed[at, :]
            sums[0] = sums[0] + fold(grad * normal)
            sums[1] = sums[1] + fold(grad)
            back = row_norm_back(grad, normal, row_scale, line(gain1_ref))
            grad_tokens_ref[image] = (grad_resid[image] + back).astype(bf16)
        sums_ref[0] = sums[0]
        sums_ref[1] = sums[1]

    store_pairs(weight_total, mine_ref, other_ref, core_ref[0])


def joint_backward(
    core,
    tokens,
    normed,
    mixed,
    grad_resid,
    grad_joint0,
    grad_joint1,
    gain1,
    joint,
    sums_expand,
    sums_shrink,
    sums_mix,
    sums_attend0,
    sums_attend1,
):
    images, cells, width = tokens.shape
    size = width // (2 * PAIRS)
    half = (PAIRS, 4 * size // 8, 8, width)
    half_spec = pl.BlockSpec((PAIRS, size // 8, 8, width), lambda step, *_: (0, step, 0, 0))
    column = lambda step, *_: (0, 0, jnp.minimum(step, 2))
    anywhere = pl.BlockSpec(memory_space=pl.ANY)
    return pl.pallas_call(
        joint_backward_kernel,
        out_shape=(
            jax.ShapeDtypeStruct((images, cells, width), bf16),
            jax.ShapeDtypeStruct(half, bf16),
            jax.ShapeDtypeStruct(half, bf16),
            jax.ShapeDtypeStruct((2, 8, width), f32),
            jax.ShapeDtypeStruct((16, width), f32),
        ),
        grid_spec=pltpu.PrefetchScalarGridSpec(
            num_scalar_prefetch=1,
            grid=(4,),
            in_specs=[
                whole((images, cells, width)),
                pl.BlockSpec((1, cells, width), column),
                pl.BlockSpec((1, cells, width), column),
                pl.BlockSpec((width, width), lambda step, *_: (0, jnp.minimum(step, 2))),
                whole((width,)),
                anywhere,
                anywhere,
                anywhere,
                whole(sums_expand.shape),
                whole(sums_shrink.shape),
                whole(sums_mix.shape),
                whole(sums_attend0.shape),
                whole(sums_attend1.shape),
            ],
            out_specs=[
                whole((images, cells, width)),
                half_spec,
                half_spec,
                whole((2, 8, width)),
                whole((16, width)),
            ],
            scratch_shapes=[
                pltpu.VMEM((images * cells, width), bf16),
                pltpu.VMEM((width, width), f32),
                pltpu.VMEM((images * cells, width), f32),
                pltpu.VMEM((images, cells, width), bf16),
                pltpu.VMEM((images, cells, width), bf16),
                pltpu.VMEM((images, cells, width), f32),
                pltpu.SemaphoreType.DMA((3,)),
            ],
        ),
        compiler_params=pltpu.CompilerParams(vmem_limit_bytes=62 * MIB),
        cost_estimate=cost(14 * images * cells * width * width, 25 * MIB),
        name="joint_backward",
    )(
        core,
        normed,
        grad_joint0,
        grad_joint1,
        joint,
        gain1,
        tokens,
        mixed,
        grad_resid,
        sums_expand,
        sums_shrink,
        sums_mix,
        sums_attend0,
        sums_attend1,
    )


def norm_means(sums, gain, per_group, count):
    inverse = 1.0 / (count * per_group)
    return [group_total(total(item) * gain, per_group) * inverse for item in sums]


def embed_weights_kernel(
    class_ref,
    core_ref,
    grad_tokens_ref,
    stem_ref,
    mine_ref,
    other_ref,
    sums_ref,
    grad_masked,
    weight_total,
    position_total,
):
    images, cells, width = grad_tokens_ref.shape
    channels = stem_ref.shape[2]
    sums = jnp.zeros((8, width), f32)
    position = jnp.zeros((cells, width), f32)
    for image in range(images):
        keep = spread_lanes(validity_mask(class_ref[image], cells), width)
        grad = grad_tokens_ref[image].astype(f32) * keep
        grad_masked[image * cells : (image + 1) * cells, :] = grad.astype(bf16)
        sums = sums + fold(grad)
        position = position + grad
    sums_ref[...] = sums
    grad_position = weight_total.at[pl.ds(0, cells)]
    grad_position[...] = position
    position_rows = cells // (2 * PAIRS)
    position_total[...] = jnp.zeros_like(position_total)
    for block in range(2 * PAIRS):
        position_total[block, 0:position_rows, :] = grad_position[
            block * position_rows : (block + 1) * position_rows, :
        ]
    weight_total[...] = dot_tn(stem_ref[...].reshape(images * cells, channels), grad_masked[...])
    core = core_ref[0]
    size = channels // (2 * PAIRS)
    for pair in range(PAIRS):
        for ref, side in ((mine_ref, core), (other_ref, 1 - core)):
            block = 2 * pair + side
            at = pl.ds(pl.multiple_of(block * size, 8), size)
            ref[pair, 0 : size // 8] = sections_of(weight_total[at, :])
            ref[pair, size // 8 :] = sections_of(position_total[block])


def embed_weights(image_class, core, grad_tokens, stem):
    images, cells, width = grad_tokens.shape
    channels = stem.shape[2]
    position_rows = -(-cells // (2 * PAIRS) // 8) * 8
    half = (PAIRS, (channels // (2 * PAIRS) + position_rows) // 8, 8, width)
    return pl.pallas_call(
        embed_weights_kernel,
        out_shape=(
            jax.ShapeDtypeStruct(half, bf16),
            jax.ShapeDtypeStruct(half, bf16),
            jax.ShapeDtypeStruct((8, width), f32),
        ),
        grid_spec=pltpu.PrefetchScalarGridSpec(
            num_scalar_prefetch=2,
            grid=(1,),
            in_specs=[whole(grad_tokens.shape), whole(stem.shape)],
            out_specs=[whole(half), whole(half), whole((8, width))],
            scratch_shapes=[
                pltpu.VMEM((images * cells, width), bf16),
                pltpu.VMEM((channels, width), f32),
                pltpu.VMEM((2 * PAIRS, position_rows, width), f32),
            ],
        ),
        compiler_params=pltpu.CompilerParams(vmem_limit_bytes=62 * MIB),
        cost_estimate=cost(8_000_000_000, 8 * MIB),
        name="embed_weights",
    )(image_class, core, grad_tokens, stem)


def embed_backward_kernel(
    class_ref,
    grad_tokens_ref,
    x_ref,
    third_ref,
    stat3_ref,
    gain3_ref,
    bias3_ref,
    embed_ref,
    grad_inner_ref,
    grad_third_ref,
    sums3_ref,
    mask,
):
    image = pl.program_id(0)
    cells, channels = x_ref.shape[1:]
    chunk = cells
    steps = cells // chunk
    image_class = class_ref[image]
    mask[...] = validity_mask(image_class, cells)
    count = valid_count(image_class)

    @pl.when(image == 0)
    def _():
        sums3_ref[...] = jnp.zeros_like(sums3_ref)

    centre, scale = stat3_ref[0, 0:1, :], stat3_ref[0, 1:2, :]
    gain = line(gain3_ref)

    def third_step(step, carry):
        rows = rows_at(step, chunk)
        keep = spread_lanes(mask[rows, :], channels)
        grad = dot_nt(grad_tokens_ref[0, rows, :], embed_ref[...]) * keep
        normal = (third_ref[0, rows, :] - centre) * scale
        argument = x_ref[0, rows, :] * keep + normal * gain + line(bias3_ref)
        cdf, pdf = cdf_pdf(argument)
        grad = grad * (cdf + argument * pdf)
        grad_inner_ref[0, rows, :] = grad
        return carry[0] + fold(grad * normal), carry[1] + fold(grad)

    zeros = jnp.zeros((8, channels), f32)
    with_normal, plain = lax.fori_loop(0, steps, third_step, (zeros, zeros))
    sums3_ref[0] += with_normal
    sums3_ref[1] += plain
    mean, cross = norm_means((plain, with_normal), gain, channels // GROUPS, count)
    outer = scale * gain
    mean = mean * scale
    cross = cross * scale

    @pl.loop(0, steps)
    def _(step):
        rows = rows_at(step, chunk)
        keep = spread_lanes(mask[rows, :], channels)
        normal = (third_ref[0, rows, :] - centre) * scale
        grad = (grad_inner_ref[0, rows, :] * outer - mean - normal * cross) * keep
        grad_third_ref[0, rows, :] = grad.astype(bf16)


def embed_backward(image_class, grad_tokens, x, third, stat3, gain3, bias3, embed):
    images, cells, channels = x.shape
    width = embed.shape[1]
    return pl.pallas_call(
        embed_backward_kernel,
        out_shape=(
            jax.ShapeDtypeStruct((images, cells, channels), f32),
            jax.ShapeDtypeStruct((images, cells, channels), bf16),
            jax.ShapeDtypeStruct((2, 8, channels), f32),
        ),
        grid_spec=pltpu.PrefetchScalarGridSpec(
            num_scalar_prefetch=1,
            grid=(images,),
            in_specs=[
                per_image((cells, width)),
                per_image((cells, channels)),
                per_image((cells, channels)),
                per_image((8, channels)),
                whole((channels,)),
                whole((channels,)),
                whole((channels, width)),
            ],
            out_specs=[
                per_image((cells, channels)),
                per_image((cells, channels)),
                whole((2, 8, channels)),
            ],
            scratch_shapes=[
                pltpu.VMEM((cells, LANES), f32),
            ],
        ),
        compiler_params=pltpu.CompilerParams(vmem_limit_bytes=62 * MIB),
        cost_estimate=cost(20_000_000_000, 30 * MIB),
        name="embed_backward",
    )(image_class, grad_tokens, x, third, stat3, gain3, bias3, embed)


def convs_backward_kernel(
    class_ref,
    core_ref,
    grad_third_ref,
    x_ref,
    first_ref,
    second_ref,
    stat1_ref,
    stat2_ref,
    std_in_ref,
    std_mid_ref,
    std_out_ref,
    w_in_ref,
    w_mid_ref,
    w_out_ref,
    gain1_ref,
    bias1_ref,
    gain2_ref,
    bias2_ref,
    sums_embed_ref,
    sums3_ref,
    sums_attn_ref,
    arrived_ref,
    grad_first_ref,
    mine_ref,
    other_ref,
    output_ref,
    vectors,
    sums1,
    sums2,
    mask,
    act,
    padded,
    columns,
    in_total,
    mid_total,
    out_total,
    mid_done,
    in_done,
):
    image = pl.program_id(0)
    last = pl.num_programs(0) - 1
    output_ref[...] = arrived_ref[...]
    cells, channels = x_ref.shape[1:]
    width = sums_embed_ref.shape[1]
    middle = first_ref.shape[2]
    image_class = class_ref[image]
    mask[...] = validity_mask(image_class, cells)
    count = valid_count(image_class)

    @pl.when(image == 0)
    def _():
        for ref in (sums1, sums2, in_total, mid_total, out_total):
            ref[...] = jnp.zeros_like(ref)

    def middle_norm(values_ref, stat_ref, gain_ref, bias_ref, sums_ref, grad_of):
        centre, scale = stat_ref[0, 0:1, :], stat_ref[0, 1:2, :]
        gain = line(gain_ref)
        keep = spread_lanes(mask[...], middle)
        normal = (values_ref[0] - centre) * scale
        argument = normal * gain + line(bias_ref)
        cdf, pdf = cdf_pdf(argument)
        act[...] = (argument * cdf * keep).astype(bf16)
        grad = grad_of() * keep * (cdf + argument * pdf)
        plain, with_normal = fold(grad), fold(grad * normal)
        sums_ref[0] += with_normal
        sums_ref[1] += plain
        mean, cross = norm_means((plain, with_normal), gain, middle // GROUPS, count)
        return (grad * (scale * gain) - mean * scale - normal * (cross * scale)) * keep

    grad_second = middle_norm(
        second_ref,
        stat2_ref,
        gain2_ref,
        bias2_ref,
        sums2,
        lambda: dot_nt(grad_third_ref[0], std_out_ref[...]),
    )
    out_total[...] += dot_tn(act[...], grad_third_ref[0])
    fill_columns(grad_second, padded, columns, -1)

    def spread_back():
        grad = jnp.zeros((cells, middle), f32)
        for tap in range(9):
            part = slice(tap * middle, (tap + 1) * middle)
            grad = grad + dot_nt(columns[:, part], std_mid_ref[part, :])
        return grad

    grad = middle_norm(first_ref, stat1_ref, gain1_ref, bias1_ref, sums1, spread_back)
    grad_low = grad.astype(bf16)
    grad_first_ref[0] = grad_low
    mid_total[...] += dot_tn(act[...], columns[...])
    low = (x_ref[0] * spread_lanes(mask[...], channels)).astype(bf16)
    in_total[...] += dot_tn(grad_low, low)

    @pl.when(image == last)
    def _():
        core = core_ref[0]
        out_total[...] = standardize_back(w_out_ref[...].astype(f32), out_total[...])
        in_done[...] = standardize_back(w_in_ref[...].astype(f32), in_total[...].T)
        rows = 9 * middle
        normal, scale = standardized(w_mid_ref[...].astype(f32))
        grads = [mid_total[:, tap * middle : (tap + 1) * middle] for tap in range(9)]
        grad_mean = sum(total(g) for g in grads) * (1.0 / rows)
        inner = sum(
            total(g * normal[tap * middle : (tap + 1) * middle]) for tap, g in enumerate(grads)
        ) * (1.0 / rows)
        for tap, g in enumerate(grads):
            part = slice(tap * middle, (tap + 1) * middle)
            mid_done[part, :] = scale * (g - grad_mean - normal[part] * inner)
        in_size = channels // (2 * PAIRS)
        mid_size = rows // (2 * PAIRS)
        out_size = middle // (2 * PAIRS)
        in_parts = in_size // 8
        mid_parts = mid_size // 8
        for pair in range(PAIRS):
            for ref, side in ((mine_ref, core), (other_ref, 1 - core)):
                block = 2 * pair + side
                at = pl.ds(pl.multiple_of(block * in_size, 8), in_size)
                ref[pair, 0:in_parts] = sections_of(in_done[at, :])
                at = pl.ds(pl.multiple_of(block * mid_size, 8), mid_size)
                ref[pair, in_parts : in_parts + mid_parts] = sections_of(mid_done[at, :])
                at = pl.ds(pl.multiple_of(block * out_size, 8), out_size)
                for k in range(channels // middle):
                    ref[pair, in_parts + mid_parts + k] = out_total[
                        at, k * middle : (k + 1) * middle
                    ].astype(bf16)
        vectors[...] = jnp.zeros_like(vectors)
        row = 0
        for item in (
            total(sums_embed_ref[...]),
            total(sums_attn_ref[0]),
            total(sums_attn_ref[1]),
            total(sums1[0]),
            total(sums1[1]),
            total(sums2[0]),
            total(sums2[1]),
            total(sums3_ref[0]),
            total(sums3_ref[1]),
        ):
            for start in range(0, item.shape[1], middle):
                vectors[row : row + 1, :] = item[:, start : start + middle]
                row += 1
        mine_ref[PAIRS] = jnp.zeros(mine_ref.shape[1:], bf16)
        store_split(mine_ref.at[PAIRS], 0, vectors[...])
        other_ref[PAIRS] = mine_ref[PAIRS]


def convs_backward(
    image_class,
    core,
    grad_third,
    x,
    first,
    second,
    stat1,
    stat2,
    stds,
    weights,
    norms,
    sums_embed,
    sums3,
    sums_attn,
    arrived,
):
    images, cells, channels = x.shape
    middle = first.shape[2]
    width = sums_embed.shape[1]
    row = lambda size: whole((size,))
    conv_rows = channels // (2 * PAIRS) + 9 * middle // (2 * PAIRS) + middle // (2 * PAIRS) * (channels // middle)
    half = (PAIRS + 1, conv_rows // 8, 8, middle)
    slot_spec = pl.BlockSpec(
        (arrived.shape[0] // images,) + arrived.shape[1:], lambda image, *_: (image, 0, 0)
    )
    return pl.pallas_call(
        convs_backward_kernel,
        out_shape=(
            jax.ShapeDtypeStruct((images, cells, middle), bf16),
            jax.ShapeDtypeStruct(half, bf16),
            jax.ShapeDtypeStruct(half, bf16),
            jax.ShapeDtypeStruct(arrived.shape, bf16),
        ),
        grid_spec=pltpu.PrefetchScalarGridSpec(
            num_scalar_prefetch=2,
            grid=(images,),
            in_specs=[
                per_image((cells, channels)),
                per_image((cells, channels)),
                per_image((cells, middle)),
                per_image((cells, middle)),
                per_image((8, middle)),
                per_image((8, middle)),
                whole((channels, middle)),
                whole((9 * middle, middle)),
                whole((middle, channels)),
                whole((channels, middle)),
                whole((9 * middle, middle)),
                whole((middle, channels)),
                row(middle),
                row(middle),
                row(middle),
                row(middle),
                whole((8, width)),
                whole((2, 8, channels)),
                whole((2, 8, width)),
                slot_spec,
            ],
            out_specs=[
                per_image((cells, middle)),
                whole(half),
                whole(half),
                slot_spec,
            ],
            scratch_shapes=[
                pltpu.VMEM((VECTORS * 8, middle), f32),
                pltpu.VMEM((2, 8, middle), f32),
                pltpu.VMEM((2, 8, middle), f32),
                pltpu.VMEM((cells, LANES), f32),
                pltpu.VMEM((cells, middle), bf16),
                pltpu.VMEM((3, cells + 2 * SIDE, middle), f32),
                pltpu.VMEM((cells, 9 * middle), bf16),
                pltpu.VMEM((middle, channels), f32),
                pltpu.VMEM((middle, 9 * middle), f32),
                pltpu.VMEM((middle, channels), f32),
                pltpu.VMEM((9 * middle, middle), f32),
                pltpu.VMEM((channels, middle), f32),
            ],
        ),
        compiler_params=pltpu.CompilerParams(vmem_limit_bytes=62 * MIB),
        cost_estimate=cost(20_000_000_000, 20 * MIB),
        name="convs_backward",
    )(
        image_class,
        core,
        grad_third,
        x,
        first,
        second,
        stat1,
        stat2,
        *stds,
        *weights,
        *norms[:4],
        sums_embed,
        sums3,
        sums_attn,
        arrived,
    )


def input_backward_kernel(class_ref, grad_inner_ref, grad_first_ref, std_in_ref, input_grad_ref):
    cells, channels = grad_inner_ref.shape[1:]
    keep = spread_lanes(validity_mask(class_ref[pl.program_id(0)], cells), channels)
    back = dot_nt(grad_first_ref[0], std_in_ref[...])
    input_grad_ref[0] = (grad_inner_ref[0] + back) * keep


def input_backward(image_class, grad_inner, grad_first, std_in):
    images, cells, channels = grad_inner.shape
    middle = grad_first.shape[2]
    return pl.pallas_call(
        input_backward_kernel,
        out_shape=jax.ShapeDtypeStruct((images, cells, channels), f32),
        grid_spec=pltpu.PrefetchScalarGridSpec(
            num_scalar_prefetch=1,
            grid=(images,),
            in_specs=[
                per_image((cells, channels)),
                per_image((cells, middle)),
                whole((channels, middle)),
            ],
            out_specs=per_image((cells, channels)),
        ),
        compiler_params=pltpu.CompilerParams(vmem_limit_bytes=62 * MIB),
        cost_estimate=cost(2 * images * cells * channels * middle, 12 * MIB),
        name="input_backward",
    )(image_class, grad_inner, grad_first, std_in)


def combine_core_kernel(plane_ref, *refs, arrays, extra):
    mines, others, outs = refs[:arrays], refs[arrays : 2 * arrays], refs[2 * arrays :]
    start = 0
    for mine, other in zip(mines, others):
        size = mine.shape[1]
        for z in range(mine.shape[0] // 4):
            for q in range(4):
                at = 4 * z + lax.bitwise_xor(plane_ref[0], q)
                summed = mine[at].astype(f32) + other[at].astype(f32)
                outs[q][z, start : start + size] = summed.astype(bf16)
        start += size
    if extra:
        vectors = load_split(mines[0].at[PAIRS], 0) + load_split(others[0].at[PAIRS], 0)
        for out in outs:
            out[PAIRS // 4] = jnp.zeros(out.shape[1:], bf16)
            store_split(out.at[PAIRS // 4], 0, vectors)


def combine_core(plane, mines, others, extra):
    arrays = len(mines)
    depth = PAIRS // 4
    steps = 1 if extra else depth
    out_shape = (sum(item.shape[1] for item in mines),) + mines[0].shape[2:]
    in_spec = lambda item: pl.BlockSpec(
        (item.shape[0] // steps,) + item.shape[1:], lambda step, *_: (step, 0, 0, 0)
    )
    out_spec = pl.BlockSpec(((depth + extra) // steps,) + out_shape, lambda step, *_: (step, 0, 0, 0))
    size = sum(item.size for item in mines)
    return pl.pallas_call(
        lambda *refs: combine_core_kernel(*refs, arrays=arrays, extra=extra),
        out_shape=[jax.ShapeDtypeStruct((depth + extra,) + out_shape, bf16)] * 4,
        grid_spec=pltpu.PrefetchScalarGridSpec(
            num_scalar_prefetch=1,
            grid=(steps,),
            in_specs=[in_spec(item) for item in mines] * 2,
            out_specs=[out_spec] * 4,
        ),
        compiler_params=pltpu.CompilerParams(vmem_limit_bytes=62 * MIB),
        cost_estimate=cost(size, 6 * size),
        name="combine_core",
    )(plane, *mines, *others)


def split_two_kernel(bits_ref, *refs, modes):
    count = len(modes)
    outs = refs[2 * count :]
    for k, (inner, bit) in enumerate(modes):
        left, right = refs[2 * k], refs[2 * k + 1]
        for at in range(left.shape[0] // 2):
            base = at // inner * 2 * inner + at % inner
            for q in range(2):
                here = base + inner * lax.bitwise_xor(bits_ref[bit], q)
                summed = left[here].astype(f32) + right[here].astype(f32)
                outs[2 * k + q][at] = summed.astype(bf16)


def split_two(bits, pairs, modes, steps):
    flat = [item for pair in pairs for item in pair]
    spec = lambda shape: pl.BlockSpec(
        (shape[0] // steps,) + shape[1:], lambda step, *_: (step, 0, 0, 0)
    )
    half = lambda item: (item.shape[0] // 2,) + item.shape[1:]
    outs = [jax.ShapeDtypeStruct(half(pair[0]), bf16) for pair in pairs for _ in range(2)]
    size = sum(item.size for item in flat)
    return pl.pallas_call(
        lambda *refs: split_two_kernel(*refs, modes=modes),
        out_shape=outs,
        grid_spec=pltpu.PrefetchScalarGridSpec(
            num_scalar_prefetch=1,
            grid=(steps,),
            in_specs=[spec(item.shape) for item in flat],
            out_specs=[spec(item.shape) for item in outs],
        ),
        compiler_params=pltpu.CompilerParams(vmem_limit_bytes=62 * MIB),
        cost_estimate=cost(size, 3 * size),
        name="split_two",
    )(bits, *flat)


def split_depth_kernel(depth_ref, *refs):
    outs = refs[-4:]
    start = 0
    for k in range(len(refs) // 2 - 2):
        left, right = refs[2 * k], refs[2 * k + 1]
        size = left.shape[1]
        for q in range(4):
            at = lax.bitwise_xor(depth_ref[0], q)
            summed = left[at].astype(f32) + right[at].astype(f32)
            outs[q][start : start + size] = summed.astype(bf16)
        start += size


def split_depth(depth, pairs):
    flat = [item for pair in pairs for item in pair]
    shape = (sum(pair[0].shape[1] for pair in pairs),) + flat[0].shape[2:]
    size = sum(item.size for item in flat)
    return pl.pallas_call(
        split_depth_kernel,
        out_shape=[jax.ShapeDtypeStruct(shape, bf16)] * 4,
        grid_spec=pltpu.PrefetchScalarGridSpec(
            num_scalar_prefetch=1,
            grid=(1,),
            in_specs=[whole(item.shape) for item in flat],
            out_specs=[whole(shape)] * 4,
        ),
        compiler_params=pltpu.CompilerParams(vmem_limit_bytes=62 * MIB),
        cost_estimate=cost(size, 3 * size),
        name="split_depth",
    )(depth, *flat)


def four(values):
    return (values[0] + values[1]) + (values[2] + values[3])


def combine_plane_kernel(depth_ref, *refs, extra):
    parts, outs = refs[:4], refs[4:]
    size = parts[0].shape[1]
    for q in range(4):
        at = lax.bitwise_xor(depth_ref[0], q)
        outs[q][0:size] = four([part[at].astype(f32) for part in parts]).astype(bf16)
    if extra:
        vectors = four([load_split(part.at[PAIRS // 4], 0) for part in parts])
        for out in outs:
            store_split(out, size, vectors)


def combine_plane(depth, parts, extra):
    shape = (parts[0].shape[1] + 2 * VECTORS * extra,) + parts[0].shape[2:]
    size = 4 * parts[0].size
    return pl.pallas_call(
        lambda *refs: combine_plane_kernel(*refs, extra=extra),
        out_shape=[jax.ShapeDtypeStruct(shape, bf16)] * 4,
        grid_spec=pltpu.PrefetchScalarGridSpec(
            num_scalar_prefetch=1,
            grid=(1,),
            in_specs=[whole(item.shape) for item in parts],
            out_specs=[whole(shape)] * 4,
        ),
        compiler_params=pltpu.CompilerParams(vmem_limit_bytes=62 * MIB),
        cost_estimate=cost(size, 3 * size),
        name="combine_plane",
    )(depth, *parts)


def store_lines(outs, vectors, lines):
    for out, pieces in zip(outs, lines):
        out[...] = jnp.concatenate(
            [vectors[row : row + 1, 0:size] for row, size in pieces], axis=1
        ).reshape(-1)


def line_shapes(lines):
    return [jax.ShapeDtypeStruct((sum(size for _, size in pieces),), f32) for pieces in lines]


def combine_depth_kernel(*refs, places, lines):
    parts, outs = refs[:4], refs[4:]
    count = len(places)
    summed = four([part[0:count].astype(f32) for part in parts])
    for section, (out, row, column, columns, rows) in enumerate(places):
        stride = columns // LANES
        for lane in range(summed.shape[2] // LANES):
            start = row * stride + column // LANES + lane
            outs[out][pl.ds(start, rows, stride=stride), :] = summed[
                section, 0:rows, lane * LANES : (lane + 1) * LANES
            ]
    if lines:
        vectors = four([load_split(part, count) for part in parts])
        store_lines(outs[len(outs) - len(lines) :], vectors, lines)


def combine_depth(parts, places, sizes, lines):
    shapes = [jax.ShapeDtypeStruct((size // LANES, LANES), f32) for size in sizes] + line_shapes(lines)
    size = 4 * parts[0].size
    outs = pl.pallas_call(
        lambda *refs: combine_depth_kernel(*refs, places=places, lines=lines),
        out_shape=shapes,
        grid=(1,),
        in_specs=[whole(item.shape) for item in parts],
        out_specs=[whole(item.shape) for item in shapes],
        compiler_params=pltpu.CompilerParams(vmem_limit_bytes=62 * MIB),
        cost_estimate=cost(size, 3 * size),
        name="combine_depth",
    )(*parts)
    return [item.reshape(-1) for item in outs[: len(sizes)]], list(outs[len(sizes) :])


def sum_vectors_kernel(gathered_ref, *outs, lines):
    store_lines(outs, jnp.sum(gathered_ref[...], axis=0), lines)


def sum_vectors(gathered, lines):
    shapes = line_shapes(lines)
    return pl.pallas_call(
        lambda *refs: sum_vectors_kernel(*refs, lines=lines),
        out_shape=shapes,
        grid=(1,),
        in_specs=[whole(gathered.shape)],
        out_specs=[whole(item.shape) for item in shapes],
        compiler_params=pltpu.CompilerParams(vmem_limit_bytes=62 * MIB),
        name="sum_vectors",
    )(gathered)


def permuted(item, distance, devices):
    return lax.ppermute(item, BOTH, [(k, k ^ distance) for k in range(devices)])


class Sums:
    def __init__(self, index, devices):
        self.devices = devices
        self.plane = ((index // 2) % 4).astype(jnp.int32).reshape(1)
        self.depth = (index // 8).astype(jnp.int32).reshape(1)
        self.bits = jnp.stack([index // 4 % 2, index // 2 % 2]).astype(jnp.int32)

    def spread(self, parts, unit):
        return [parts[0]] + [permuted(parts[q], q * unit, self.devices) for q in (1, 2, 3)]

    def start_core(self, mines, others):
        return mines, [permuted(item, 1, self.devices) for item in others]

    def end_core(self, started, extra=0):
        return combine_core(self.plane, *started, extra)

    def halves(self, pairs, modes, distances, steps):
        outs = split_two(self.bits, pairs, modes, steps)
        return [
            (outs[2 * k], permuted(outs[2 * k + 1], distance, self.devices))
            for k, distance in enumerate(distances)
        ]

    def start_plane(self, parts):
        return self.spread(parts, 2)

    def end_plane(self, started, extra=0):
        return combine_plane(self.depth, started, extra)

    def start_depth(self, parts):
        return self.spread(parts, 8)


def after(value, *others):
    return lax.optimization_barrier((value,) + others)[0]


def ahead(value, others):
    leaves, tree = jax.tree.flatten(others)
    held = lax.optimization_barrier((value, leaves))
    return jax.tree.unflatten(tree, held[1])


def octets(out, rows, columns, width, offset=0):
    return [
        (out, 8 * part, start, columns, min(8, rows - 8 * part))
        for start in range(0, columns, width)
        for part in range(-(-rows // 8))
    ]


def scattered(mine, other, places, sizes, devices):
    blocks = jnp.stack([mine, other], axis=1).reshape((2 * PAIRS,) + mine.shape[1:])
    results = []
    for out, size in sizes:
        chosen = [k for k, place in enumerate(places) if place[0] == out]
        columns = places[chosen[0]][3]
        width = mine.shape[-1]
        rows = size // columns
        groups = columns // width
        values = blocks[:, chosen[0] : chosen[-1] + 1]
        values = values.reshape(2 * PAIRS, groups, -1, width)[:, :, :rows]
        values = jnp.moveaxis(values, 1, 2).reshape(devices, -1)
        length = values.shape[1]
        padded = -(-length // LANES) * LANES
        values = jnp.pad(values, ((0, 0), (0, padded - length))).reshape(devices, -1, LANES)
        own = lax.psum_scatter(values, BOTH, scatter_dimension=0, tiled=True)
        results.append(own.astype(f32).reshape(-1)[:length])
    return results


def shards(
    stem_input,
    image_class,
    owner,
    conv_in_weight,
    first_gain,
    first_bias,
    conv_mid_weight,
    second_gain,
    second_bias,
    conv_out_weight,
    third_gain,
    third_bias,
    embed_weight,
    embed_bias,
    position_table,
    attn_gain,
    attn_bias,
    joint_weight,
    query_bias,
    value_bias,
    mix_weight,
    mix_bias,
    mlp_gain,
    mlp_bias,
    expand_weight,
    expand_bias,
    shrink_weight,
    shrink_bias,
    cotangent,
):
    sections = lax.axis_size("section")
    devices = sections * lax.axis_size("batch")
    staged = (devices, sections) == (2 * PAIRS, 4)
    index = lax.axis_index(BOTH)
    images, cells, channels = stem_input.shape
    middle = conv_in_weight.shape[1]
    width = embed_weight.shape[1]
    inner = expand_weight.shape[1]
    section_index = lax.axis_index("section")
    mine = lax.dynamic_index_in_dim(owner.reshape(sections, images), section_index, 0, keepdims=False)
    core = ((index % 2) if staged else jnp.zeros((), jnp.int32)).astype(jnp.int32).reshape(1)
    received = lax.all_to_all(cotangent[0], "section", split_axis=0, concat_axis=0, tiled=True)
    norms = (first_gain, first_bias, second_gain, second_bias, third_gain, third_bias)
    weights = (conv_in_weight, conv_mid_weight.reshape(-1, middle), conv_out_weight)
    std_in, std_mid, std_out, first, second, third, stat1, stat2, stat3, stem, tokens = stem_forward(
        image_class, stem_input, *weights, norms, embed_weight, embed_bias, position_table
    )
    normed, query, key, value, log_total, mixed, resid, normed_two = attend_forward(
        image_class,
        tokens,
        attn_gain,
        attn_bias,
        joint_weight,
        query_bias,
        value_bias,
        mix_weight,
        mix_bias,
        mlp_gain,
        mlp_bias,
    )
    (
        outgoing,
        grad_resid,
        grad_mixed,
        shrink_mine,
        shrink_other,
        expand_mine,
        expand_other,
        sums_expand,
        sums_shrink,
        sums_mix,
    ) = feed(
        image_class,
        mine,
        core,
        normed_two,
        resid,
        received,
        expand_weight,
        expand_bias,
        shrink_weight,
        shrink_bias,
        mlp_gain,
        mix_weight,
    )
    sums = Sums(index, devices)
    if staged:
        feed_core = sums.start_core([shrink_mine, expand_mine], [shrink_other, expand_other])
    arrived = lax.all_to_all(outgoing, "section", split_axis=0, concat_axis=0, tiled=True)
    grad_joint0, sums_attend0 = attend_backward(
        0, image_class, query, key, value, log_total, grad_mixed
    )
    if staged:
        feed_core = ahead(grad_joint0, feed_core)
        feed_half = sums.halves(
            list(zip(*feed_core)), ((2, 0), (1, 1)), (4, 2), 4
        )
        grad_mixed = after(grad_mixed, feed_half[0][0])
    grad_joint1, sums_attend1 = attend_backward(
        1, image_class, query, key, value, log_total, grad_mixed
    )
    grad_tokens, joint_mine, joint_other, sums_attn, vectors_block = joint_backward(
        core,
        tokens,
        normed,
        mixed,
        grad_resid,
        grad_joint0,
        grad_joint1,
        attn_gain,
        joint_weight,
        sums_expand,
        sums_shrink,
        sums_mix,
        sums_attend0,
        sums_attend1,
    )
    gathered = lax.all_gather(vectors_block, BOTH)
    if staged:
        feed_half, arrived, joint_other = ahead(grad_tokens, (feed_half, arrived, joint_other))
        joint_other = after(joint_other, *feed_half[0], *feed_half[1], arrived)
        joint_core = sums.start_core([joint_mine], [joint_other])
        feed_quarter = sums.halves(feed_half, ((1, 1), (1, 0)), (2, 4), 1)
        grad_tokens = after(grad_tokens, feed_quarter[0][0])
    embed_mine, embed_other, sums_embed = embed_weights(image_class, core, grad_tokens, stem)
    if staged:
        joint_core, feed_quarter, grad_tokens = ahead(
            embed_mine, (joint_core, feed_quarter, grad_tokens)
        )
        embed_core = sums.start_core([embed_mine], [embed_other])
        joint_parts = sums.end_core(joint_core)
        joint_plane = sums.start_plane(joint_parts)
        feed_depth = split_depth(sums.depth, feed_quarter)
        grad_tokens = after(grad_tokens, joint_plane[0], feed_depth[0])
    grad_inner, grad_third, sums3 = embed_backward(
        image_class,
        grad_tokens,
        stem_input,
        third,
        stat3,
        third_gain,
        third_bias,
        embed_weight,
    )
    if staged:
        embed_core, joint_plane = ahead(grad_third, (embed_core, joint_plane))
        feed_depth = after(feed_depth, *joint_plane)
        feed_depth = sums.start_depth(feed_depth)
        embed_half = sums.halves(
            [(embed_core[0][0], embed_core[1][0])], ((2, 0),), (4,), 4
        )
        joint_parts = sums.end_plane(joint_plane)
        grad_third = after(grad_third, joint_parts[0], embed_half[0][0])
    grad_first, conv_mine, conv_other, block_output = convs_backward(
        image_class,
        core,
        grad_third,
        stem_input,
        first,
        second,
        stat1,
        stat2,
        (std_in, std_mid, std_out),
        weights,
        norms,
        sums_embed,
        sums3,
        sums_attn,
        arrived,
    )
    block_output = block_output[None]
    if staged:
        feed_depth, embed_half = ahead(grad_first, (feed_depth, embed_half))
        conv_other = after(conv_other, *feed_depth, *embed_half[0])
        conv_core = sums.start_core([conv_mine], [conv_other])
        embed_quarter = sums.halves(embed_half, ((1, 1),), (2,), 1)
        joint_depth = sums.start_depth(joint_parts)
        grad_first = after(grad_first, embed_quarter[0][0])
    input_grad = input_backward(image_class, grad_inner, grad_first, std_in)

    parts = 2 * PAIRS
    shrink_places = octets(0, inner // parts, width, width)
    expand_places = octets(1, width // parts, inner, width)
    feed_sizes = [inner // parts * width] * 2
    joint_places = octets(0, width // parts, 3 * width, width) + octets(1, width // parts, width, width)
    joint_sizes = [3 * width * width // parts, width * width // parts]
    embed_places = octets(0, channels // parts, width, width) + octets(1, cells // parts, width, width)
    embed_sizes = [channels * width // parts, cells * width // parts]
    conv_places = (
        octets(0, channels // parts, middle, middle)
        + octets(1, 9 * middle // parts, middle, middle)
        + octets(2, middle // parts, channels, middle)
    )
    conv_sizes = [
        channels * middle // parts,
        9 * middle * middle // parts,
        middle * channels // parts,
    ]
    block_lines = [[(row, width) for row in range(inner // width)]] + [
        [(row, width)] for row in range(inner // width, inner // width + 6)
    ]
    stem_lines = []
    row = 0
    for size in [width] * 3 + [middle] * 4 + [channels] * 2:
        stem_lines.append([(row + k, middle) for k in range(size // middle)])
        row += size // middle
    block_vectors = sum_vectors(gathered.reshape((-1,) + vectors_block.shape), block_lines)
    if staged:
        conv_plane = sums.start_plane(sums.end_core(conv_core, 1))
        embed_depth = sums.start_depth(split_depth(sums.depth, embed_quarter))
        (grad_shrink, grad_expand), _ = combine_depth(
            feed_depth, shrink_places + expand_places, feed_sizes, []
        )
        (grad_joint, grad_mix), _ = combine_depth(joint_depth, joint_places, joint_sizes, [])
        conv_plane = ahead(
            (input_grad, grad_shrink, grad_joint, block_vectors), conv_plane
        )
        conv_depth = sums.start_depth(sums.end_plane(conv_plane, 1))
        (grad_embed, grad_position), _ = combine_depth(embed_depth, embed_places, embed_sizes, [])
        (grad_in, grad_mid, grad_out), stem_vectors = combine_depth(
            conv_depth, conv_places, conv_sizes, stem_lines
        )
    else:
        (grad_shrink,) = scattered(
            shrink_mine, shrink_other, shrink_places, [(0, feed_sizes[0])], devices
        )
        (grad_expand,) = scattered(
            expand_mine, expand_other, expand_places, [(1, feed_sizes[1])], devices
        )
        grad_joint, grad_mix = scattered(
            joint_mine, joint_other, joint_places, list(enumerate(joint_sizes)), devices
        )
        grad_embed, grad_position = scattered(
            embed_mine, embed_other, embed_places, list(enumerate(embed_sizes)), devices
        )
        rows = conv_mine[PAIRS, :VECTORS].astype(f32) + conv_mine[PAIRS, VECTORS : 2 * VECTORS].astype(f32)
        rows = lax.psum(rows.reshape(-1, middle), BOTH)
        stem_vectors = [rows[pieces[0][0] : pieces[-1][0] + 1].reshape(-1) for pieces in stem_lines]
        conv_mine, conv_other = conv_mine[:PAIRS], conv_other[:PAIRS]
        grad_in, grad_mid, grad_out = scattered(
            conv_mine, conv_other, conv_places, list(enumerate(conv_sizes)), devices
        )
    (
        grad_expand_bias,
        grad_shrink_bias,
        grad_mlp_gain,
        grad_mlp_bias,
        grad_mix_bias,
        grad_query_bias,
        grad_value_bias,
    ) = block_vectors
    (
        grad_embed_bias,
        grad_attn_gain,
        grad_attn_bias,
        grad_first_gain,
        grad_first_bias,
        grad_second_gain,
        grad_second_bias,
        grad_third_gain,
        grad_third_bias,
    ) = stem_vectors
    return (
        block_output,
        input_grad,
        grad_in,
        grad_first_gain,
        grad_first_bias,
        grad_mid,
        grad_second_gain,
        grad_second_bias,
        grad_out,
        grad_third_gain,
        grad_third_bias,
        grad_embed,
        grad_embed_bias,
        grad_position,
        grad_attn_gain,
        grad_attn_bias,
        grad_joint,
        grad_query_bias,
        grad_value_bias,
        grad_mix,
        grad_mix_bias,
        grad_mlp_gain,
        grad_mlp_bias,
        grad_expand,
        grad_expand_bias,
        grad_shrink,
        grad_shrink_bias,
    )


def solution(mesh):
    split = P(BOTH)
    images = P(BOTH, None, None)
    slots = P(BOTH, None, None, None)
    full = P()
    in_specs = (images, split, P("batch")) + (full,) * 25 + (slots,)
    out_specs = (
        slots,
        images,
        split,
        full,
        full,
        split,
        full,
        full,
        split,
        full,
        full,
        split,
        full,
        split,
        full,
        full,
        split,
        full,
        full,
        split,
        full,
        full,
        full,
        split,
        full,
        split,
        full,
    )
    return jax.shard_map(shards, mesh=mesh, in_specs=in_specs, out_specs=out_specs, check_vma=False)
```

```python
import jax
import jax.numpy as jnp
from jax import lax
from jax.experimental import pallas as pl
from jax.experimental.pallas import tpu as pltpu
from jax.sharding import PartitionSpec as P

HEADS = 12
GROUPS = 32
SIDE = 24
SIDE_SMALL = 14
LANES = 128
MIB = 1024 * 1024
BOTH = ("batch", "section")

f32 = jnp.float32
bf16 = jnp.bfloat16


def dot_nn(left, right):
    return jnp.dot(left, right, preferred_element_type=f32)


def dot_tn(left, right):
    return lax.dot_general(left, right, (((0,), (0,)), ((), ())), preferred_element_type=f32)


def dot_nt(left, right):
    return lax.dot_general(left, right, (((1,), (1,)), ((), ())), preferred_element_type=f32)


def fold(values):
    rows, columns = values.shape
    return jnp.sum(values.reshape(rows // 8, 8, columns), axis=0)


def total(values):
    return jnp.sum(values, axis=0, keepdims=True)


def line(ref):
    return ref[...].reshape(1, -1)


def spread_lanes(mask, columns):
    return jnp.concatenate([mask] * (columns // LANES), axis=1)


def cdf_pdf(values):
    bell = jnp.exp(-0.5 * (values * values))
    t = 1.0 / (1.0 + 0.23164189 * jnp.abs(values))
    tail = (
        ((((0.5307027145 * t - 0.7265760135) * t + 0.7107068705) * t - 0.142248368) * t + 0.127414796)
        * t
        * bell
    )
    return jnp.where(values < 0.0, tail, 1.0 - tail), bell * 0.3989422804014327


def group_total(row, per_group):
    channels = row.shape[1]
    rows = jnp.broadcast_to(row, (8, channels))
    lane = lax.broadcasted_iota(jnp.int32, (8, LANES), 1)
    parts = []
    for k in range(channels // LANES):
        part = rows[:, k * LANES : (k + 1) * LANES]
        step = 1
        while step < per_group:
            up = pltpu.roll(part, LANES - step, 1)
            down = pltpu.roll(part, step, 1)
            part = part + jnp.where((lane & step) == 0, up, down)
            step *= 2
        parts.append(part)
    return jnp.concatenate(parts, axis=1)[0:1]


def cell_grid(cells):
    cell = lax.broadcasted_iota(jnp.int32, (cells, LANES), 0).astype(f32)
    row = jnp.floor((cell + 0.5) * (1.0 / SIDE))
    return row, cell - row * SIDE


def validity_mask(image_class, cells):
    row, column = cell_grid(cells)
    corner = jnp.where((row < SIDE_SMALL) & (column < SIDE_SMALL), 1.0, 0.0)
    return jnp.where(image_class == 1, 1.0, corner)


def valid_count(image_class):
    return jnp.where(image_class == 1, float(SIDE * SIDE), float(SIDE_SMALL * SIDE_SMALL))


def rows_at(index, size):
    return pl.ds(pl.multiple_of(index * size, size), size)


def fill_columns(grid_value, padded, columns, sign):
    cells, channels = grid_value.shape
    _, column = cell_grid(cells)
    has_left = spread_lanes(jnp.where(column > 0.5, 1.0, 0.0), channels)
    has_right = spread_lanes(jnp.where(column < SIDE - 1.5, 1.0, 0.0), channels)
    zeros = jnp.zeros((SIDE, channels), f32)
    shifted = (
        pltpu.roll(grid_value, 1, 0) * has_left,
        grid_value,
        pltpu.roll(grid_value, cells - 1, 0) * has_right,
    )
    for k in range(3):
        padded[k, 0:SIDE, :] = zeros
        padded[k, SIDE + cells : 2 * SIDE + cells, :] = zeros
        padded[k, SIDE : SIDE + cells, :] = shifted[k]
    for row_shift in range(3):
        for column_shift in range(3):
            tap = row_shift * 3 + column_shift
            down = row_shift if sign > 0 else 2 - row_shift
            across = column_shift if sign > 0 else 2 - column_shift
            columns[:, tap * channels : (tap + 1) * channels] = padded[
                across, down * SIDE : down * SIDE + cells, :
            ].astype(bf16)


def standardized(weight):
    rows = weight.shape[0]
    centred = weight - total(weight) * (1.0 / rows)
    spread = total(centred * centred) * (1.0 / rows)
    scale = lax.rsqrt(spread + 1e-05)
    return centred * scale, scale


def standardize_back(weight, grad):
    rows = weight.shape[0]
    normal, scale = standardized(weight)
    grad_mean = total(grad) * (1.0 / rows)
    inner = total(grad * normal) * (1.0 / rows)
    return scale * (grad - grad_mean - normal * inner)


PAIRS = 16
VECTORS = 7


def store_pairs(values, mine_ref, other_ref, core):
    pairs, parts = mine_ref.shape[:2]
    for pair in range(pairs):
        for ref, side in ((mine_ref, core), (other_ref, 1 - core)):
            at = pl.multiple_of((2 * pair + side) * parts * 8, 8)
            ref[pair] = sections_of(values[pl.ds(at, parts * 8), :])


def store_split(ref, start, values):
    high = values.astype(bf16)
    low = (values - high.astype(f32)).astype(bf16)
    shape = (VECTORS, 8, values.shape[-1])
    ref[start : start + VECTORS] = high.astype(f32).reshape(shape).astype(bf16)
    ref[start + VECTORS : start + 2 * VECTORS] = low.astype(f32).reshape(shape).astype(bf16)


def load_split(ref, start):
    high = ref[start : start + VECTORS].astype(f32)
    low = ref[start + VECTORS : start + 2 * VECTORS].astype(f32)
    rows = high + low
    return rows.reshape(VECTORS * 8, rows.shape[-1])


def sections_of(values):
    rows, columns = values.shape
    return values.reshape(rows // 8, 8, columns).astype(bf16)


def stem_forward_kernel(
    class_ref,
    x_ref,
    w_in_ref,
    w_mid_ref,
    w_out_ref,
    gain1_ref,
    bias1_ref,
    gain2_ref,
    bias2_ref,
    gain3_ref,
    bias3_ref,
    embed_ref,
    embed_bias_ref,
    position_ref,
    std_in_ref,
    std_mid_ref,
    std_out_ref,
    first_ref,
    second_ref,
    third_ref,
    stat1_ref,
    stat2_ref,
    stat3_ref,
    stem_ref,
    tokens_ref,
    mask,
    padded,
    columns,
    act_two,
):
    image = pl.program_id(0)
    cells = x_ref.shape[1]
    channels = x_ref.shape[2]
    middle = w_in_ref.shape[1]

    @pl.when(image == 0)
    def _():
        std_in_ref[...] = standardized(w_in_ref[...].astype(f32))[0].astype(bf16)
        std_mid_ref[...] = standardized(w_mid_ref[...].astype(f32))[0].astype(bf16)
        std_out_ref[...] = standardized(w_out_ref[...].astype(f32))[0].astype(bf16)

    image_class = class_ref[image]
    mask[...] = validity_mask(image_class, cells)
    count = valid_count(image_class)
    chunk = cells
    steps = cells // chunk

    def stats(values_ref, stat_ref, sums):
        width = values_ref.shape[2]
        per_group = width // GROUPS
        inverse = 1.0 / (count * per_group)
        centre = group_total(total(sums), per_group) * inverse

        def one(step, carry):
            rows = rows_at(step, chunk)
            centred = (values_ref[0, rows, :] - centre) * spread_lanes(mask[rows, :], width)
            return carry + fold(centred * centred)

        squares = lax.fori_loop(0, steps, one, jnp.zeros((8, width), f32))
        scale = lax.rsqrt(group_total(total(squares), per_group) * inverse + 1e-05)
        stat_ref[0, 0:1, :] = centre
        stat_ref[0, 1:2, :] = scale
        return centre, scale

    def first_step(step, carry):
        rows = rows_at(step, chunk)
        low = (x_ref[0, rows, :] * spread_lanes(mask[rows, :], channels)).astype(bf16)
        values = dot_nn(low, std_in_ref[...])
        first_ref[0, rows, :] = values
        return carry + fold(values)

    sums = lax.fori_loop(0, steps, first_step, jnp.zeros((8, middle), f32))
    centre, scale = stats(first_ref, stat1_ref, sums)
    gain = scale * line(gain1_ref)
    normed = (first_ref[0] - centre) * gain + line(bias1_ref)
    act = normed * cdf_pdf(normed)[0] * spread_lanes(mask[...], middle)
    fill_columns(act, padded, columns, 1)

    def second_step(step, carry):
        rows = rows_at(step, chunk)
        values = dot_nn(columns[rows, :], std_mid_ref[...])
        second_ref[0, rows, :] = values
        return carry + fold(values * spread_lanes(mask[rows, :], middle))

    sums = lax.fori_loop(0, steps, second_step, jnp.zeros((8, middle), f32))
    centre, scale = stats(second_ref, stat2_ref, sums)
    gain = scale * line(gain2_ref)
    normed = (second_ref[0] - centre) * gain + line(bias2_ref)
    act_two[...] = (normed * cdf_pdf(normed)[0] * spread_lanes(mask[...], middle)).astype(bf16)

    def third_step(step, carry):
        rows = rows_at(step, chunk)
        values = dot_nn(act_two[rows, :], std_out_ref[...])
        third_ref[0, rows, :] = values
        return carry + fold(values)

    sums = lax.fori_loop(0, steps, third_step, jnp.zeros((8, channels), f32))
    centre, scale = stats(third_ref, stat3_ref, sums)
    gain = scale * line(gain3_ref)

    @pl.loop(0, steps)
    def _(step):
        rows = rows_at(step, chunk)
        keep = mask[rows, :]
        keep_wide = spread_lanes(keep, channels)
        argument = (
            x_ref[0, rows, :] * keep_wide + (third_ref[0, rows, :] - centre) * gain + line(bias3_ref)
        )
        stem = (argument * cdf_pdf(argument)[0] * keep_wide).astype(bf16)
        stem_ref[0, rows, :] = stem
        values = dot_nn(stem, embed_ref[...]) + line(embed_bias_ref) + position_ref[rows, :].astype(f32)
        tokens_ref[0, rows, :] = (values * spread_lanes(keep, values.shape[1])).astype(bf16)


def cost(flops, moved):
    return pl.CostEstimate(flops=flops, bytes_accessed=moved, transcendentals=0)


def whole(shape):
    return pl.BlockSpec(shape, lambda *_: (0,) * len(shape))


def per_image(shape):
    return pl.BlockSpec((1,) + shape, lambda image, *_: (image,) + (0,) * len(shape))


def stem_forward(image_class, x, w_in, w_mid, w_out, norms, embed, embed_bias, position):
    images, cells, channels = x.shape
    middle = w_in.shape[1]
    width = embed.shape[1]
    row = lambda size: whole((size,))
    return pl.pallas_call(
        stem_forward_kernel,
        out_shape=(
            jax.ShapeDtypeStruct((channels, middle), bf16),
            jax.ShapeDtypeStruct((9 * middle, middle), bf16),
            jax.ShapeDtypeStruct((middle, channels), bf16),
            jax.ShapeDtypeStruct((images, cells, middle), f32),
            jax.ShapeDtypeStruct((images, cells, middle), f32),
            jax.ShapeDtypeStruct((images, cells, channels), f32),
            jax.ShapeDtypeStruct((images, 8, middle), f32),
            jax.ShapeDtypeStruct((images, 8, middle), f32),
            jax.ShapeDtypeStruct((images, 8, channels), f32),
            jax.ShapeDtypeStruct((images, cells, channels), bf16),
            jax.ShapeDtypeStruct((images, cells, width), bf16),
        ),
        grid_spec=pltpu.PrefetchScalarGridSpec(
            num_scalar_prefetch=1,
            grid=(images,),
            in_specs=[
                per_image((cells, channels)),
                whole((channels, middle)),
                whole((9 * middle, middle)),
                whole((middle, channels)),
                row(middle),
                row(middle),
                row(middle),
                row(middle),
                row(channels),
                row(channels),
                whole((channels, width)),
                row(width),
                whole((cells, width)),
            ],
            out_specs=[
                whole((channels, middle)),
                whole((9 * middle, middle)),
                whole((middle, channels)),
                per_image((cells, middle)),
                per_image((cells, middle)),
                per_image((cells, channels)),
                per_image((8, middle)),
                per_image((8, middle)),
                per_image((8, channels)),
                per_image((cells, channels)),
                per_image((cells, width)),
            ],
            scratch_shapes=[
                pltpu.VMEM((cells, LANES), f32),
                pltpu.VMEM((3, cells + 2 * SIDE, middle), f32),
                pltpu.VMEM((cells, 9 * middle), bf16),
                pltpu.VMEM((cells, middle), bf16),
            ],
        ),
        compiler_params=pltpu.CompilerParams(vmem_limit_bytes=62 * MIB),
        cost_estimate=cost(25_000_000_000, 30 * MIB),
        name="stem_forward",
    )(image_class, x, w_in, w_mid, w_out, *norms, embed, embed_bias, position)


def row_norm(values):
    centre = jnp.mean(values, axis=-1, keepdims=True)
    centred = values - centre
    scale = lax.rsqrt(jnp.mean(centred * centred, axis=-1, keepdims=True) + 1e-06)
    return centred * scale, scale


def attend_forward_kernel(
    class_ref,
    tokens_ref,
    gain1_ref,
    bias1_ref,
    joint_ref,
    query_bias_ref,
    value_bias_ref,
    mix_ref,
    mix_bias_ref,
    gain2_ref,
    bias2_ref,
    normed_ref,
    query_ref,
    key_ref,
    value_ref,
    log_total_ref,
    mixed_ref,
    resid_ref,
    normed_two_ref,
):
    image = pl.program_id(0)
    cells, width = tokens_ref.shape[1:]
    chunk = cells
    steps = cells // chunk
    scale = (width // HEADS) ** -0.5

    @pl.loop(0, steps)
    def _(step):
        rows = rows_at(step, chunk)
        normal, _ = row_norm(tokens_ref[0, rows, :].astype(f32))
        normed_ref[0, rows, :] = (normal * line(gain1_ref) + line(bias1_ref)).astype(bf16)

    block = 256
    query_bias = line(query_bias_ref)
    value_bias = line(value_bias_ref)
    for start in range(0, width, block):
        here = slice(start, start + block)
        later = slice(width + start, width + start + block)
        last = slice(2 * width + start, 2 * width + start + block)
        normed = normed_ref[0]
        query = dot_nn(normed, joint_ref[:, here]) + query_bias[:, here]
        query_ref[0, :, here] = query.astype(bf16)
        key_ref[0, :, here] = dot_nn(normed, joint_ref[:, later]).astype(bf16)
        value = dot_nn(normed, joint_ref[:, last]) + value_bias[:, here]
        value_ref[0, :, here] = value.astype(bf16)

    upper = lax.broadcasted_iota(jnp.int32, (cells, LANES), 1) >= LANES // 2
    key_bias = (validity_mask(class_ref[image], cells) - 1.0) * 1000000000.0
    key_bias = key_bias.astype(bf16)
    lane = lax.broadcasted_iota(jnp.int32, (cells, LANES), 1)

    @pl.loop(0, width // LANES, unroll=True)
    def _(pair):
        lanes = rows_at(pair, LANES)
        query = query_ref[0, :, lanes] * bf16(scale)
        key = key_ref[0, :, lanes]
        value = value_ref[0, :, lanes]
        outs = []
        for half in range(2):
            mine = upper if half else jnp.logical_not(upper)
            spare = lane == (0 if half else LANES // 2)
            scores = dot_nt(
                jnp.where(mine, key, jnp.where(spare, key_bias, bf16(0))),
                jnp.where(spare, bf16(1), query),
            )
            top = jnp.max(scores, axis=0, keepdims=True)
            weights = jnp.exp(scores - top)
            weight_sum = total(weights)
            probs = (weights * (1.0 / weight_sum)).astype(bf16)
            outs.append(dot_tn(probs, value))
            log_total_ref[0, 2 * pair + half] = jnp.broadcast_to(top + jnp.log(weight_sum), (8, cells))
        mixed_ref[0, :, lanes] = jnp.where(upper, outs[1], outs[0]).astype(bf16)

    @pl.loop(0, steps)
    def _(step):
        rows = rows_at(step, chunk)
        resid = (
            tokens_ref[0, rows, :].astype(f32)
            + dot_nn(mixed_ref[0, rows, :], mix_ref[...])
            + line(mix_bias_ref)
        )
        resid_ref[0, rows, :] = resid
        normal, _ = row_norm(resid)
        normed_two_ref[0, rows, :] = (normal * line(gain2_ref) + line(bias2_ref)).astype(bf16)


def attend_forward(
    image_class, tokens, gain1, bias1, joint, query_bias, value_bias, mix, mix_bias, gain2, bias2
):
    images, cells, width = tokens.shape
    row = whole((width,))
    low = jax.ShapeDtypeStruct((images, cells, width), bf16)
    low_spec = per_image((cells, width))
    return pl.pallas_call(
        attend_forward_kernel,
        out_shape=(
            low,
            low,
            low,
            low,
            jax.ShapeDtypeStruct((images, HEADS, 8, cells), f32),
            low,
            jax.ShapeDtypeStruct((images, cells, width), f32),
            low,
        ),
        grid_spec=pltpu.PrefetchScalarGridSpec(
            num_scalar_prefetch=1,
            grid=(images,),
            in_specs=[
                low_spec,
                row,
                row,
                whole((width, 3 * width)),
                row,
                row,
                whole((width, width)),
                row,
                row,
                row,
            ],
            out_specs=[
                low_spec,
                low_spec,
                low_spec,
                low_spec,
                per_image((HEADS, 8, cells)),
                low_spec,
                low_spec,
                low_spec,
            ],
        ),
        compiler_params=pltpu.CompilerParams(vmem_limit_bytes=62 * MIB),
        cost_estimate=cost(35_000_000_000, 30 * MIB),
        name="attend_forward",
    )(image_class, tokens, gain1, bias1, joint, query_bias, value_bias, mix, mix_bias, gain2, bias2)


def feed_kernel(
    class_ref,
    mine_ref,
    core_ref,
    normed_ref,
    cotangent0_ref,
    cotangent1_ref,
    expand_ref,
    expand_bias_ref,
    shrink_ref,
    shrink_bias_ref,
    gain2_ref,
    resid_ref,
    mix_ref,
    output_ref,
    grad_resid_ref,
    grad_mixed_ref,
    shrink_mine_ref,
    shrink_other_ref,
    expand_mine_ref,
    expand_other_ref,
    grad_expand_bias_ref,
    grad_shrink_bias_ref,
    sums_ref,
    sent,
    result,
    grad_normed,
    hidden,
    grad_pre,
    normed_turned,
    shrink_total,
    expand_total,
    biases,
    resid,
    mix,
    empty,
    in_sems,
    out_sems,
    empty_sems,
):
    step = pl.program_id(0)
    last = pl.num_programs(0) - 1
    images, cells, width = normed_ref.shape
    slots = output_ref.shape[0]
    block = expand_ref.shape[1]
    part = cells // 2
    loads = [
        pltpu.make_async_copy(resid_ref, resid, in_sems.at[0]),
        pltpu.make_async_copy(mix_ref, mix, in_sems.at[1]),
    ]

    def image_rows(image):
        return slice(image * cells, (image + 1) * cells)

    def each_empty(act):
        for slot in range(slots):
            taken = mine_ref[0] == slot
            for image in range(1, images):
                taken = taken | (mine_ref[image] == slot)

            @pl.when(jnp.logical_not(taken))
            def _():
                act(pltpu.make_async_copy(empty, output_ref.at[slot], empty_sems.at[slot]))

    @pl.when(step == 0)
    def _():
        empty[...] = jnp.zeros_like(empty)
        each_empty(lambda copy: copy.start())
        for copy in loads:
            copy.start()
        sums = jnp.zeros((8, width), f32)
        for image, ref in enumerate((cotangent0_ref, cotangent1_ref)):
            keep = spread_lanes(validity_mask(class_ref[image], cells), width)
            grad = ref[0].astype(f32) * keep
            sent[image_rows(image), :] = grad.astype(bf16)
            sums = sums + fold(grad)
        grad_shrink_bias_ref[...] = sums
        result[...] = jnp.zeros_like(result)
        grad_normed[...] = jnp.zeros_like(grad_normed)
        every = line(expand_bias_ref)
        for k in range(biases.shape[0]):
            biases[k : k + 1, :] = every[:, k * block : (k + 1) * block]

    bias_sums = jnp.zeros((8, block), f32)
    for image in range(images):
        for piece in range(cells // part):
            local = slice(piece * part, (piece + 1) * part)
            rows = slice(image * cells + piece * part, image * cells + (piece + 1) * part)
            pre = dot_nn(normed_ref[image, local, :], expand_ref[...]) + biases[pl.ds(step, 1), :]
            back = dot_nt(sent[rows, :], shrink_ref[...])
            cdf, pdf = cdf_pdf(pre)
            low = (pre * cdf).astype(bf16)
            hidden[rows, :] = low
            grad = back * (cdf + pre * pdf)
            bias_sums = bias_sums + fold(grad)
            grad_low = grad.astype(bf16)
            grad_pre[rows, :] = grad_low
            result[rows, :] += dot_nn(low, shrink_ref[...])
            grad_normed[rows, :] += dot_nt(grad_low, expand_ref[...])
    grad_expand_bias_ref[...] = bias_sums
    shrink_total[...] = dot_tn(hidden[...], sent[...])
    expand_total[...] = dot_tn(normed_ref[...].reshape(images * cells, width), grad_pre[...])
    core = core_ref[0]
    store_pairs(shrink_total, shrink_mine_ref, shrink_other_ref, core)
    store_pairs(expand_total, expand_mine_ref, expand_other_ref, core)

    @pl.when(step == last)
    def _():
        for copy in loads:
            copy.wait()
        stores = []
        for image in range(images):
            rows = image_rows(image)
            keep = spread_lanes(validity_mask(class_ref[image], cells), width)
            out = (resid[image] + result[rows, :] + line(shrink_bias_ref)) * keep
            hidden[rows, :] = out.astype(bf16)
            stores.append(
                pltpu.make_async_copy(
                    hidden.at[pl.ds(image * cells, cells)],
                    output_ref.at[mine_ref[image]],
                    out_sems.at[3 * image],
                )
            )
            stores[-1].start()
        sums = [jnp.zeros((8, width), f32)] * 3
        for image in range(images):
            rows = image_rows(image)
            normal, row_scale = row_norm(resid[image])
            grad = grad_normed[rows, :]
            sums[0] = sums[0] + fold(grad * normal)
            sums[1] = sums[1] + fold(grad)
            grad = sent[rows, :].astype(f32) + row_norm_back(grad, normal, row_scale, line(gain2_ref))
            sums[2] = sums[2] + fold(grad)
            resid[image] = grad
            stores.append(
                pltpu.make_async_copy(resid.at[image], grad_resid_ref.at[image], out_sems.at[3 * image + 1])
            )
            stores[-1].start()
            grad_pre[rows, :] = dot_nt(grad.astype(bf16), mix[...]).astype(bf16)
            stores.append(
                pltpu.make_async_copy(
                    grad_pre.at[pl.ds(image * cells, cells)],
                    grad_mixed_ref.at[image],
                    out_sems.at[3 * image + 2],
                )
            )
            stores[-1].start()
        for k in range(3):
            sums_ref[k] = sums[k]
        each_empty(lambda copy: copy.wait())
        for copy in stores:
            copy.wait()


def feed(
    image_class, mine, core, normed, resid, cotangent, expand, expand_bias, shrink, shrink_bias, gain2, mix
):
    images, cells, width = normed.shape
    inner = expand.shape[1]
    slots = cotangent.shape[0]
    block = width
    rows = images * cells
    shrink_size = inner // (2 * PAIRS)
    pairs = block // (2 * shrink_size)
    expand_size = width // (2 * PAIRS)
    shrink_half = jax.ShapeDtypeStruct((PAIRS, shrink_size // 8, 8, width), bf16)
    expand_half = jax.ShapeDtypeStruct((PAIRS, expand_size // 8 * (inner // width), 8, width), bf16)
    shrink_spec = pl.BlockSpec((pairs, shrink_size // 8, 8, width), lambda step, *_: (step, 0, 0, 0))
    expand_spec = pl.BlockSpec((PAIRS, expand_size // 8, 8, block), lambda step, *_: (0, step, 0, 0))
    anywhere = pl.BlockSpec(memory_space=pl.ANY)
    return pl.pallas_call(
        feed_kernel,
        out_shape=(
            jax.ShapeDtypeStruct((slots, cells, width), bf16),
            jax.ShapeDtypeStruct((images, cells, width), f32),
            jax.ShapeDtypeStruct((images, cells, width), bf16),
            shrink_half,
            shrink_half,
            expand_half,
            expand_half,
            jax.ShapeDtypeStruct((8, inner), f32),
            jax.ShapeDtypeStruct((8, width), f32),
            jax.ShapeDtypeStruct((3, 8, width), f32),
        ),
        grid_spec=pltpu.PrefetchScalarGridSpec(
            num_scalar_prefetch=3,
            grid=(inner // block,),
            in_specs=[
                whole((images, cells, width)),
                pl.BlockSpec((1, cells, width), lambda step, classes, mine, core: (mine[0], 0, 0)),
                pl.BlockSpec((1, cells, width), lambda step, classes, mine, core: (mine[1], 0, 0)),
                pl.BlockSpec((width, block), lambda step, *_: (0, step)),
                whole((inner,)),
                pl.BlockSpec((block, width), lambda step, *_: (step, 0)),
                whole((width,)),
                whole((width,)),
                anywhere,
                anywhere,
            ],
            out_specs=[
                anywhere,
                anywhere,
                anywhere,
                shrink_spec,
                shrink_spec,
                expand_spec,
                expand_spec,
                pl.BlockSpec((8, block), lambda step, *_: (0, step)),
                whole((8, width)),
                whole((3, 8, width)),
            ],
            scratch_shapes=[
                pltpu.VMEM((rows, width), bf16),
                pltpu.VMEM((rows, width), f32),
                pltpu.VMEM((rows, width), f32),
                pltpu.VMEM((rows, block), bf16),
                pltpu.VMEM((rows, block), bf16),
                pltpu.VMEM((width, rows), bf16),
                pltpu.VMEM((block, width), f32),
                pltpu.VMEM((width, block), f32),
                pltpu.VMEM((inner // block, block), f32),
                pltpu.VMEM((images, cells, width), f32),
                pltpu.VMEM((width, width), bf16),
                pltpu.VMEM((cells, width), bf16),
                pltpu.SemaphoreType.DMA((2,)),
                pltpu.SemaphoreType.DMA((3 * images,)),
                pltpu.SemaphoreType.DMA((slots,)),
            ],
        ),
        compiler_params=pltpu.CompilerParams(vmem_limit_bytes=62 * MIB),
        cost_estimate=cost(14 * rows * width * inner, 40 * MIB),
        name="feed",
    )(
        image_class,
        mine,
        core,
        normed,
        cotangent,
        cotangent,
        expand,
        expand_bias,
        shrink,
        shrink_bias,
        gain2,
        resid,
        mix,
    )


def row_norm_back(grad, normal, scale, gain):
    inner = grad * gain
    mean = jnp.mean(inner, axis=-1, keepdims=True)
    cross = jnp.mean(inner * normal, axis=-1, keepdims=True)
    return scale * (inner - mean - normal * cross)


def attend_backward_kernel(
    class_ref,
    query_ref,
    key_ref,
    value_ref,
    log_total_ref,
    grad_mixed_ref,
    grad_joint_ref,
    sums_ref,
    *,
    image,
):
    cells, width = query_ref.shape[1:]
    scale = (width // HEADS) ** -0.5

    upper = lax.broadcasted_iota(jnp.int32, (cells, LANES), 1) >= LANES // 2
    key_bias = (validity_mask(class_ref[image], cells) - 1.0) * 1000000000.0
    key_bias = key_bias.astype(bf16)
    lane = lax.broadcasted_iota(jnp.int32, (cells, LANES), 1)

    @pl.loop(0, width // LANES, unroll=True)
    def _(pair):
        lanes = rows_at(pair, LANES)
        query = query_ref[0, :, lanes] * bf16(scale)
        key = key_ref[0, :, lanes]
        value = value_ref[0, :, lanes]
        grad_out = grad_mixed_ref[0, :, lanes]
        grads = []
        for half in range(2):
            mine = upper if half else jnp.logical_not(upper)
            spare = lane == (0 if half else LANES // 2)
            scores = dot_nt(
                jnp.where(mine, key, jnp.where(spare, key_bias, bf16(0))),
                jnp.where(spare, bf16(1), query),
            )
            log_total = log_total_ref[0, 2 * pair + half, 0:1, :]
            probs = jnp.exp(scores - log_total)
            grad_probs = dot_nt(jnp.where(mine, value, bf16(0)), grad_out)
            weighted = probs * grad_probs
            grad_scores = (weighted - probs * total(weighted)).astype(bf16)
            grad_value = dot_nn(probs.astype(bf16), grad_out)
            grad_key = dot_nn(grad_scores, query)
            grad_query = dot_tn(grad_scores, key) * scale
            grads.append((grad_query, grad_key, grad_value))
        for k in range(3):
            grad = jnp.where(upper, grads[1][k], grads[0][k])
            if k != 1:
                sums_ref[k // 2, :, lanes] = fold(grad)
            where = pl.ds(pl.multiple_of(k * width + pair * LANES, LANES), LANES)
            grad_joint_ref[0, :, where] = grad.astype(bf16)


def attend_backward(image, image_class, query, key, value, log_total, grad_mixed):
    images, cells, width = query.shape
    own = lambda shape: pl.BlockSpec((1,) + shape, lambda *_: (image,) + (0,) * len(shape))
    rows = own((cells, width))
    return pl.pallas_call(
        lambda *refs: attend_backward_kernel(*refs, image=image),
        out_shape=(
            jax.ShapeDtypeStruct((1, cells, 3 * width), bf16),
            jax.ShapeDtypeStruct((2, 8, width), f32),
        ),
        grid_spec=pltpu.PrefetchScalarGridSpec(
            num_scalar_prefetch=1,
            grid=(1,),
            in_specs=[rows, rows, rows, own((HEADS, 8, cells)), rows],
            out_specs=[whole((1, cells, 3 * width)), whole((2, 8, width))],
        ),
        compiler_params=pltpu.CompilerParams(vmem_limit_bytes=62 * MIB),
        cost_estimate=cost(40 * cells * cells * width, 6 * MIB),
        name="attend_backward",
    )(image_class, query, key, value, log_total, grad_mixed)


def joint_backward_kernel(
    core_ref,
    normed_ref,
    grad_joint0_ref,
    grad_joint1_ref,
    joint_ref,
    gain1_ref,
    tokens_ref,
    mixed_ref,
    grad_resid_ref,
    grad_tokens_ref,
    mine_ref,
    other_ref,
    sums_ref,
    grad_joint,
    weight_total,
    grad_normed,
    tokens,
    mixed,
    grad_resid,
    sems,
):
    step = pl.program_id(0)
    last = pl.num_programs(0) - 1
    images, cells, width = normed_ref.shape
    rows = images * cells
    loads = [
        pltpu.make_async_copy(mixed_ref, mixed, sems.at[0]),
        pltpu.make_async_copy(grad_resid_ref, grad_resid, sems.at[1]),
        pltpu.make_async_copy(tokens_ref, tokens, sems.at[2]),
    ]

    @pl.when(step == 0)
    def _():
        for copy in loads:
            copy.start()
        grad_normed[...] = jnp.zeros_like(grad_normed)

    @pl.when(step < last)
    def _():
        grad_joint[0:cells, :] = grad_joint0_ref[0]
        grad_joint[cells:rows, :] = grad_joint1_ref[0]
        weight_total[...] = dot_tn(normed_ref[...].reshape(rows, width), grad_joint[...])
        grad_normed[...] += dot_nt(grad_joint[...], joint_ref[...])

    @pl.when(step == last)
    def _():
        for copy in loads:
            copy.wait()
        low = grad_resid[...].reshape(rows, width).astype(bf16)
        weight_total[...] = dot_tn(mixed[...].reshape(rows, width), low)
        sums = [jnp.zeros((8, width), f32)] * 2
        for image in range(images):
            at = slice(image * cells, (image + 1) * cells)
            normal, row_scale = row_norm(tokens[image].astype(f32))
            grad = grad_normed[at, :]
            sums[0] = sums[0] + fold(grad * normal)
            sums[1] = sums[1] + fold(grad)
            back = row_norm_back(grad, normal, row_scale, line(gain1_ref))
            grad_tokens_ref[image] = (grad_resid[image] + back).astype(bf16)
        sums_ref[0] = sums[0]
        sums_ref[1] = sums[1]

    store_pairs(weight_total, mine_ref, other_ref, core_ref[0])


def joint_backward(
    core,
    tokens,
    normed,
    mixed,
    grad_resid,
    grad_joint0,
    grad_joint1,
    gain1,
    joint,
):
    images, cells, width = tokens.shape
    size = width // (2 * PAIRS)
    half = (PAIRS, 4 * size // 8, 8, width)
    half_spec = pl.BlockSpec((PAIRS, size // 8, 8, width), lambda step, *_: (0, step, 0, 0))
    column = lambda step, *_: (0, 0, jnp.minimum(step, 2))
    anywhere = pl.BlockSpec(memory_space=pl.ANY)
    return pl.pallas_call(
        joint_backward_kernel,
        out_shape=(
            jax.ShapeDtypeStruct((images, cells, width), bf16),
            jax.ShapeDtypeStruct(half, bf16),
            jax.ShapeDtypeStruct(half, bf16),
            jax.ShapeDtypeStruct((2, 8, width), f32),
        ),
        grid_spec=pltpu.PrefetchScalarGridSpec(
            num_scalar_prefetch=1,
            grid=(4,),
            in_specs=[
                whole((images, cells, width)),
                pl.BlockSpec((1, cells, width), column),
                pl.BlockSpec((1, cells, width), column),
                pl.BlockSpec((width, width), lambda step, *_: (0, jnp.minimum(step, 2))),
                whole((width,)),
                anywhere,
                anywhere,
                anywhere,
            ],
            out_specs=[
                whole((images, cells, width)),
                half_spec,
                half_spec,
                whole((2, 8, width)),
            ],
            scratch_shapes=[
                pltpu.VMEM((images * cells, width), bf16),
                pltpu.VMEM((width, width), f32),
                pltpu.VMEM((images * cells, width), f32),
                pltpu.VMEM((images, cells, width), bf16),
                pltpu.VMEM((images, cells, width), bf16),
                pltpu.VMEM((images, cells, width), f32),
                pltpu.SemaphoreType.DMA((3,)),
            ],
        ),
        compiler_params=pltpu.CompilerParams(vmem_limit_bytes=62 * MIB),
        cost_estimate=cost(14 * images * cells * width * width, 25 * MIB),
        name="joint_backward",
    )(
        core,
        normed,
        grad_joint0,
        grad_joint1,
        joint,
        gain1,
        tokens,
        mixed,
        grad_resid,
    )


def norm_means(sums, gain, per_group, count):
    inverse = 1.0 / (count * per_group)
    return [group_total(total(item) * gain, per_group) * inverse for item in sums]


def embed_weights_kernel(
    class_ref,
    grad_tokens_ref,
    stem_ref,
    blocks_ref,
    sums_ref,
    grad_masked,
    weight_total,
    position_total,
):
    images, cells, width = grad_tokens_ref.shape
    channels = stem_ref.shape[2]
    sums = jnp.zeros((8, width), f32)
    position = jnp.zeros((cells, width), f32)
    for image in range(images):
        keep = spread_lanes(validity_mask(class_ref[image], cells), width)
        grad = grad_tokens_ref[image].astype(f32) * keep
        grad_masked[image * cells : (image + 1) * cells, :] = grad.astype(bf16)
        sums = sums + fold(grad)
        position = position + grad
    sums_ref[...] = sums
    grad_position = weight_total.at[pl.ds(0, cells)]
    grad_position[...] = position
    position_rows = cells // (2 * PAIRS)
    position_total[...] = jnp.zeros_like(position_total)
    for block in range(2 * PAIRS):
        position_total[block, 0:position_rows, :] = grad_position[
            block * position_rows : (block + 1) * position_rows, :
        ]
    weight_total[...] = dot_tn(stem_ref[...].reshape(images * cells, channels), grad_masked[...])
    size = channels // (2 * PAIRS)
    for block in range(2 * PAIRS):
        blocks_ref[block, 0 : size // 8] = sections_of(weight_total[block * size : (block + 1) * size, :])
        blocks_ref[block, size // 8 :] = sections_of(position_total[block])


def embed_weights(image_class, grad_tokens, stem):
    images, cells, width = grad_tokens.shape
    channels = stem.shape[2]
    position_rows = -(-cells // (2 * PAIRS) // 8) * 8
    blocks = (2 * PAIRS, (channels // (2 * PAIRS) + position_rows) // 8, 8, width)
    return pl.pallas_call(
        embed_weights_kernel,
        out_shape=(
            jax.ShapeDtypeStruct(blocks, bf16),
            jax.ShapeDtypeStruct((8, width), f32),
        ),
        grid_spec=pltpu.PrefetchScalarGridSpec(
            num_scalar_prefetch=1,
            grid=(1,),
            in_specs=[whole(grad_tokens.shape), whole(stem.shape)],
            out_specs=[whole(blocks), whole((8, width))],
            scratch_shapes=[
                pltpu.VMEM((images * cells, width), bf16),
                pltpu.VMEM((channels, width), f32),
                pltpu.VMEM((2 * PAIRS, position_rows, width), f32),
            ],
        ),
        compiler_params=pltpu.CompilerParams(vmem_limit_bytes=62 * MIB),
        cost_estimate=cost(8_000_000_000, 8 * MIB),
        name="embed_weights",
    )(image_class, grad_tokens, stem)


def embed_backward_kernel(
    class_ref,
    grad_tokens_ref,
    x_ref,
    third_ref,
    stat3_ref,
    gain3_ref,
    bias3_ref,
    embed_ref,
    grad_inner_ref,
    grad_third_ref,
    sums3_ref,
    mask,
):
    image = pl.program_id(0)
    cells, channels = x_ref.shape[1:]
    chunk = cells
    steps = cells // chunk
    image_class = class_ref[image]
    mask[...] = validity_mask(image_class, cells)
    count = valid_count(image_class)

    @pl.when(image == 0)
    def _():
        sums3_ref[...] = jnp.zeros_like(sums3_ref)

    centre, scale = stat3_ref[0, 0:1, :], stat3_ref[0, 1:2, :]
    gain = line(gain3_ref)

    def third_step(step, carry):
        rows = rows_at(step, chunk)
        keep = spread_lanes(mask[rows, :], channels)
        grad = dot_nt(grad_tokens_ref[0, rows, :], embed_ref[...]) * keep
        normal = (third_ref[0, rows, :] - centre) * scale
        argument = x_ref[0, rows, :] * keep + normal * gain + line(bias3_ref)
        cdf, pdf = cdf_pdf(argument)
        grad = grad * (cdf + argument * pdf)
        grad_inner_ref[0, rows, :] = grad
        return carry[0] + fold(grad * normal), carry[1] + fold(grad)

    zeros = jnp.zeros((8, channels), f32)
    with_normal, plain = lax.fori_loop(0, steps, third_step, (zeros, zeros))
    sums3_ref[0] += with_normal
    sums3_ref[1] += plain
    mean, cross = norm_means((plain, with_normal), gain, channels // GROUPS, count)
    outer = scale * gain
    mean = mean * scale
    cross = cross * scale

    @pl.loop(0, steps)
    def _(step):
        rows = rows_at(step, chunk)
        keep = spread_lanes(mask[rows, :], channels)
        normal = (third_ref[0, rows, :] - centre) * scale
        grad = (grad_inner_ref[0, rows, :] * outer - mean - normal * cross) * keep
        grad_third_ref[0, rows, :] = grad.astype(bf16)


def embed_backward(image_class, grad_tokens, x, third, stat3, gain3, bias3, embed):
    images, cells, channels = x.shape
    width = embed.shape[1]
    return pl.pallas_call(
        embed_backward_kernel,
        out_shape=(
            jax.ShapeDtypeStruct((images, cells, channels), f32),
            jax.ShapeDtypeStruct((images, cells, channels), bf16),
            jax.ShapeDtypeStruct((2, 8, channels), f32),
        ),
        grid_spec=pltpu.PrefetchScalarGridSpec(
            num_scalar_prefetch=1,
            grid=(images,),
            in_specs=[
                per_image((cells, width)),
                per_image((cells, channels)),
                per_image((cells, channels)),
                per_image((8, channels)),
                whole((channels,)),
                whole((channels,)),
                whole((channels, width)),
            ],
            out_specs=[
                per_image((cells, channels)),
                per_image((cells, channels)),
                whole((2, 8, channels)),
            ],
            scratch_shapes=[
                pltpu.VMEM((cells, LANES), f32),
            ],
        ),
        compiler_params=pltpu.CompilerParams(vmem_limit_bytes=62 * MIB),
        cost_estimate=cost(20_000_000_000, 30 * MIB),
        name="embed_backward",
    )(image_class, grad_tokens, x, third, stat3, gain3, bias3, embed)


def convs_backward_kernel(
    class_ref,
    core_ref,
    grad_third_ref,
    x_ref,
    first_ref,
    second_ref,
    stat1_ref,
    stat2_ref,
    std_in_ref,
    std_mid_ref,
    std_out_ref,
    w_in_ref,
    w_mid_ref,
    w_out_ref,
    gain1_ref,
    bias1_ref,
    gain2_ref,
    bias2_ref,
    sums_embed_ref,
    sums3_ref,
    sums_attn_ref,
    sums_expand_ref,
    sums_shrink_ref,
    sums_mix_ref,
    sums_attend0_ref,
    sums_attend1_ref,
    arrived_ref,
    grad_first_ref,
    mine_ref,
    other_ref,
    output_ref,
    vectors,
    sums1,
    sums2,
    mask,
    act,
    padded,
    columns,
    in_total,
    mid_total,
    out_total,
    mid_done,
    in_done,
):
    image = pl.program_id(0)
    last = pl.num_programs(0) - 1
    output_ref[...] = arrived_ref[...]
    cells, channels = x_ref.shape[1:]
    width = sums_embed_ref.shape[1]
    middle = first_ref.shape[2]
    image_class = class_ref[image]
    mask[...] = validity_mask(image_class, cells)
    count = valid_count(image_class)

    @pl.when(image == 0)
    def _():
        for ref in (sums1, sums2, in_total, mid_total, out_total):
            ref[...] = jnp.zeros_like(ref)

    def middle_norm(values_ref, stat_ref, gain_ref, bias_ref, sums_ref, grad_of):
        centre, scale = stat_ref[0, 0:1, :], stat_ref[0, 1:2, :]
        gain = line(gain_ref)
        keep = spread_lanes(mask[...], middle)
        normal = (values_ref[0] - centre) * scale
        argument = normal * gain + line(bias_ref)
        cdf, pdf = cdf_pdf(argument)
        act[...] = (argument * cdf * keep).astype(bf16)
        grad = grad_of() * keep * (cdf + argument * pdf)
        plain, with_normal = fold(grad), fold(grad * normal)
        sums_ref[0] += with_normal
        sums_ref[1] += plain
        mean, cross = norm_means((plain, with_normal), gain, middle // GROUPS, count)
        return (grad * (scale * gain) - mean * scale - normal * (cross * scale)) * keep

    grad_second = middle_norm(
        second_ref,
        stat2_ref,
        gain2_ref,
        bias2_ref,
        sums2,
        lambda: dot_nt(grad_third_ref[0], std_out_ref[...]),
    )
    out_total[...] += dot_tn(act[...], grad_third_ref[0])
    fill_columns(grad_second, padded, columns, -1)

    def spread_back():
        grad = jnp.zeros((cells, middle), f32)
        for tap in range(9):
            part = slice(tap * middle, (tap + 1) * middle)
            grad = grad + dot_nt(columns[:, part], std_mid_ref[part, :])
        return grad

    grad = middle_norm(first_ref, stat1_ref, gain1_ref, bias1_ref, sums1, spread_back)
    grad_low = grad.astype(bf16)
    grad_first_ref[0] = grad_low
    mid_total[...] += dot_tn(act[...], columns[...])
    low = (x_ref[0] * spread_lanes(mask[...], channels)).astype(bf16)
    in_total[...] += dot_tn(grad_low, low)

    @pl.when(image == last)
    def _():
        core = core_ref[0]
        out_total[...] = standardize_back(w_out_ref[...].astype(f32), out_total[...])
        in_done[...] = standardize_back(w_in_ref[...].astype(f32), in_total[...].T)
        rows = 9 * middle
        normal, scale = standardized(w_mid_ref[...].astype(f32))
        grads = [mid_total[:, tap * middle : (tap + 1) * middle] for tap in range(9)]
        grad_mean = sum(total(g) for g in grads) * (1.0 / rows)
        inner = sum(
            total(g * normal[tap * middle : (tap + 1) * middle]) for tap, g in enumerate(grads)
        ) * (1.0 / rows)
        for tap, g in enumerate(grads):
            part = slice(tap * middle, (tap + 1) * middle)
            mid_done[part, :] = scale * (g - grad_mean - normal[part] * inner)
        in_size = channels // (2 * PAIRS)
        mid_size = rows // (2 * PAIRS)
        out_size = middle // (2 * PAIRS)
        in_parts = in_size // 8
        mid_parts = mid_size // 8
        for pair in range(PAIRS):
            for ref, side in ((mine_ref, core), (other_ref, 1 - core)):
                block = 2 * pair + side
                at = pl.ds(pl.multiple_of(block * in_size, 8), in_size)
                ref[pair, 0:in_parts] = sections_of(in_done[at, :])
                at = pl.ds(pl.multiple_of(block * mid_size, 8), mid_size)
                ref[pair, in_parts : in_parts + mid_parts] = sections_of(mid_done[at, :])
                at = pl.ds(pl.multiple_of(block * out_size, 8), out_size)
                for k in range(channels // middle):
                    ref[pair, in_parts + mid_parts + k] = out_total[
                        at, k * middle : (k + 1) * middle
                    ].astype(bf16)
        vectors[...] = jnp.zeros_like(vectors)
        row = 0
        for item in (
            total(sums_embed_ref[...]),
            total(sums_attn_ref[0]),
            total(sums_attn_ref[1]),
            total(sums1[0]),
            total(sums1[1]),
            total(sums2[0]),
            total(sums2[1]),
            total(sums3_ref[0]),
            total(sums3_ref[1]),
            total(sums_expand_ref[...]),
            total(sums_shrink_ref[...]),
            total(sums_mix_ref[0]),
            total(sums_mix_ref[1]),
            total(sums_mix_ref[2]),
            total(sums_attend0_ref[0] + sums_attend1_ref[0]),
            total(sums_attend0_ref[1] + sums_attend1_ref[1]),
        ):
            for start in range(0, item.shape[1], middle):
                vectors[row : row + 1, :] = item[:, start : start + middle]
                row += 1
        mine_ref[PAIRS] = jnp.zeros(mine_ref.shape[1:], bf16)
        store_split(mine_ref.at[PAIRS], 0, vectors[...])
        other_ref[PAIRS] = mine_ref[PAIRS]


def convs_backward(
    image_class,
    core,
    grad_third,
    x,
    first,
    second,
    stat1,
    stat2,
    stds,
    weights,
    norms,
    sums_embed,
    sums3,
    sums_attn,
    sums_block,
    arrived,
):
    images, cells, channels = x.shape
    middle = first.shape[2]
    width = sums_embed.shape[1]
    row = lambda size: whole((size,))
    conv_rows = channels // (2 * PAIRS) + 9 * middle // (2 * PAIRS) + middle // (2 * PAIRS) * (channels // middle)
    half = (PAIRS + 1, conv_rows // 8, 8, middle)
    slot_spec = pl.BlockSpec(
        (arrived.shape[0] // images,) + arrived.shape[1:], lambda image, *_: (image, 0, 0)
    )
    return pl.pallas_call(
        convs_backward_kernel,
        out_shape=(
            jax.ShapeDtypeStruct((images, cells, middle), bf16),
            jax.ShapeDtypeStruct(half, bf16),
            jax.ShapeDtypeStruct(half, bf16),
            jax.ShapeDtypeStruct(arrived.shape, bf16),
        ),
        grid_spec=pltpu.PrefetchScalarGridSpec(
            num_scalar_prefetch=2,
            grid=(images,),
            in_specs=[
                per_image((cells, channels)),
                per_image((cells, channels)),
                per_image((cells, middle)),
                per_image((cells, middle)),
                per_image((8, middle)),
                per_image((8, middle)),
                whole((channels, middle)),
                whole((9 * middle, middle)),
                whole((middle, channels)),
                whole((channels, middle)),
                whole((9 * middle, middle)),
                whole((middle, channels)),
                row(middle),
                row(middle),
                row(middle),
                row(middle),
                whole((8, width)),
                whole((2, 8, channels)),
                whole((2, 8, width)),
                *[whole(item.shape) for item in sums_block],
                slot_spec,
            ],
            out_specs=[
                per_image((cells, middle)),
                whole(half),
                whole(half),
                slot_spec,
            ],
            scratch_shapes=[
                pltpu.VMEM((VECTORS * 8, middle), f32),
                pltpu.VMEM((2, 8, middle), f32),
                pltpu.VMEM((2, 8, middle), f32),
                pltpu.VMEM((cells, LANES), f32),
                pltpu.VMEM((cells, middle), bf16),
                pltpu.VMEM((3, cells + 2 * SIDE, middle), f32),
                pltpu.VMEM((cells, 9 * middle), bf16),
                pltpu.VMEM((middle, channels), f32),
                pltpu.VMEM((middle, 9 * middle), f32),
                pltpu.VMEM((middle, channels), f32),
                pltpu.VMEM((9 * middle, middle), f32),
                pltpu.VMEM((channels, middle), f32),
            ],
        ),
        compiler_params=pltpu.CompilerParams(vmem_limit_bytes=62 * MIB),
        cost_estimate=cost(20_000_000_000, 20 * MIB),
        name="convs_backward",
    )(
        image_class,
        core,
        grad_third,
        x,
        first,
        second,
        stat1,
        stat2,
        *stds,
        *weights,
        *norms[:4],
        sums_embed,
        sums3,
        sums_attn,
        *sums_block,
        arrived,
    )


def input_backward_kernel(class_ref, grad_inner_ref, grad_first_ref, std_in_ref, input_grad_ref):
    cells, channels = grad_inner_ref.shape[1:]
    keep = spread_lanes(validity_mask(class_ref[pl.program_id(0)], cells), channels)
    back = dot_nt(grad_first_ref[0], std_in_ref[...])
    input_grad_ref[0] = (grad_inner_ref[0] + back) * keep


def input_backward(image_class, grad_inner, grad_first, std_in):
    images, cells, channels = grad_inner.shape
    middle = grad_first.shape[2]
    return pl.pallas_call(
        input_backward_kernel,
        out_shape=jax.ShapeDtypeStruct((images, cells, channels), f32),
        grid_spec=pltpu.PrefetchScalarGridSpec(
            num_scalar_prefetch=1,
            grid=(images,),
            in_specs=[
                per_image((cells, channels)),
                per_image((cells, middle)),
                whole((channels, middle)),
            ],
            out_specs=per_image((cells, channels)),
        ),
        compiler_params=pltpu.CompilerParams(vmem_limit_bytes=62 * MIB),
        cost_estimate=cost(2 * images * cells * channels * middle, 12 * MIB),
        name="input_backward",
    )(image_class, grad_inner, grad_first, std_in)


def combine_core_kernel(plane_ref, *refs, arrays, extra):
    mines, others, outs = refs[:arrays], refs[arrays : 2 * arrays], refs[2 * arrays :]
    start = 0
    for mine, other in zip(mines, others):
        size = mine.shape[1]
        for z in range(mine.shape[0] // 4):
            for q in range(4):
                at = 4 * z + lax.bitwise_xor(plane_ref[0], q)
                summed = mine[at].astype(f32) + other[at].astype(f32)
                outs[q][z, start : start + size] = summed.astype(bf16)
        start += size
    if extra:
        vectors = load_split(mines[0].at[PAIRS], 0) + load_split(others[0].at[PAIRS], 0)
        for out in outs:
            out[PAIRS // 4] = jnp.zeros(out.shape[1:], bf16)
            store_split(out.at[PAIRS // 4], 0, vectors)


def combine_core(plane, mines, others, extra):
    arrays = len(mines)
    depth = PAIRS // 4
    steps = 1 if extra else depth
    out_shape = (sum(item.shape[1] for item in mines),) + mines[0].shape[2:]
    in_spec = lambda item: pl.BlockSpec(
        (item.shape[0] // steps,) + item.shape[1:], lambda step, *_: (step, 0, 0, 0)
    )
    out_spec = pl.BlockSpec(((depth + extra) // steps,) + out_shape, lambda step, *_: (step, 0, 0, 0))
    size = sum(item.size for item in mines)
    return pl.pallas_call(
        lambda *refs: combine_core_kernel(*refs, arrays=arrays, extra=extra),
        out_shape=[jax.ShapeDtypeStruct((depth + extra,) + out_shape, bf16)] * 4,
        grid_spec=pltpu.PrefetchScalarGridSpec(
            num_scalar_prefetch=1,
            grid=(steps,),
            in_specs=[in_spec(item) for item in mines] * 2,
            out_specs=[out_spec] * 4,
        ),
        compiler_params=pltpu.CompilerParams(vmem_limit_bytes=62 * MIB),
        cost_estimate=cost(size, 6 * size),
        name="combine_core",
    )(plane, *mines, *others)


def split_two_kernel(bits_ref, *refs, modes):
    count = len(modes)
    outs = refs[2 * count :]
    for k, (inner, bit) in enumerate(modes):
        left, right = refs[2 * k], refs[2 * k + 1]
        for at in range(left.shape[0] // 2):
            base = at // inner * 2 * inner + at % inner
            for q in range(2):
                here = base + inner * lax.bitwise_xor(bits_ref[bit], q)
                summed = left[here].astype(f32) + right[here].astype(f32)
                outs[2 * k + q][at] = summed.astype(bf16)


def split_two(bits, pairs, modes, steps):
    flat = [item for pair in pairs for item in pair]
    spec = lambda shape: pl.BlockSpec(
        (shape[0] // steps,) + shape[1:], lambda step, *_: (step, 0, 0, 0)
    )
    half = lambda item: (item.shape[0] // 2,) + item.shape[1:]
    outs = [jax.ShapeDtypeStruct(half(pair[0]), bf16) for pair in pairs for _ in range(2)]
    size = sum(item.size for item in flat)
    return pl.pallas_call(
        lambda *refs: split_two_kernel(*refs, modes=modes),
        out_shape=outs,
        grid_spec=pltpu.PrefetchScalarGridSpec(
            num_scalar_prefetch=1,
            grid=(steps,),
            in_specs=[spec(item.shape) for item in flat],
            out_specs=[spec(item.shape) for item in outs],
        ),
        compiler_params=pltpu.CompilerParams(vmem_limit_bytes=62 * MIB),
        cost_estimate=cost(size, 3 * size),
        name="split_two",
    )(bits, *flat)


def split_merged_kernel(bits_ref, *refs, bit):
    outs = refs[-2:]
    start = 0
    for k in range(len(refs) // 2 - 1):
        left, right = refs[2 * k], refs[2 * k + 1]
        size = left.shape[1]
        for at in range(left.shape[0] // 2):
            for q in range(2):
                here = 2 * at + lax.bitwise_xor(bits_ref[bit], q)
                summed = left[here].astype(f32) + right[here].astype(f32)
                outs[q][at, start : start + size] = summed.astype(bf16)
        start += size


def split_merged(bits, pairs, bit):
    flat = [item for pair in pairs for item in pair]
    shape = (flat[0].shape[0] // 2, sum(pair[0].shape[1] for pair in pairs)) + flat[0].shape[2:]
    size = sum(item.size for item in flat)
    return pl.pallas_call(
        lambda *refs: split_merged_kernel(*refs, bit=bit),
        out_shape=[jax.ShapeDtypeStruct(shape, bf16)] * 2,
        grid_spec=pltpu.PrefetchScalarGridSpec(
            num_scalar_prefetch=1,
            grid=(1,),
            in_specs=[whole(item.shape) for item in flat],
            out_specs=[whole(shape)] * 2,
        ),
        compiler_params=pltpu.CompilerParams(vmem_limit_bytes=62 * MIB),
        cost_estimate=cost(size, 3 * size),
        name="split_merged",
    )(bits, *flat)


def four(values):
    if len(values) == 1:
        return values[0]
    if len(values) == 2:
        return values[0] + values[1]
    return (values[0] + values[1]) + (values[2] + values[3])


def combine_plane_kernel(depth_ref, *refs, extra, beside):
    parts, outs = refs[:4], refs[4 + beside :]
    size = parts[0].shape[1]
    columns = parts[0].shape[3]
    for q in range(4):
        at = lax.bitwise_xor(depth_ref[0], q)
        outs[q][0:size] = four([part[at].astype(f32) for part in parts]).astype(bf16)
        if beside:
            summed = refs[4][at].astype(f32) + refs[5][at].astype(f32)
            start = size + 2 * VECTORS * extra
            for section in range(summed.shape[0]):
                for k in range(summed.shape[2] // columns):
                    outs[q][start] = summed[section, :, k * columns : (k + 1) * columns].astype(bf16)
                    start += 1
    if extra:
        vectors = four([load_split(part.at[PAIRS // 4], 0) for part in parts])
        for out in outs:
            store_split(out, size, vectors)


def combine_plane(depth, parts, extra, beside=()):
    columns = parts[0].shape[3]
    sections = parts[0].shape[1] + 2 * VECTORS * extra
    if beside:
        sections += beside[0].shape[1] * (beside[0].shape[3] // columns)
    shape = (sections,) + parts[0].shape[2:]
    flat = list(parts) + list(beside)
    size = sum(item.size for item in flat)
    return pl.pallas_call(
        lambda *refs: combine_plane_kernel(*refs, extra=extra, beside=len(beside)),
        out_shape=[jax.ShapeDtypeStruct(shape, bf16)] * 4,
        grid_spec=pltpu.PrefetchScalarGridSpec(
            num_scalar_prefetch=1,
            grid=(1,),
            in_specs=[whole(item.shape) for item in flat],
            out_specs=[whole(shape)] * 4,
        ),
        compiler_params=pltpu.CompilerParams(vmem_limit_bytes=62 * MIB),
        cost_estimate=cost(size, 3 * size),
        name="combine_plane",
    )(depth, *flat)


def store_lines(outs, vectors, lines):
    for out, pieces in zip(outs, lines):
        out[...] = jnp.concatenate(
            [vectors[row : row + 1, 0:size] for row, size in pieces], axis=1
        ).reshape(-1)


def line_shapes(lines):
    return [jax.ShapeDtypeStruct((sum(size for _, size in pieces),), f32) for pieces in lines]


def combine_depth_kernel(*refs, batches):
    outs = refs[sum(count for count, _, _, _ in batches) :]
    first = first_out = 0
    for count, places, sizes, lines in batches:
        parts = refs[first : first + count]
        here = outs[first_out : first_out + sizes + len(lines)]
        summed = four([part[...].astype(f32) for part in parts])
        for section, place in enumerate(places):
            if place is None:
                continue
            out, row, column, columns, rows = place
            stride = columns // LANES
            for lane in range(summed.shape[2] // LANES):
                start = row * stride + column // LANES + lane
                here[out][pl.ds(start, rows, stride=stride), :] = summed[
                    section, 0:rows, lane * LANES : (lane + 1) * LANES
                ]
        if lines:
            vectors = four([load_split(part, places.index(None)) for part in parts])
            store_lines(here[sizes:], vectors, lines)
        first += count
        first_out += sizes + len(lines)


def combine_depth(batches):
    flat = [item for parts, _, _, _ in batches for item in parts]
    shapes = []
    for _, _, sizes, lines in batches:
        shapes += [jax.ShapeDtypeStruct((size // LANES, LANES), f32) for size in sizes]
        shapes += line_shapes(lines)
    size = sum(item.size for item in flat)
    known = [(len(parts), places, len(sizes), lines) for parts, places, sizes, lines in batches]
    outs = pl.pallas_call(
        lambda *refs: combine_depth_kernel(*refs, batches=known),
        out_shape=shapes,
        grid=(1,),
        in_specs=[whole(item.shape) for item in flat],
        out_specs=[whole(item.shape) for item in shapes],
        compiler_params=pltpu.CompilerParams(vmem_limit_bytes=62 * MIB),
        cost_estimate=cost(size, 3 * size),
        name="combine_depth",
    )(*flat)
    return [item.reshape(-1) for item in outs]


def permuted(item, distance, devices):
    return lax.ppermute(item, BOTH, [(k, k ^ distance) for k in range(devices)])


class Sums:
    def __init__(self, index, devices):
        self.devices = devices
        self.plane = ((index // 2) % 4).astype(jnp.int32).reshape(1)
        self.depth = (index // 8).astype(jnp.int32).reshape(1)
        self.bits = jnp.stack([index // unit % 2 for unit in (4, 2, 8, 16)]).astype(jnp.int32)

    def spread(self, parts, unit):
        return [parts[0]] + [permuted(parts[q], q * unit, self.devices) for q in (1, 2, 3)]

    def start_core(self, mines, others):
        return mines, [permuted(item, 1, self.devices) for item in others]

    def end_core(self, started, extra=0):
        return combine_core(self.plane, *started, extra)

    def halves(self, pairs, modes, distances, steps):
        outs = split_two(self.bits, pairs, modes, steps)
        return [
            (outs[2 * k], permuted(outs[2 * k + 1], distance, self.devices))
            for k, distance in enumerate(distances)
        ]

    def start_plane(self, parts):
        return self.spread(parts, 2)

    def merged(self, pairs, bit, distance):
        keep, send = split_merged(self.bits, pairs, bit)
        return keep, permuted(send, distance, self.devices)

    def end_plane(self, started, extra=0, beside=()):
        return combine_plane(self.depth, started, extra, beside)

    def start_depth(self, parts):
        return self.spread(parts, 8)


def after(value, *others):
    return lax.optimization_barrier((value,) + others)[0]


def ahead(value, others):
    leaves, tree = jax.tree.flatten(others)
    held = lax.optimization_barrier((value, leaves))
    return jax.tree.unflatten(tree, held[1])


def octets(out, rows, columns, width, offset=0):
    return [
        (out, 8 * part, start, columns, min(8, rows - 8 * part))
        for start in range(0, columns, width)
        for part in range(-(-rows // 8))
    ]


def scattered(mine, other, places, sizes, devices):
    blocks = jnp.stack([mine, other], axis=1).reshape((2 * PAIRS,) + mine.shape[1:])
    return scattered_blocks(blocks, places, sizes, devices)


def scattered_blocks(blocks, places, sizes, devices):
    results = []
    for out, size in sizes:
        chosen = [k for k, place in enumerate(places) if place[0] == out]
        columns = places[chosen[0]][3]
        width = blocks.shape[-1]
        rows = size // columns
        groups = columns // width
        values = blocks[:, chosen[0] : chosen[-1] + 1]
        values = values.reshape(2 * PAIRS, groups, -1, width)[:, :, :rows]
        values = jnp.moveaxis(values, 1, 2).reshape(devices, -1)
        length = values.shape[1]
        padded = -(-length // LANES) * LANES
        values = jnp.pad(values, ((0, 0), (0, padded - length))).reshape(devices, -1, LANES)
        own = lax.psum_scatter(values, BOTH, scatter_dimension=0, tiled=True)
        results.append(own.astype(f32).reshape(-1)[:length])
    return results


def shards(
    stem_input,
    image_class,
    owner,
    conv_in_weight,
    first_gain,
    first_bias,
    conv_mid_weight,
    second_gain,
    second_bias,
    conv_out_weight,
    third_gain,
    third_bias,
    embed_weight,
    embed_bias,
    position_table,
    attn_gain,
    attn_bias,
    joint_weight,
    query_bias,
    value_bias,
    mix_weight,
    mix_bias,
    mlp_gain,
    mlp_bias,
    expand_weight,
    expand_bias,
    shrink_weight,
    shrink_bias,
    cotangent,
):
    sections = lax.axis_size("section")
    devices = sections * lax.axis_size("batch")
    staged = (devices, sections) == (2 * PAIRS, 4)
    index = lax.axis_index(BOTH)
    images, cells, channels = stem_input.shape
    middle = conv_in_weight.shape[1]
    width = embed_weight.shape[1]
    inner = expand_weight.shape[1]
    section_index = lax.axis_index("section")
    mine = lax.dynamic_index_in_dim(owner.reshape(sections, images), section_index, 0, keepdims=False)
    core = ((index % 2) if staged else jnp.zeros((), jnp.int32)).astype(jnp.int32).reshape(1)
    received = lax.all_to_all(cotangent[0], "section", split_axis=0, concat_axis=0, tiled=True)
    norms = (first_gain, first_bias, second_gain, second_bias, third_gain, third_bias)
    weights = (conv_in_weight, conv_mid_weight.reshape(-1, middle), conv_out_weight)
    std_in, std_mid, std_out, first, second, third, stat1, stat2, stat3, stem, tokens = stem_forward(
        image_class, stem_input, *weights, norms, embed_weight, embed_bias, position_table
    )
    normed, query, key, value, log_total, mixed, resid, normed_two = attend_forward(
        image_class,
        tokens,
        attn_gain,
        attn_bias,
        joint_weight,
        query_bias,
        value_bias,
        mix_weight,
        mix_bias,
        mlp_gain,
        mlp_bias,
    )
    (
        outgoing,
        grad_resid,
        grad_mixed,
        shrink_mine,
        shrink_other,
        expand_mine,
        expand_other,
        sums_expand,
        sums_shrink,
        sums_mix,
    ) = feed(
        image_class,
        mine,
        core,
        normed_two,
        resid,
        received,
        expand_weight,
        expand_bias,
        shrink_weight,
        shrink_bias,
        mlp_gain,
        mix_weight,
    )
    sums = Sums(index, devices)
    if staged:
        feed_core = sums.start_core([shrink_mine, expand_mine], [shrink_other, expand_other])
    arrived = lax.all_to_all(outgoing, "section", split_axis=0, concat_axis=0, tiled=True)
    grad_joint0, sums_attend0 = attend_backward(
        0, image_class, query, key, value, log_total, grad_mixed
    )
    if staged:
        feed_core = ahead(grad_joint0, feed_core)
        feed_half = sums.halves(
            list(zip(*feed_core)), ((2, 0), (1, 1)), (4, 2), 4
        )
        grad_mixed = after(grad_mixed, feed_half[0][0])
    grad_joint1, sums_attend1 = attend_backward(
        1, image_class, query, key, value, log_total, grad_mixed
    )
    grad_tokens, joint_mine, joint_other, sums_attn = joint_backward(
        core,
        tokens,
        normed,
        mixed,
        grad_resid,
        grad_joint0,
        grad_joint1,
        attn_gain,
        joint_weight,
    )
    if staged:
        feed_half, arrived, joint_other = ahead(grad_tokens, (feed_half, arrived, joint_other))
        joint_other = after(joint_other, *feed_half[0], *feed_half[1], arrived)
        joint_core = sums.start_core([joint_mine], [joint_other])
        feed_quarter = sums.halves(feed_half, ((1, 1), (1, 0)), (2, 4), 1)
        grad_tokens = after(grad_tokens, feed_quarter[0][0])
    embed_blocks, sums_embed = embed_weights(image_class, grad_tokens, stem)
    if staged:
        embed_own = lax.psum_scatter(embed_blocks, BOTH, scatter_dimension=0, tiled=True)
    if staged:
        joint_core, feed_quarter, grad_tokens = ahead(
            embed_blocks, (joint_core, feed_quarter, grad_tokens)
        )
        joint_parts = sums.end_core(joint_core)
        joint_plane = sums.start_plane(joint_parts)
        feed_eighth = sums.merged(feed_quarter, 2, 8)
        grad_tokens = after(grad_tokens, joint_plane[0], feed_eighth[0])
    grad_inner, grad_third, sums3 = embed_backward(
        image_class,
        grad_tokens,
        stem_input,
        third,
        stat3,
        third_gain,
        third_bias,
        embed_weight,
    )
    if staged:
        joint_plane, feed_eighth = ahead(grad_third, (joint_plane, feed_eighth))
        joint_depth = sums.start_depth(sums.end_plane(joint_plane))
        feed_last = sums.merged([feed_eighth], 3, 16)
        grad_third = after(grad_third, joint_depth[0], feed_last[0])
    grad_first, conv_mine, conv_other, block_output = convs_backward(
        image_class,
        core,
        grad_third,
        stem_input,
        first,
        second,
        stat1,
        stat2,
        (std_in, std_mid, std_out),
        weights,
        norms,
        sums_embed,
        sums3,
        sums_attn,
        (sums_expand, sums_shrink, sums_mix, sums_attend0, sums_attend1),
        arrived,
    )
    block_output = block_output[None]
    if staged:
        feed_last, joint_depth = ahead(grad_first, (feed_last, joint_depth))
        conv_other = after(conv_other, *feed_last, *joint_depth)
        conv_core = sums.start_core([conv_mine], [conv_other])
    input_grad = input_backward(image_class, grad_inner, grad_first, std_in)

    parts = 2 * PAIRS
    shrink_places = octets(0, inner // parts, width, width)
    expand_places = octets(1, width // parts, inner, width)
    feed_sizes = [inner // parts * width] * 2
    joint_places = octets(0, width // parts, 3 * width, width) + octets(1, width // parts, width, width)
    joint_sizes = [3 * width * width // parts, width * width // parts]
    embed_places = octets(0, channels // parts, width, width) + octets(1, cells // parts, width, width)
    embed_sizes = [channels * width // parts, cells * width // parts]
    conv_places = (
        octets(0, channels // parts, middle, middle)
        + octets(1, 9 * middle // parts, middle, middle)
        + octets(2, middle // parts, channels, middle)
    )
    conv_sizes = [
        channels * middle // parts,
        9 * middle * middle // parts,
        middle * channels // parts,
    ]
    stem_lines = []
    row = 0
    for size in [width] * 3 + [middle] * 4 + [channels] * 2 + [inner] + [width] * 6:
        stem_lines.append([(row + k, middle) for k in range(size // middle)])
        row += size // middle
    if staged:
        conv_plane = sums.start_plane(sums.end_core(conv_core, 1))
        grad_shrink, grad_expand, grad_joint, grad_mix = combine_depth(
            [
                ([item[0] for item in feed_last], shrink_places + expand_places, feed_sizes, []),
                (joint_depth, joint_places, joint_sizes, []),
            ]
        )
        conv_plane = ahead((input_grad, grad_shrink), conv_plane)
        last_depth = sums.start_depth(sums.end_plane(conv_plane, 1))
        grad_embed, grad_position, *grads = combine_depth(
            [
                ([embed_own[0]], embed_places, embed_sizes, []),
                (last_depth, conv_places + [None] * (2 * VECTORS), conv_sizes, stem_lines),
            ]
        )
        grad_in, grad_mid, grad_out = grads[:3]
        stem_vectors = grads[3:]
    else:
        (grad_shrink,) = scattered(
            shrink_mine, shrink_other, shrink_places, [(0, feed_sizes[0])], devices
        )
        (grad_expand,) = scattered(
            expand_mine, expand_other, expand_places, [(1, feed_sizes[1])], devices
        )
        grad_joint, grad_mix = scattered(
            joint_mine, joint_other, joint_places, list(enumerate(joint_sizes)), devices
        )
        grad_embed, grad_position = scattered_blocks(
            embed_blocks, embed_places, list(enumerate(embed_sizes)), devices
        )
        rows = conv_mine[PAIRS, :VECTORS].astype(f32) + conv_mine[PAIRS, VECTORS : 2 * VECTORS].astype(f32)
        rows = lax.psum(rows.reshape(-1, middle), BOTH)
        stem_vectors = [rows[pieces[0][0] : pieces[-1][0] + 1].reshape(-1) for pieces in stem_lines]
        conv_mine, conv_other = conv_mine[:PAIRS], conv_other[:PAIRS]
        grad_in, grad_mid, grad_out = scattered(
            conv_mine, conv_other, conv_places, list(enumerate(conv_sizes)), devices
        )
    (
        grad_embed_bias,
        grad_attn_gain,
        grad_attn_bias,
        grad_first_gain,
        grad_first_bias,
        grad_second_gain,
        grad_second_bias,
        grad_third_gain,
        grad_third_bias,
        grad_expand_bias,
        grad_shrink_bias,
        grad_mlp_gain,
        grad_mlp_bias,
        grad_mix_bias,
        grad_query_bias,
        grad_value_bias,
    ) = stem_vectors
    return (
        block_output,
        input_grad,
        grad_in,
        grad_first_gain,
        grad_first_bias,
        grad_mid,
        grad_second_gain,
        grad_second_bias,
        grad_out,
        grad_third_gain,
        grad_third_bias,
        grad_embed,
        grad_embed_bias,
        grad_position,
        grad_attn_gain,
        grad_attn_bias,
        grad_joint,
        grad_query_bias,
        grad_value_bias,
        grad_mix,
        grad_mix_bias,
        grad_mlp_gain,
        grad_mlp_bias,
        grad_expand,
        grad_expand_bias,
        grad_shrink,
        grad_shrink_bias,
    )


def solution(mesh):
    split = P(BOTH)
    images = P(BOTH, None, None)
    slots = P(BOTH, None, None, None)
    full = P()
    in_specs = (images, split, P("batch")) + (full,) * 25 + (slots,)
    out_specs = (
        slots,
        images,
        split,
        full,
        full,
        split,
        full,
        full,
        split,
        full,
        full,
        split,
        full,
        split,
        full,
        full,
        split,
        full,
        full,
        split,
        full,
        full,
        full,
        split,
        full,
        split,
        full,
    )
    return jax.shard_map(shards, mesh=mesh, in_specs=in_specs, out_specs=out_specs, check_vma=False)
```

```python
import jax
import jax.numpy as jnp
from jax import lax
from jax.experimental import pallas as pl
from jax.experimental.pallas import tpu as pltpu
from jax.sharding import PartitionSpec as P

HEADS = 12
GROUPS = 32
SIDE = 24
SIDE_SMALL = 14
LANES = 128
MIB = 1024 * 1024
BOTH = ("batch", "section")

f32 = jnp.float32
bf16 = jnp.bfloat16


def dot_nn(left, right):
    return jnp.dot(left, right, preferred_element_type=f32)


def dot_tn(left, right):
    return lax.dot_general(left, right, (((0,), (0,)), ((), ())), preferred_element_type=f32)


def dot_nt(left, right):
    return lax.dot_general(left, right, (((1,), (1,)), ((), ())), preferred_element_type=f32)


def fold(values):
    rows, columns = values.shape
    return jnp.sum(values.reshape(rows // 8, 8, columns), axis=0)


def total(values):
    return jnp.sum(values, axis=0, keepdims=True)


def line(ref):
    return ref[...].reshape(1, -1)


def spread_lanes(mask, columns):
    return jnp.concatenate([mask] * (columns // LANES), axis=1)


def cdf_pdf(values):
    bell = jnp.exp(-0.5 * (values * values))
    t = 1.0 / (1.0 + 0.23164189 * jnp.abs(values))
    tail = (
        ((((0.5307027145 * t - 0.7265760135) * t + 0.7107068705) * t - 0.142248368) * t + 0.127414796)
        * t
        * bell
    )
    return jnp.where(values < 0.0, tail, 1.0 - tail), bell * 0.3989422804014327


def group_total(row, per_group):
    channels = row.shape[1]
    rows = jnp.broadcast_to(row, (8, channels))
    lane = lax.broadcasted_iota(jnp.int32, (8, LANES), 1)
    parts = []
    for k in range(channels // LANES):
        part = rows[:, k * LANES : (k + 1) * LANES]
        step = 1
        while step < per_group:
            up = pltpu.roll(part, LANES - step, 1)
            down = pltpu.roll(part, step, 1)
            part = part + jnp.where((lane & step) == 0, up, down)
            step *= 2
        parts.append(part)
    return jnp.concatenate(parts, axis=1)[0:1]


def cell_grid(cells):
    cell = lax.broadcasted_iota(jnp.int32, (cells, LANES), 0).astype(f32)
    row = jnp.floor((cell + 0.5) * (1.0 / SIDE))
    return row, cell - row * SIDE


def validity_mask(image_class, cells):
    row, column = cell_grid(cells)
    corner = jnp.where((row < SIDE_SMALL) & (column < SIDE_SMALL), 1.0, 0.0)
    return jnp.where(image_class == 1, 1.0, corner)


def valid_count(image_class):
    return jnp.where(image_class == 1, float(SIDE * SIDE), float(SIDE_SMALL * SIDE_SMALL))


def rows_at(index, size):
    return pl.ds(pl.multiple_of(index * size, size), size)


def fill_columns(grid_value, padded, columns, sign):
    cells, channels = grid_value.shape
    _, column = cell_grid(cells)
    has_left = spread_lanes(jnp.where(column > 0.5, 1.0, 0.0), channels)
    has_right = spread_lanes(jnp.where(column < SIDE - 1.5, 1.0, 0.0), channels)
    zeros = jnp.zeros((SIDE, channels), f32)
    shifted = (
        pltpu.roll(grid_value, 1, 0) * has_left,
        grid_value,
        pltpu.roll(grid_value, cells - 1, 0) * has_right,
    )
    for k in range(3):
        padded[k, 0:SIDE, :] = zeros
        padded[k, SIDE + cells : 2 * SIDE + cells, :] = zeros
        padded[k, SIDE : SIDE + cells, :] = shifted[k]
    for row_shift in range(3):
        for column_shift in range(3):
            tap = row_shift * 3 + column_shift
            down = row_shift if sign > 0 else 2 - row_shift
            across = column_shift if sign > 0 else 2 - column_shift
            columns[:, tap * channels : (tap + 1) * channels] = padded[
                across, down * SIDE : down * SIDE + cells, :
            ].astype(bf16)


def standardized(weight):
    rows = weight.shape[0]
    centred = weight - total(weight) * (1.0 / rows)
    spread = total(centred * centred) * (1.0 / rows)
    scale = lax.rsqrt(spread + 1e-05)
    return centred * scale, scale


def standardize_back(weight, grad):
    rows = weight.shape[0]
    normal, scale = standardized(weight)
    grad_mean = total(grad) * (1.0 / rows)
    inner = total(grad * normal) * (1.0 / rows)
    return scale * (grad - grad_mean - normal * inner)


PAIRS = 16
VECTORS = 7


def store_pairs(values, mine_ref, other_ref, core):
    pairs, parts = mine_ref.shape[:2]
    for pair in range(pairs):
        for ref, side in ((mine_ref, core), (other_ref, 1 - core)):
            at = pl.multiple_of((2 * pair + side) * parts * 8, 8)
            ref[pair] = sections_of(values[pl.ds(at, parts * 8), :])


def store_split(ref, start, values):
    high = values.astype(bf16)
    low = (values - high.astype(f32)).astype(bf16)
    shape = (VECTORS, 8, values.shape[-1])
    ref[start : start + VECTORS] = high.astype(f32).reshape(shape).astype(bf16)
    ref[start + VECTORS : start + 2 * VECTORS] = low.astype(f32).reshape(shape).astype(bf16)


def load_split(ref, start):
    high = ref[start : start + VECTORS].astype(f32)
    low = ref[start + VECTORS : start + 2 * VECTORS].astype(f32)
    rows = high + low
    return rows.reshape(VECTORS * 8, rows.shape[-1])


def sections_of(values):
    rows, columns = values.shape
    return values.reshape(rows // 8, 8, columns).astype(bf16)


def stem_forward_kernel(
    class_ref,
    x_ref,
    w_in_ref,
    w_mid_ref,
    w_out_ref,
    gain1_ref,
    bias1_ref,
    gain2_ref,
    bias2_ref,
    gain3_ref,
    bias3_ref,
    embed_ref,
    embed_bias_ref,
    position_ref,
    std_in_ref,
    std_mid_ref,
    std_out_ref,
    first_ref,
    second_ref,
    third_ref,
    stat1_ref,
    stat2_ref,
    stat3_ref,
    stem_ref,
    tokens_ref,
    mask,
    padded,
    columns,
    act_two,
):
    image = pl.program_id(0)
    cells = x_ref.shape[1]
    channels = x_ref.shape[2]
    middle = w_in_ref.shape[1]

    @pl.when(image == 0)
    def _():
        std_in_ref[...] = standardized(w_in_ref[...].astype(f32))[0].astype(bf16)
        std_mid_ref[...] = standardized(w_mid_ref[...].astype(f32))[0].astype(bf16)
        std_out_ref[...] = standardized(w_out_ref[...].astype(f32))[0].astype(bf16)

    image_class = class_ref[image]
    mask[...] = validity_mask(image_class, cells)
    count = valid_count(image_class)
    chunk = cells
    steps = cells // chunk

    def stats(values_ref, stat_ref, sums):
        width = values_ref.shape[2]
        per_group = width // GROUPS
        inverse = 1.0 / (count * per_group)
        centre = group_total(total(sums), per_group) * inverse

        def one(step, carry):
            rows = rows_at(step, chunk)
            centred = (values_ref[0, rows, :] - centre) * spread_lanes(mask[rows, :], width)
            return carry + fold(centred * centred)

        squares = lax.fori_loop(0, steps, one, jnp.zeros((8, width), f32))
        scale = lax.rsqrt(group_total(total(squares), per_group) * inverse + 1e-05)
        stat_ref[0, 0:1, :] = centre
        stat_ref[0, 1:2, :] = scale
        return centre, scale

    def first_step(step, carry):
        rows = rows_at(step, chunk)
        low = (x_ref[0, rows, :] * spread_lanes(mask[rows, :], channels)).astype(bf16)
        values = dot_nn(low, std_in_ref[...])
        first_ref[0, rows, :] = values
        return carry + fold(values)

    sums = lax.fori_loop(0, steps, first_step, jnp.zeros((8, middle), f32))
    centre, scale = stats(first_ref, stat1_ref, sums)
    gain = scale * line(gain1_ref)
    normed = (first_ref[0] - centre) * gain + line(bias1_ref)
    act = normed * cdf_pdf(normed)[0] * spread_lanes(mask[...], middle)
    fill_columns(act, padded, columns, 1)

    def second_step(step, carry):
        rows = rows_at(step, chunk)
        values = dot_nn(columns[rows, :], std_mid_ref[...])
        second_ref[0, rows, :] = values
        return carry + fold(values * spread_lanes(mask[rows, :], middle))

    sums = lax.fori_loop(0, steps, second_step, jnp.zeros((8, middle), f32))
    centre, scale = stats(second_ref, stat2_ref, sums)
    gain = scale * line(gain2_ref)
    normed = (second_ref[0] - centre) * gain + line(bias2_ref)
    act_two[...] = (normed * cdf_pdf(normed)[0] * spread_lanes(mask[...], middle)).astype(bf16)

    def third_step(step, carry):
        rows = rows_at(step, chunk)
        values = dot_nn(act_two[rows, :], std_out_ref[...])
        third_ref[0, rows, :] = values
        return carry + fold(values)

    sums = lax.fori_loop(0, steps, third_step, jnp.zeros((8, channels), f32))
    centre, scale = stats(third_ref, stat3_ref, sums)
    gain = scale * line(gain3_ref)

    @pl.loop(0, steps)
    def _(step):
        rows = rows_at(step, chunk)
        keep = mask[rows, :]
        keep_wide = spread_lanes(keep, channels)
        argument = (
            x_ref[0, rows, :] * keep_wide + (third_ref[0, rows, :] - centre) * gain + line(bias3_ref)
        )
        stem = (argument * cdf_pdf(argument)[0] * keep_wide).astype(bf16)
        stem_ref[0, rows, :] = stem
        values = dot_nn(stem, embed_ref[...]) + line(embed_bias_ref) + position_ref[rows, :].astype(f32)
        tokens_ref[0, rows, :] = (values * spread_lanes(keep, values.shape[1])).astype(bf16)


def cost(flops, moved):
    return pl.CostEstimate(flops=flops, bytes_accessed=moved, transcendentals=0)


def whole(shape):
    return pl.BlockSpec(shape, lambda *_: (0,) * len(shape))


def per_image(shape):
    return pl.BlockSpec((1,) + shape, lambda image, *_: (image,) + (0,) * len(shape))


def stem_forward(image_class, x, w_in, w_mid, w_out, norms, embed, embed_bias, position):
    images, cells, channels = x.shape
    middle = w_in.shape[1]
    width = embed.shape[1]
    row = lambda size: whole((size,))
    return pl.pallas_call(
        stem_forward_kernel,
        out_shape=(
            jax.ShapeDtypeStruct((channels, middle), bf16),
            jax.ShapeDtypeStruct((9 * middle, middle), bf16),
            jax.ShapeDtypeStruct((middle, channels), bf16),
            jax.ShapeDtypeStruct((images, cells, middle), f32),
            jax.ShapeDtypeStruct((images, cells, middle), f32),
            jax.ShapeDtypeStruct((images, cells, channels), f32),
            jax.ShapeDtypeStruct((images, 8, middle), f32),
            jax.ShapeDtypeStruct((images, 8, middle), f32),
            jax.ShapeDtypeStruct((images, 8, channels), f32),
            jax.ShapeDtypeStruct((images, cells, channels), bf16),
            jax.ShapeDtypeStruct((images, cells, width), bf16),
        ),
        grid_spec=pltpu.PrefetchScalarGridSpec(
            num_scalar_prefetch=1,
            grid=(images,),
            in_specs=[
                per_image((cells, channels)),
                whole((channels, middle)),
                whole((9 * middle, middle)),
                whole((middle, channels)),
                row(middle),
                row(middle),
                row(middle),
                row(middle),
                row(channels),
                row(channels),
                whole((channels, width)),
                row(width),
                whole((cells, width)),
            ],
            out_specs=[
                whole((channels, middle)),
                whole((9 * middle, middle)),
                whole((middle, channels)),
                per_image((cells, middle)),
                per_image((cells, middle)),
                per_image((cells, channels)),
                per_image((8, middle)),
                per_image((8, middle)),
                per_image((8, channels)),
                per_image((cells, channels)),
                per_image((cells, width)),
            ],
            scratch_shapes=[
                pltpu.VMEM((cells, LANES), f32),
                pltpu.VMEM((3, cells + 2 * SIDE, middle), f32),
                pltpu.VMEM((cells, 9 * middle), bf16),
                pltpu.VMEM((cells, middle), bf16),
            ],
        ),
        compiler_params=pltpu.CompilerParams(vmem_limit_bytes=62 * MIB),
        cost_estimate=cost(25_000_000_000, 30 * MIB),
        name="stem_forward",
    )(image_class, x, w_in, w_mid, w_out, *norms, embed, embed_bias, position)


def row_norm(values):
    centre = jnp.mean(values, axis=-1, keepdims=True)
    centred = values - centre
    scale = lax.rsqrt(jnp.mean(centred * centred, axis=-1, keepdims=True) + 1e-06)
    return centred * scale, scale


def attend_forward_kernel(
    class_ref,
    tokens_ref,
    gain1_ref,
    bias1_ref,
    joint_ref,
    query_bias_ref,
    value_bias_ref,
    mix_ref,
    mix_bias_ref,
    gain2_ref,
    bias2_ref,
    normed_ref,
    query_ref,
    key_ref,
    value_ref,
    log_total_ref,
    mixed_ref,
    resid_ref,
    normed_two_ref,
):
    image = pl.program_id(0)
    cells, width = tokens_ref.shape[1:]
    chunk = cells
    steps = cells // chunk
    scale = (width // HEADS) ** -0.5

    @pl.loop(0, steps)
    def _(step):
        rows = rows_at(step, chunk)
        normal, _ = row_norm(tokens_ref[0, rows, :].astype(f32))
        normed_ref[0, rows, :] = (normal * line(gain1_ref) + line(bias1_ref)).astype(bf16)

    block = 256
    query_bias = line(query_bias_ref)
    value_bias = line(value_bias_ref)
    for start in range(0, width, block):
        here = slice(start, start + block)
        later = slice(width + start, width + start + block)
        last = slice(2 * width + start, 2 * width + start + block)
        normed = normed_ref[0]
        query = dot_nn(normed, joint_ref[:, here]) + query_bias[:, here]
        query_ref[0, :, here] = query.astype(bf16)
        key_ref[0, :, here] = dot_nn(normed, joint_ref[:, later]).astype(bf16)
        value = dot_nn(normed, joint_ref[:, last]) + value_bias[:, here]
        value_ref[0, :, here] = value.astype(bf16)

    upper = lax.broadcasted_iota(jnp.int32, (cells, LANES), 1) >= LANES // 2
    key_bias = (validity_mask(class_ref[image], cells) - 1.0) * 1000000000.0
    key_bias = key_bias.astype(bf16)
    lane = lax.broadcasted_iota(jnp.int32, (cells, LANES), 1)

    @pl.loop(0, width // LANES, unroll=True)
    def _(pair):
        lanes = rows_at(pair, LANES)
        query = query_ref[0, :, lanes] * bf16(scale)
        key = key_ref[0, :, lanes]
        value = value_ref[0, :, lanes]
        outs = []
        for half in range(2):
            mine = upper if half else jnp.logical_not(upper)
            spare = lane == (0 if half else LANES // 2)
            scores = dot_nt(
                jnp.where(mine, key, jnp.where(spare, key_bias, bf16(0))),
                jnp.where(spare, bf16(1), query),
            )
            top = jnp.max(scores, axis=0, keepdims=True)
            weights = jnp.exp(scores - top)
            weight_sum = total(weights)
            probs = (weights * (1.0 / weight_sum)).astype(bf16)
            outs.append(dot_tn(probs, value))
            log_total_ref[0, 2 * pair + half] = jnp.broadcast_to(top + jnp.log(weight_sum), (8, cells))
        mixed_ref[0, :, lanes] = jnp.where(upper, outs[1], outs[0]).astype(bf16)

    @pl.loop(0, steps)
    def _(step):
        rows = rows_at(step, chunk)
        resid = (
            tokens_ref[0, rows, :].astype(f32)
            + dot_nn(mixed_ref[0, rows, :], mix_ref[...])
            + line(mix_bias_ref)
        )
        resid_ref[0, rows, :] = resid
        normal, _ = row_norm(resid)
        normed_two_ref[0, rows, :] = (normal * line(gain2_ref) + line(bias2_ref)).astype(bf16)


def attend_forward(
    image_class, tokens, gain1, bias1, joint, query_bias, value_bias, mix, mix_bias, gain2, bias2
):
    images, cells, width = tokens.shape
    row = whole((width,))
    low = jax.ShapeDtypeStruct((images, cells, width), bf16)
    low_spec = per_image((cells, width))
    return pl.pallas_call(
        attend_forward_kernel,
        out_shape=(
            low,
            low,
            low,
            low,
            jax.ShapeDtypeStruct((images, HEADS, 8, cells), f32),
            low,
            jax.ShapeDtypeStruct((images, cells, width), f32),
            low,
        ),
        grid_spec=pltpu.PrefetchScalarGridSpec(
            num_scalar_prefetch=1,
            grid=(images,),
            in_specs=[
                low_spec,
                row,
                row,
                whole((width, 3 * width)),
                row,
                row,
                whole((width, width)),
                row,
                row,
                row,
            ],
            out_specs=[
                low_spec,
                low_spec,
                low_spec,
                low_spec,
                per_image((HEADS, 8, cells)),
                low_spec,
                low_spec,
                low_spec,
            ],
        ),
        compiler_params=pltpu.CompilerParams(vmem_limit_bytes=62 * MIB),
        cost_estimate=cost(35_000_000_000, 30 * MIB),
        name="attend_forward",
    )(image_class, tokens, gain1, bias1, joint, query_bias, value_bias, mix, mix_bias, gain2, bias2)


def feed_kernel(
    class_ref,
    mine_ref,
    core_ref,
    normed_ref,
    cotangent0_ref,
    cotangent1_ref,
    expand_ref,
    expand_bias_ref,
    shrink_ref,
    shrink_bias_ref,
    gain2_ref,
    resid_ref,
    mix_ref,
    output_ref,
    grad_resid_ref,
    grad_mixed_ref,
    shrink_mine_ref,
    shrink_other_ref,
    expand_mine_ref,
    expand_other_ref,
    grad_expand_bias_ref,
    grad_shrink_bias_ref,
    sums_ref,
    sent,
    result,
    grad_normed,
    hidden,
    grad_pre,
    normed_turned,
    shrink_total,
    expand_total,
    biases,
    resid,
    mix,
    empty,
    in_sems,
    out_sems,
    empty_sems,
):
    step = pl.program_id(0)
    last = pl.num_programs(0) - 1
    images, cells, width = normed_ref.shape
    slots = output_ref.shape[0]
    block = expand_ref.shape[1]
    part = cells // 2
    loads = [
        pltpu.make_async_copy(resid_ref, resid, in_sems.at[0]),
        pltpu.make_async_copy(mix_ref, mix, in_sems.at[1]),
    ]

    def image_rows(image):
        return slice(image * cells, (image + 1) * cells)

    def each_empty(act):
        for slot in range(slots):
            taken = mine_ref[0] == slot
            for image in range(1, images):
                taken = taken | (mine_ref[image] == slot)

            @pl.when(jnp.logical_not(taken))
            def _():
                act(pltpu.make_async_copy(empty, output_ref.at[slot], empty_sems.at[slot]))

    @pl.when(step == 0)
    def _():
        empty[...] = jnp.zeros_like(empty)
        each_empty(lambda copy: copy.start())
        for copy in loads:
            copy.start()
        sums = jnp.zeros((8, width), f32)
        for image, ref in enumerate((cotangent0_ref, cotangent1_ref)):
            keep = spread_lanes(validity_mask(class_ref[image], cells), width)
            grad = ref[0].astype(f32) * keep
            sent[image_rows(image), :] = grad.astype(bf16)
            sums = sums + fold(grad)
        grad_shrink_bias_ref[...] = sums
        result[...] = jnp.zeros_like(result)
        grad_normed[...] = jnp.zeros_like(grad_normed)
        every = line(expand_bias_ref)
        for k in range(biases.shape[0]):
            biases[k : k + 1, :] = every[:, k * block : (k + 1) * block]

    bias_sums = jnp.zeros((8, block), f32)
    for image in range(images):
        for piece in range(cells // part):
            local = slice(piece * part, (piece + 1) * part)
            rows = slice(image * cells + piece * part, image * cells + (piece + 1) * part)
            pre = dot_nn(normed_ref[image, local, :], expand_ref[...]) + biases[pl.ds(step, 1), :]
            back = dot_nt(sent[rows, :], shrink_ref[...])
            cdf, pdf = cdf_pdf(pre)
            low = (pre * cdf).astype(bf16)
            hidden[rows, :] = low
            grad = back * (cdf + pre * pdf)
            bias_sums = bias_sums + fold(grad)
            grad_low = grad.astype(bf16)
            grad_pre[rows, :] = grad_low
            result[rows, :] += dot_nn(low, shrink_ref[...])
            grad_normed[rows, :] += dot_nt(grad_low, expand_ref[...])
    grad_expand_bias_ref[...] = bias_sums
    shrink_total[...] = dot_tn(hidden[...], sent[...])
    expand_total[...] = dot_tn(normed_ref[...].reshape(images * cells, width), grad_pre[...])
    core = core_ref[0]
    store_pairs(shrink_total, shrink_mine_ref, shrink_other_ref, core)
    store_pairs(expand_total, expand_mine_ref, expand_other_ref, core)

    @pl.when(step == last)
    def _():
        for copy in loads:
            copy.wait()
        stores = []
        for image in range(images):
            rows = image_rows(image)
            keep = spread_lanes(validity_mask(class_ref[image], cells), width)
            out = (resid[image] + result[rows, :] + line(shrink_bias_ref)) * keep
            hidden[rows, :] = out.astype(bf16)
            stores.append(
                pltpu.make_async_copy(
                    hidden.at[pl.ds(image * cells, cells)],
                    output_ref.at[mine_ref[image]],
                    out_sems.at[3 * image],
                )
            )
            stores[-1].start()
        sums = [jnp.zeros((8, width), f32)] * 3
        for image in range(images):
            rows = image_rows(image)
            normal, row_scale = row_norm(resid[image])
            grad = grad_normed[rows, :]
            sums[0] = sums[0] + fold(grad * normal)
            sums[1] = sums[1] + fold(grad)
            grad = sent[rows, :].astype(f32) + row_norm_back(grad, normal, row_scale, line(gain2_ref))
            sums[2] = sums[2] + fold(grad)
            resid[image] = grad
            stores.append(
                pltpu.make_async_copy(resid.at[image], grad_resid_ref.at[image], out_sems.at[3 * image + 1])
            )
            stores[-1].start()
            grad_pre[rows, :] = dot_nt(grad.astype(bf16), mix[...]).astype(bf16)
            stores.append(
                pltpu.make_async_copy(
                    grad_pre.at[pl.ds(image * cells, cells)],
                    grad_mixed_ref.at[image],
                    out_sems.at[3 * image + 2],
                )
            )
            stores[-1].start()
        for k in range(3):
            sums_ref[k] = sums[k]
        each_empty(lambda copy: copy.wait())
        for copy in stores:
            copy.wait()


def feed(
    image_class, mine, core, normed, resid, cotangent, expand, expand_bias, shrink, shrink_bias, gain2, mix
):
    images, cells, width = normed.shape
    inner = expand.shape[1]
    slots = cotangent.shape[0]
    block = width
    rows = images * cells
    shrink_size = inner // (2 * PAIRS)
    pairs = block // (2 * shrink_size)
    expand_size = width // (2 * PAIRS)
    shrink_half = jax.ShapeDtypeStruct((PAIRS, shrink_size // 8, 8, width), bf16)
    expand_half = jax.ShapeDtypeStruct((PAIRS, expand_size // 8 * (inner // width), 8, width), bf16)
    shrink_spec = pl.BlockSpec((pairs, shrink_size // 8, 8, width), lambda step, *_: (step, 0, 0, 0))
    expand_spec = pl.BlockSpec((PAIRS, expand_size // 8, 8, block), lambda step, *_: (0, step, 0, 0))
    anywhere = pl.BlockSpec(memory_space=pl.ANY)
    return pl.pallas_call(
        feed_kernel,
        out_shape=(
            jax.ShapeDtypeStruct((slots, cells, width), bf16),
            jax.ShapeDtypeStruct((images, cells, width), f32),
            jax.ShapeDtypeStruct((images, cells, width), bf16),
            shrink_half,
            shrink_half,
            expand_half,
            expand_half,
            jax.ShapeDtypeStruct((8, inner), f32),
            jax.ShapeDtypeStruct((8, width), f32),
            jax.ShapeDtypeStruct((3, 8, width), f32),
        ),
        grid_spec=pltpu.PrefetchScalarGridSpec(
            num_scalar_prefetch=3,
            grid=(inner // block,),
            in_specs=[
                whole((images, cells, width)),
                pl.BlockSpec((1, cells, width), lambda step, classes, mine, core: (mine[0], 0, 0)),
                pl.BlockSpec((1, cells, width), lambda step, classes, mine, core: (mine[1], 0, 0)),
                pl.BlockSpec((width, block), lambda step, *_: (0, step)),
                whole((inner,)),
                pl.BlockSpec((block, width), lambda step, *_: (step, 0)),
                whole((width,)),
                whole((width,)),
                anywhere,
                anywhere,
            ],
            out_specs=[
                anywhere,
                anywhere,
                anywhere,
                shrink_spec,
                shrink_spec,
                expand_spec,
                expand_spec,
                pl.BlockSpec((8, block), lambda step, *_: (0, step)),
                whole((8, width)),
                whole((3, 8, width)),
            ],
            scratch_shapes=[
                pltpu.VMEM((rows, width), bf16),
                pltpu.VMEM((rows, width), f32),
                pltpu.VMEM((rows, width), f32),
                pltpu.VMEM((rows, block), bf16),
                pltpu.VMEM((rows, block), bf16),
                pltpu.VMEM((width, rows), bf16),
                pltpu.VMEM((block, width), f32),
                pltpu.VMEM((width, block), f32),
                pltpu.VMEM((inner // block, block), f32),
                pltpu.VMEM((images, cells, width), f32),
                pltpu.VMEM((width, width), bf16),
                pltpu.VMEM((cells, width), bf16),
                pltpu.SemaphoreType.DMA((2,)),
                pltpu.SemaphoreType.DMA((3 * images,)),
                pltpu.SemaphoreType.DMA((slots,)),
            ],
        ),
        compiler_params=pltpu.CompilerParams(vmem_limit_bytes=62 * MIB),
        cost_estimate=cost(14 * rows * width * inner, 40 * MIB),
        name="feed",
    )(
        image_class,
        mine,
        core,
        normed,
        cotangent,
        cotangent,
        expand,
        expand_bias,
        shrink,
        shrink_bias,
        gain2,
        resid,
        mix,
    )


def row_norm_back(grad, normal, scale, gain):
    inner = grad * gain
    mean = jnp.mean(inner, axis=-1, keepdims=True)
    cross = jnp.mean(inner * normal, axis=-1, keepdims=True)
    return scale * (inner - mean - normal * cross)


def attend_backward_kernel(
    class_ref,
    query_ref,
    key_ref,
    value_ref,
    log_total_ref,
    grad_mixed_ref,
    grad_joint_ref,
    sums_ref,
    *,
    image,
):
    cells, width = query_ref.shape[1:]
    scale = (width // HEADS) ** -0.5

    upper = lax.broadcasted_iota(jnp.int32, (cells, LANES), 1) >= LANES // 2
    key_bias = (validity_mask(class_ref[image], cells) - 1.0) * 1000000000.0
    key_bias = key_bias.astype(bf16)
    lane = lax.broadcasted_iota(jnp.int32, (cells, LANES), 1)

    @pl.loop(0, width // LANES, unroll=True)
    def _(pair):
        lanes = rows_at(pair, LANES)
        query = query_ref[0, :, lanes] * bf16(scale)
        key = key_ref[0, :, lanes]
        value = value_ref[0, :, lanes]
        grad_out = grad_mixed_ref[0, :, lanes]
        grads = []
        for half in range(2):
            mine = upper if half else jnp.logical_not(upper)
            spare = lane == (0 if half else LANES // 2)
            scores = dot_nt(
                jnp.where(mine, key, jnp.where(spare, key_bias, bf16(0))),
                jnp.where(spare, bf16(1), query),
            )
            log_total = log_total_ref[0, 2 * pair + half, 0:1, :]
            probs = jnp.exp(scores - log_total)
            grad_probs = dot_nt(jnp.where(mine, value, bf16(0)), grad_out)
            weighted = probs * grad_probs
            grad_scores = (weighted - probs * total(weighted)).astype(bf16)
            grad_value = dot_nn(probs.astype(bf16), grad_out)
            grad_key = dot_nn(grad_scores, query)
            grad_query = dot_tn(grad_scores, key) * scale
            grads.append((grad_query, grad_key, grad_value))
        for k in range(3):
            grad = jnp.where(upper, grads[1][k], grads[0][k])
            if k != 1:
                sums_ref[k // 2, :, lanes] = fold(grad)
            where = pl.ds(pl.multiple_of(k * width + pair * LANES, LANES), LANES)
            grad_joint_ref[0, :, where] = grad.astype(bf16)


def attend_backward(image, image_class, query, key, value, log_total, grad_mixed):
    images, cells, width = query.shape
    own = lambda shape: pl.BlockSpec((1,) + shape, lambda *_: (image,) + (0,) * len(shape))
    rows = own((cells, width))
    return pl.pallas_call(
        lambda *refs: attend_backward_kernel(*refs, image=image),
        out_shape=(
            jax.ShapeDtypeStruct((1, cells, 3 * width), bf16),
            jax.ShapeDtypeStruct((2, 8, width), f32),
        ),
        grid_spec=pltpu.PrefetchScalarGridSpec(
            num_scalar_prefetch=1,
            grid=(1,),
            in_specs=[rows, rows, rows, own((HEADS, 8, cells)), rows],
            out_specs=[whole((1, cells, 3 * width)), whole((2, 8, width))],
        ),
        compiler_params=pltpu.CompilerParams(vmem_limit_bytes=62 * MIB),
        cost_estimate=cost(40 * cells * cells * width, 6 * MIB),
        name="attend_backward",
    )(image_class, query, key, value, log_total, grad_mixed)


def joint_backward_kernel(
    core_ref,
    normed_ref,
    grad_joint0_ref,
    grad_joint1_ref,
    joint_ref,
    gain1_ref,
    tokens_ref,
    mixed_ref,
    grad_resid_ref,
    grad_tokens_ref,
    mine_ref,
    other_ref,
    sums_ref,
    grad_joint,
    weight_total,
    grad_normed,
    tokens,
    mixed,
    grad_resid,
    sems,
):
    step = pl.program_id(0)
    last = pl.num_programs(0) - 1
    images, cells, width = normed_ref.shape
    rows = images * cells
    loads = [
        pltpu.make_async_copy(mixed_ref, mixed, sems.at[0]),
        pltpu.make_async_copy(grad_resid_ref, grad_resid, sems.at[1]),
        pltpu.make_async_copy(tokens_ref, tokens, sems.at[2]),
    ]

    @pl.when(step == 0)
    def _():
        for copy in loads:
            copy.start()
        grad_normed[...] = jnp.zeros_like(grad_normed)

    @pl.when(step < last)
    def _():
        grad_joint[0:cells, :] = grad_joint0_ref[0]
        grad_joint[cells:rows, :] = grad_joint1_ref[0]
        weight_total[...] = dot_tn(normed_ref[...].reshape(rows, width), grad_joint[...])
        grad_normed[...] += dot_nt(grad_joint[...], joint_ref[...])

    @pl.when(step == last)
    def _():
        for copy in loads:
            copy.wait()
        low = grad_resid[...].reshape(rows, width).astype(bf16)
        weight_total[...] = dot_tn(mixed[...].reshape(rows, width), low)
        sums = [jnp.zeros((8, width), f32)] * 2
        for image in range(images):
            at = slice(image * cells, (image + 1) * cells)
            normal, row_scale = row_norm(tokens[image].astype(f32))
            grad = grad_normed[at, :]
            sums[0] = sums[0] + fold(grad * normal)
            sums[1] = sums[1] + fold(grad)
            back = row_norm_back(grad, normal, row_scale, line(gain1_ref))
            grad_tokens_ref[image] = (grad_resid[image] + back).astype(bf16)
        sums_ref[0] = sums[0]
        sums_ref[1] = sums[1]

    store_pairs(weight_total, mine_ref, other_ref, core_ref[0])


def joint_backward(
    core,
    tokens,
    normed,
    mixed,
    grad_resid,
    grad_joint0,
    grad_joint1,
    gain1,
    joint,
):
    images, cells, width = tokens.shape
    size = width // (2 * PAIRS)
    half = (PAIRS, 4 * size // 8, 8, width)
    half_spec = pl.BlockSpec((PAIRS, size // 8, 8, width), lambda step, *_: (0, step, 0, 0))
    column = lambda step, *_: (0, 0, jnp.minimum(step, 2))
    anywhere = pl.BlockSpec(memory_space=pl.ANY)
    return pl.pallas_call(
        joint_backward_kernel,
        out_shape=(
            jax.ShapeDtypeStruct((images, cells, width), bf16),
            jax.ShapeDtypeStruct(half, bf16),
            jax.ShapeDtypeStruct(half, bf16),
            jax.ShapeDtypeStruct((2, 8, width), f32),
        ),
        grid_spec=pltpu.PrefetchScalarGridSpec(
            num_scalar_prefetch=1,
            grid=(4,),
            in_specs=[
                whole((images, cells, width)),
                pl.BlockSpec((1, cells, width), column),
                pl.BlockSpec((1, cells, width), column),
                pl.BlockSpec((width, width), lambda step, *_: (0, jnp.minimum(step, 2))),
                whole((width,)),
                anywhere,
                anywhere,
                anywhere,
            ],
            out_specs=[
                whole((images, cells, width)),
                half_spec,
                half_spec,
                whole((2, 8, width)),
            ],
            scratch_shapes=[
                pltpu.VMEM((images * cells, width), bf16),
                pltpu.VMEM((width, width), f32),
                pltpu.VMEM((images * cells, width), f32),
                pltpu.VMEM((images, cells, width), bf16),
                pltpu.VMEM((images, cells, width), bf16),
                pltpu.VMEM((images, cells, width), f32),
                pltpu.SemaphoreType.DMA((3,)),
            ],
        ),
        compiler_params=pltpu.CompilerParams(vmem_limit_bytes=62 * MIB),
        cost_estimate=cost(14 * images * cells * width * width, 25 * MIB),
        name="joint_backward",
    )(
        core,
        normed,
        grad_joint0,
        grad_joint1,
        joint,
        gain1,
        tokens,
        mixed,
        grad_resid,
    )


def norm_means(sums, gain, per_group, count):
    inverse = 1.0 / (count * per_group)
    return [group_total(total(item) * gain, per_group) * inverse for item in sums]


def embed_weights_kernel(
    class_ref,
    grad_tokens_ref,
    stem_ref,
    blocks_ref,
    sums_ref,
    grad_masked,
    weight_total,
    position_total,
):
    images, cells, width = grad_tokens_ref.shape
    channels = stem_ref.shape[2]
    sums = jnp.zeros((8, width), f32)
    position = jnp.zeros((cells, width), f32)
    for image in range(images):
        keep = spread_lanes(validity_mask(class_ref[image], cells), width)
        grad = grad_tokens_ref[image].astype(f32) * keep
        grad_masked[image * cells : (image + 1) * cells, :] = grad.astype(bf16)
        sums = sums + fold(grad)
        position = position + grad
    sums_ref[...] = sums
    grad_position = weight_total.at[pl.ds(0, cells)]
    grad_position[...] = position
    position_rows = cells // (2 * PAIRS)
    position_total[...] = jnp.zeros_like(position_total)
    for block in range(2 * PAIRS):
        position_total[block, 0:position_rows, :] = grad_position[
            block * position_rows : (block + 1) * position_rows, :
        ]
    weight_total[...] = dot_tn(stem_ref[...].reshape(images * cells, channels), grad_masked[...])
    size = channels // (2 * PAIRS)
    for block in range(2 * PAIRS):
        blocks_ref[block, 0 : size // 8] = sections_of(weight_total[block * size : (block + 1) * size, :])
        blocks_ref[block, size // 8 :] = sections_of(position_total[block])


def embed_weights(image_class, grad_tokens, stem):
    images, cells, width = grad_tokens.shape
    channels = stem.shape[2]
    position_rows = -(-cells // (2 * PAIRS) // 8) * 8
    blocks = (2 * PAIRS, (channels // (2 * PAIRS) + position_rows) // 8, 8, width)
    return pl.pallas_call(
        embed_weights_kernel,
        out_shape=(
            jax.ShapeDtypeStruct(blocks, bf16),
            jax.ShapeDtypeStruct((8, width), f32),
        ),
        grid_spec=pltpu.PrefetchScalarGridSpec(
            num_scalar_prefetch=1,
            grid=(1,),
            in_specs=[whole(grad_tokens.shape), whole(stem.shape)],
            out_specs=[whole(blocks), whole((8, width))],
            scratch_shapes=[
                pltpu.VMEM((images * cells, width), bf16),
                pltpu.VMEM((channels, width), f32),
                pltpu.VMEM((2 * PAIRS, position_rows, width), f32),
            ],
        ),
        compiler_params=pltpu.CompilerParams(vmem_limit_bytes=62 * MIB),
        cost_estimate=cost(8_000_000_000, 8 * MIB),
        name="embed_weights",
    )(image_class, grad_tokens, stem)


def embed_backward_kernel(
    class_ref,
    grad_tokens_ref,
    x_ref,
    third_ref,
    stat3_ref,
    gain3_ref,
    bias3_ref,
    embed_ref,
    grad_inner_ref,
    grad_third_ref,
    sums3_ref,
    mask,
):
    image = pl.program_id(0)
    cells, channels = x_ref.shape[1:]
    chunk = cells
    steps = cells // chunk
    image_class = class_ref[image]
    mask[...] = validity_mask(image_class, cells)
    count = valid_count(image_class)

    @pl.when(image == 0)
    def _():
        sums3_ref[...] = jnp.zeros_like(sums3_ref)

    centre, scale = stat3_ref[0, 0:1, :], stat3_ref[0, 1:2, :]
    gain = line(gain3_ref)

    def third_step(step, carry):
        rows = rows_at(step, chunk)
        keep = spread_lanes(mask[rows, :], channels)
        grad = dot_nt(grad_tokens_ref[0, rows, :], embed_ref[...]) * keep
        normal = (third_ref[0, rows, :] - centre) * scale
        argument = x_ref[0, rows, :] * keep + normal * gain + line(bias3_ref)
        cdf, pdf = cdf_pdf(argument)
        grad = grad * (cdf + argument * pdf)
        grad_inner_ref[0, rows, :] = grad
        return carry[0] + fold(grad * normal), carry[1] + fold(grad)

    zeros = jnp.zeros((8, channels), f32)
    with_normal, plain = lax.fori_loop(0, steps, third_step, (zeros, zeros))
    sums3_ref[0] += with_normal
    sums3_ref[1] += plain
    mean, cross = norm_means((plain, with_normal), gain, channels // GROUPS, count)
    outer = scale * gain
    mean = mean * scale
    cross = cross * scale

    @pl.loop(0, steps)
    def _(step):
        rows = rows_at(step, chunk)
        keep = spread_lanes(mask[rows, :], channels)
        normal = (third_ref[0, rows, :] - centre) * scale
        grad = (grad_inner_ref[0, rows, :] * outer - mean - normal * cross) * keep
        grad_third_ref[0, rows, :] = grad.astype(bf16)


def embed_backward(image_class, grad_tokens, x, third, stat3, gain3, bias3, embed):
    images, cells, channels = x.shape
    width = embed.shape[1]
    return pl.pallas_call(
        embed_backward_kernel,
        out_shape=(
            jax.ShapeDtypeStruct((images, cells, channels), f32),
            jax.ShapeDtypeStruct((images, cells, channels), bf16),
            jax.ShapeDtypeStruct((2, 8, channels), f32),
        ),
        grid_spec=pltpu.PrefetchScalarGridSpec(
            num_scalar_prefetch=1,
            grid=(images,),
            in_specs=[
                per_image((cells, width)),
                per_image((cells, channels)),
                per_image((cells, channels)),
                per_image((8, channels)),
                whole((channels,)),
                whole((channels,)),
                whole((channels, width)),
            ],
            out_specs=[
                per_image((cells, channels)),
                per_image((cells, channels)),
                whole((2, 8, channels)),
            ],
            scratch_shapes=[
                pltpu.VMEM((cells, LANES), f32),
            ],
        ),
        compiler_params=pltpu.CompilerParams(vmem_limit_bytes=62 * MIB),
        cost_estimate=cost(20_000_000_000, 30 * MIB),
        name="embed_backward",
    )(image_class, grad_tokens, x, third, stat3, gain3, bias3, embed)


def convs_backward_kernel(
    class_ref,
    core_ref,
    grad_third_ref,
    x_ref,
    first_ref,
    second_ref,
    stat1_ref,
    stat2_ref,
    std_in_ref,
    std_mid_ref,
    std_out_ref,
    w_in_ref,
    w_mid_ref,
    w_out_ref,
    gain1_ref,
    bias1_ref,
    gain2_ref,
    bias2_ref,
    sums_embed_ref,
    sums3_ref,
    sums_attn_ref,
    sums_expand_ref,
    sums_shrink_ref,
    sums_mix_ref,
    sums_attend0_ref,
    sums_attend1_ref,
    arrived_ref,
    grad_first_ref,
    mine_ref,
    other_ref,
    output_ref,
    vectors,
    sums1,
    sums2,
    mask,
    act,
    padded,
    columns,
    in_total,
    mid_total,
    out_total,
    mid_done,
    in_done,
):
    image = pl.program_id(0)
    last = pl.num_programs(0) - 1
    output_ref[...] = arrived_ref[...]
    cells, channels = x_ref.shape[1:]
    width = sums_embed_ref.shape[1]
    middle = first_ref.shape[2]
    image_class = class_ref[image]
    mask[...] = validity_mask(image_class, cells)
    count = valid_count(image_class)

    @pl.when(image == 0)
    def _():
        for ref in (sums1, sums2, in_total, mid_total, out_total):
            ref[...] = jnp.zeros_like(ref)

    def middle_norm(values_ref, stat_ref, gain_ref, bias_ref, sums_ref, grad_of):
        centre, scale = stat_ref[0, 0:1, :], stat_ref[0, 1:2, :]
        gain = line(gain_ref)
        keep = spread_lanes(mask[...], middle)
        normal = (values_ref[0] - centre) * scale
        argument = normal * gain + line(bias_ref)
        cdf, pdf = cdf_pdf(argument)
        act[...] = (argument * cdf * keep).astype(bf16)
        grad = grad_of() * keep * (cdf + argument * pdf)
        plain, with_normal = fold(grad), fold(grad * normal)
        sums_ref[0] += with_normal
        sums_ref[1] += plain
        mean, cross = norm_means((plain, with_normal), gain, middle // GROUPS, count)
        return (grad * (scale * gain) - mean * scale - normal * (cross * scale)) * keep

    grad_second = middle_norm(
        second_ref,
        stat2_ref,
        gain2_ref,
        bias2_ref,
        sums2,
        lambda: dot_nt(grad_third_ref[0], std_out_ref[...]),
    )
    out_total[...] += dot_tn(act[...], grad_third_ref[0])
    fill_columns(grad_second, padded, columns, -1)

    def spread_back():
        grad = jnp.zeros((cells, middle), f32)
        for tap in range(9):
            part = slice(tap * middle, (tap + 1) * middle)
            grad = grad + dot_nt(columns[:, part], std_mid_ref[part, :])
        return grad

    grad = middle_norm(first_ref, stat1_ref, gain1_ref, bias1_ref, sums1, spread_back)
    grad_low = grad.astype(bf16)
    grad_first_ref[0] = grad_low
    mid_total[...] += dot_tn(act[...], columns[...])
    low = (x_ref[0] * spread_lanes(mask[...], channels)).astype(bf16)
    in_total[...] += dot_tn(grad_low, low)

    @pl.when(image == last)
    def _():
        core = core_ref[0]
        out_total[...] = standardize_back(w_out_ref[...].astype(f32), out_total[...])
        in_done[...] = standardize_back(w_in_ref[...].astype(f32), in_total[...].T)
        rows = 9 * middle
        normal, scale = standardized(w_mid_ref[...].astype(f32))
        grads = [mid_total[:, tap * middle : (tap + 1) * middle] for tap in range(9)]
        grad_mean = sum(total(g) for g in grads) * (1.0 / rows)
        inner = sum(
            total(g * normal[tap * middle : (tap + 1) * middle]) for tap, g in enumerate(grads)
        ) * (1.0 / rows)
        for tap, g in enumerate(grads):
            part = slice(tap * middle, (tap + 1) * middle)
            mid_done[part, :] = scale * (g - grad_mean - normal[part] * inner)
        in_size = channels // (2 * PAIRS)
        mid_size = rows // (2 * PAIRS)
        out_size = middle // (2 * PAIRS)
        in_parts = in_size // 8
        mid_parts = mid_size // 8
        for pair in range(PAIRS):
            for ref, side in ((mine_ref, core), (other_ref, 1 - core)):
                block = 2 * pair + side
                at = pl.ds(pl.multiple_of(block * in_size, 8), in_size)
                ref[pair, 0:in_parts] = sections_of(in_done[at, :])
                at = pl.ds(pl.multiple_of(block * mid_size, 8), mid_size)
                ref[pair, in_parts : in_parts + mid_parts] = sections_of(mid_done[at, :])
                at = pl.ds(pl.multiple_of(block * out_size, 8), out_size)
                for k in range(channels // middle):
                    ref[pair, in_parts + mid_parts + k] = out_total[
                        at, k * middle : (k + 1) * middle
                    ].astype(bf16)
        vectors[...] = jnp.zeros_like(vectors)
        row = 0
        for item in (
            total(sums_embed_ref[...]),
            total(sums_attn_ref[0]),
            total(sums_attn_ref[1]),
            total(sums1[0]),
            total(sums1[1]),
            total(sums2[0]),
            total(sums2[1]),
            total(sums3_ref[0]),
            total(sums3_ref[1]),
            total(sums_expand_ref[...]),
            total(sums_shrink_ref[...]),
            total(sums_mix_ref[0]),
            total(sums_mix_ref[1]),
            total(sums_mix_ref[2]),
            total(sums_attend0_ref[0] + sums_attend1_ref[0]),
            total(sums_attend0_ref[1] + sums_attend1_ref[1]),
        ):
            for start in range(0, item.shape[1], middle):
                vectors[row : row + 1, :] = item[:, start : start + middle]
                row += 1
        mine_ref[PAIRS] = jnp.zeros(mine_ref.shape[1:], bf16)
        store_split(mine_ref.at[PAIRS], 0, vectors[...])
        other_ref[PAIRS] = mine_ref[PAIRS]


def convs_backward(
    image_class,
    core,
    grad_third,
    x,
    first,
    second,
    stat1,
    stat2,
    stds,
    weights,
    norms,
    sums_embed,
    sums3,
    sums_attn,
    sums_block,
    arrived,
):
    images, cells, channels = x.shape
    middle = first.shape[2]
    width = sums_embed.shape[1]
    row = lambda size: whole((size,))
    conv_rows = channels // (2 * PAIRS) + 9 * middle // (2 * PAIRS) + middle // (2 * PAIRS) * (channels // middle)
    half = (PAIRS + 1, conv_rows // 8, 8, middle)
    slot_spec = pl.BlockSpec(
        (arrived.shape[0] // images,) + arrived.shape[1:], lambda image, *_: (image, 0, 0)
    )
    return pl.pallas_call(
        convs_backward_kernel,
        out_shape=(
            jax.ShapeDtypeStruct((images, cells, middle), bf16),
            jax.ShapeDtypeStruct(half, bf16),
            jax.ShapeDtypeStruct(half, bf16),
            jax.ShapeDtypeStruct(arrived.shape, bf16),
        ),
        grid_spec=pltpu.PrefetchScalarGridSpec(
            num_scalar_prefetch=2,
            grid=(images,),
            in_specs=[
                per_image((cells, channels)),
                per_image((cells, channels)),
                per_image((cells, middle)),
                per_image((cells, middle)),
                per_image((8, middle)),
                per_image((8, middle)),
                whole((channels, middle)),
                whole((9 * middle, middle)),
                whole((middle, channels)),
                whole((channels, middle)),
                whole((9 * middle, middle)),
                whole((middle, channels)),
                row(middle),
                row(middle),
                row(middle),
                row(middle),
                whole((8, width)),
                whole((2, 8, channels)),
                whole((2, 8, width)),
                *[whole(item.shape) for item in sums_block],
                slot_spec,
            ],
            out_specs=[
                per_image((cells, middle)),
                whole(half),
                whole(half),
                slot_spec,
            ],
            scratch_shapes=[
                pltpu.VMEM((VECTORS * 8, middle), f32),
                pltpu.VMEM((2, 8, middle), f32),
                pltpu.VMEM((2, 8, middle), f32),
                pltpu.VMEM((cells, LANES), f32),
                pltpu.VMEM((cells, middle), bf16),
                pltpu.VMEM((3, cells + 2 * SIDE, middle), f32),
                pltpu.VMEM((cells, 9 * middle), bf16),
                pltpu.VMEM((middle, channels), f32),
                pltpu.VMEM((middle, 9 * middle), f32),
                pltpu.VMEM((middle, channels), f32),
                pltpu.VMEM((9 * middle, middle), f32),
                pltpu.VMEM((channels, middle), f32),
            ],
        ),
        compiler_params=pltpu.CompilerParams(vmem_limit_bytes=62 * MIB),
        cost_estimate=cost(20_000_000_000, 20 * MIB),
        name="convs_backward",
    )(
        image_class,
        core,
        grad_third,
        x,
        first,
        second,
        stat1,
        stat2,
        *stds,
        *weights,
        *norms[:4],
        sums_embed,
        sums3,
        sums_attn,
        *sums_block,
        arrived,
    )


def input_backward_kernel(class_ref, grad_inner_ref, grad_first_ref, std_in_ref, input_grad_ref):
    cells, channels = grad_inner_ref.shape[1:]
    keep = spread_lanes(validity_mask(class_ref[pl.program_id(0)], cells), channels)
    back = dot_nt(grad_first_ref[0], std_in_ref[...])
    input_grad_ref[0] = (grad_inner_ref[0] + back) * keep


def input_backward(image_class, grad_inner, grad_first, std_in):
    images, cells, channels = grad_inner.shape
    middle = grad_first.shape[2]
    return pl.pallas_call(
        input_backward_kernel,
        out_shape=jax.ShapeDtypeStruct((images, cells, channels), f32),
        grid_spec=pltpu.PrefetchScalarGridSpec(
            num_scalar_prefetch=1,
            grid=(images,),
            in_specs=[
                per_image((cells, channels)),
                per_image((cells, middle)),
                whole((channels, middle)),
            ],
            out_specs=per_image((cells, channels)),
        ),
        compiler_params=pltpu.CompilerParams(vmem_limit_bytes=62 * MIB),
        cost_estimate=cost(2 * images * cells * channels * middle, 12 * MIB),
        name="input_backward",
    )(image_class, grad_inner, grad_first, std_in)


def combine_core_kernel(plane_ref, *refs, arrays, extra):
    mines, others, outs = refs[:arrays], refs[arrays : 2 * arrays], refs[2 * arrays :]
    start = 0
    for mine, other in zip(mines, others):
        size = mine.shape[1]
        for z in range(mine.shape[0] // 4):
            for q in range(4):
                at = 4 * z + lax.bitwise_xor(plane_ref[0], q)
                summed = mine[at].astype(f32) + other[at].astype(f32)
                outs[q][z, start : start + size] = summed.astype(bf16)
        start += size
    if extra:
        vectors = load_split(mines[0].at[PAIRS], 0) + load_split(others[0].at[PAIRS], 0)
        for out in outs:
            out[PAIRS // 4] = jnp.zeros(out.shape[1:], bf16)
            store_split(out.at[PAIRS // 4], 0, vectors)


def combine_core(plane, mines, others, extra):
    arrays = len(mines)
    depth = PAIRS // 4
    steps = 1 if extra else depth
    out_shape = (sum(item.shape[1] for item in mines),) + mines[0].shape[2:]
    in_spec = lambda item: pl.BlockSpec(
        (item.shape[0] // steps,) + item.shape[1:], lambda step, *_: (step, 0, 0, 0)
    )
    out_spec = pl.BlockSpec(((depth + extra) // steps,) + out_shape, lambda step, *_: (step, 0, 0, 0))
    size = sum(item.size for item in mines)
    return pl.pallas_call(
        lambda *refs: combine_core_kernel(*refs, arrays=arrays, extra=extra),
        out_shape=[jax.ShapeDtypeStruct((depth + extra,) + out_shape, bf16)] * 4,
        grid_spec=pltpu.PrefetchScalarGridSpec(
            num_scalar_prefetch=1,
            grid=(steps,),
            in_specs=[in_spec(item) for item in mines] * 2,
            out_specs=[out_spec] * 4,
        ),
        compiler_params=pltpu.CompilerParams(vmem_limit_bytes=62 * MIB),
        cost_estimate=cost(size, 6 * size),
        name="combine_core",
    )(plane, *mines, *others)


def split_two_kernel(bits_ref, *refs, modes):
    count = len(modes)
    outs = refs[2 * count :]
    for k, (inner, bit) in enumerate(modes):
        left, right = refs[2 * k], refs[2 * k + 1]
        for at in range(left.shape[0] // 2):
            base = at // inner * 2 * inner + at % inner
            for q in range(2):
                here = base + inner * lax.bitwise_xor(bits_ref[bit], q)
                summed = left[here].astype(f32) + right[here].astype(f32)
                outs[2 * k + q][at] = summed.astype(bf16)


def split_two(bits, pairs, modes, steps):
    flat = [item for pair in pairs for item in pair]
    spec = lambda shape: pl.BlockSpec(
        (shape[0] // steps,) + shape[1:], lambda step, *_: (step, 0, 0, 0)
    )
    half = lambda item: (item.shape[0] // 2,) + item.shape[1:]
    outs = [jax.ShapeDtypeStruct(half(pair[0]), bf16) for pair in pairs for _ in range(2)]
    size = sum(item.size for item in flat)
    return pl.pallas_call(
        lambda *refs: split_two_kernel(*refs, modes=modes),
        out_shape=outs,
        grid_spec=pltpu.PrefetchScalarGridSpec(
            num_scalar_prefetch=1,
            grid=(steps,),
            in_specs=[spec(item.shape) for item in flat],
            out_specs=[spec(item.shape) for item in outs],
        ),
        compiler_params=pltpu.CompilerParams(vmem_limit_bytes=62 * MIB),
        cost_estimate=cost(size, 3 * size),
        name="split_two",
    )(bits, *flat)


def split_merged_kernel(bits_ref, *refs, bit):
    outs = refs[-2:]
    start = 0
    for k in range(len(refs) // 2 - 1):
        left, right = refs[2 * k], refs[2 * k + 1]
        size = left.shape[1]
        for at in range(left.shape[0] // 2):
            for q in range(2):
                here = 2 * at + lax.bitwise_xor(bits_ref[bit], q)
                summed = left[here].astype(f32) + right[here].astype(f32)
                outs[q][at, start : start + size] = summed.astype(bf16)
        start += size


def split_merged(bits, pairs, bit):
    flat = [item for pair in pairs for item in pair]
    shape = (flat[0].shape[0] // 2, sum(pair[0].shape[1] for pair in pairs)) + flat[0].shape[2:]
    size = sum(item.size for item in flat)
    return pl.pallas_call(
        lambda *refs: split_merged_kernel(*refs, bit=bit),
        out_shape=[jax.ShapeDtypeStruct(shape, bf16)] * 2,
        grid_spec=pltpu.PrefetchScalarGridSpec(
            num_scalar_prefetch=1,
            grid=(1,),
            in_specs=[whole(item.shape) for item in flat],
            out_specs=[whole(shape)] * 2,
        ),
        compiler_params=pltpu.CompilerParams(vmem_limit_bytes=62 * MIB),
        cost_estimate=cost(size, 3 * size),
        name="split_merged",
    )(bits, *flat)


def four(values):
    if len(values) == 1:
        return values[0]
    if len(values) == 2:
        return values[0] + values[1]
    return (values[0] + values[1]) + (values[2] + values[3])


def combine_plane_kernel(depth_ref, *refs, extra, beside):
    parts, outs = refs[:4], refs[4 + beside :]
    size = parts[0].shape[1]
    columns = parts[0].shape[3]
    for q in range(4):
        at = lax.bitwise_xor(depth_ref[0], q)
        outs[q][0:size] = four([part[at].astype(f32) for part in parts]).astype(bf16)
        if beside:
            summed = refs[4][at].astype(f32) + refs[5][at].astype(f32)
            start = size + 2 * VECTORS * extra
            for section in range(summed.shape[0]):
                for k in range(summed.shape[2] // columns):
                    outs[q][start] = summed[section, :, k * columns : (k + 1) * columns].astype(bf16)
                    start += 1
    if extra:
        vectors = four([load_split(part.at[PAIRS // 4], 0) for part in parts])
        for out in outs:
            store_split(out, size, vectors)


def combine_plane(depth, parts, extra, beside=()):
    columns = parts[0].shape[3]
    sections = parts[0].shape[1] + 2 * VECTORS * extra
    if beside:
        sections += beside[0].shape[1] * (beside[0].shape[3] // columns)
    shape = (sections,) + parts[0].shape[2:]
    flat = list(parts) + list(beside)
    size = sum(item.size for item in flat)
    return pl.pallas_call(
        lambda *refs: combine_plane_kernel(*refs, extra=extra, beside=len(beside)),
        out_shape=[jax.ShapeDtypeStruct(shape, bf16)] * 4,
        grid_spec=pltpu.PrefetchScalarGridSpec(
            num_scalar_prefetch=1,
            grid=(1,),
            in_specs=[whole(item.shape) for item in flat],
            out_specs=[whole(shape)] * 4,
        ),
        compiler_params=pltpu.CompilerParams(vmem_limit_bytes=62 * MIB),
        cost_estimate=cost(size, 3 * size),
        name="combine_plane",
    )(depth, *flat)


def store_lines(outs, vectors, lines):
    for out, pieces in zip(outs, lines):
        out[...] = jnp.concatenate(
            [vectors[row : row + 1, 0:size] for row, size in pieces], axis=1
        ).reshape(-1)


def line_shapes(lines):
    return [jax.ShapeDtypeStruct((sum(size for _, size in pieces),), f32) for pieces in lines]


def combine_depth_kernel(*refs, batches):
    outs = refs[sum(count for count, _, _, _ in batches) :]
    first = first_out = 0
    for count, places, sizes, lines in batches:
        parts = refs[first : first + count]
        here = outs[first_out : first_out + sizes + len(lines)]
        summed = four([part[...].astype(f32) for part in parts])
        for section, place in enumerate(places):
            if place is None:
                continue
            out, row, column, columns, rows = place
            stride = columns // LANES
            for lane in range(summed.shape[2] // LANES):
                start = row * stride + column // LANES + lane
                here[out][pl.ds(start, rows, stride=stride), :] = summed[
                    section, 0:rows, lane * LANES : (lane + 1) * LANES
                ]
        if lines:
            vectors = four([load_split(part, places.index(None)) for part in parts])
            store_lines(here[sizes:], vectors, lines)
        first += count
        first_out += sizes + len(lines)


def combine_depth(batches):
    flat = [item for parts, _, _, _ in batches for item in parts]
    shapes = []
    for _, _, sizes, lines in batches:
        shapes += [jax.ShapeDtypeStruct((size // LANES, LANES), f32) for size in sizes]
        shapes += line_shapes(lines)
    size = sum(item.size for item in flat)
    known = [(len(parts), places, len(sizes), lines) for parts, places, sizes, lines in batches]
    outs = pl.pallas_call(
        lambda *refs: combine_depth_kernel(*refs, batches=known),
        out_shape=shapes,
        grid=(1,),
        in_specs=[whole(item.shape) for item in flat],
        out_specs=[whole(item.shape) for item in shapes],
        compiler_params=pltpu.CompilerParams(vmem_limit_bytes=62 * MIB),
        cost_estimate=cost(size, 3 * size),
        name="combine_depth",
    )(*flat)
    return [item.reshape(-1) for item in outs]


def permuted(item, distance, devices):
    return lax.ppermute(item, BOTH, [(k, k ^ distance) for k in range(devices)])


class Sums:
    def __init__(self, index, devices):
        self.devices = devices
        self.plane = ((index // 2) % 4).astype(jnp.int32).reshape(1)
        self.depth = (index // 8).astype(jnp.int32).reshape(1)
        self.bits = jnp.stack([index // unit % 2 for unit in (4, 2, 8, 16)]).astype(jnp.int32)

    def spread(self, parts, unit):
        return [parts[0]] + [permuted(parts[q], q * unit, self.devices) for q in (1, 2, 3)]

    def start_core(self, mines, others):
        return mines, [permuted(item, 1, self.devices) for item in others]

    def end_core(self, started, extra=0):
        return combine_core(self.plane, *started, extra)

    def halves(self, pairs, modes, distances, steps):
        outs = split_two(self.bits, pairs, modes, steps)
        return [
            (outs[2 * k], permuted(outs[2 * k + 1], distance, self.devices))
            for k, distance in enumerate(distances)
        ]

    def start_plane(self, parts):
        return self.spread(parts, 2)

    def merged(self, pairs, bit, distance):
        keep, send = split_merged(self.bits, pairs, bit)
        return keep, permuted(send, distance, self.devices)

    def end_plane(self, started, extra=0, beside=()):
        return combine_plane(self.depth, started, extra, beside)

    def start_depth(self, parts):
        return self.spread(parts, 8)


def after(value, *others):
    return lax.optimization_barrier((value,) + others)[0]


def ahead(value, others):
    leaves, tree = jax.tree.flatten(others)
    held = lax.optimization_barrier((value, leaves))
    return jax.tree.unflatten(tree, held[1])


def octets(out, rows, columns, width, offset=0):
    return [
        (out, 8 * part, start, columns, min(8, rows - 8 * part))
        for start in range(0, columns, width)
        for part in range(-(-rows // 8))
    ]


def scattered(mine, other, places, sizes, devices):
    blocks = jnp.stack([mine, other], axis=1).reshape((2 * PAIRS,) + mine.shape[1:])
    return scattered_blocks(blocks, places, sizes, devices)


def scattered_blocks(blocks, places, sizes, devices):
    results = []
    for out, size in sizes:
        chosen = [k for k, place in enumerate(places) if place[0] == out]
        columns = places[chosen[0]][3]
        width = blocks.shape[-1]
        rows = size // columns
        groups = columns // width
        values = blocks[:, chosen[0] : chosen[-1] + 1]
        values = values.reshape(2 * PAIRS, groups, -1, width)[:, :, :rows]
        values = jnp.moveaxis(values, 1, 2).reshape(devices, -1)
        length = values.shape[1]
        padded = -(-length // LANES) * LANES
        values = jnp.pad(values, ((0, 0), (0, padded - length))).reshape(devices, -1, LANES)
        own = lax.psum_scatter(values, BOTH, scatter_dimension=0, tiled=True)
        results.append(own.astype(f32).reshape(-1)[:length])
    return results


def shards(
    stem_input,
    image_class,
    owner,
    conv_in_weight,
    first_gain,
    first_bias,
    conv_mid_weight,
    second_gain,
    second_bias,
    conv_out_weight,
    third_gain,
    third_bias,
    embed_weight,
    embed_bias,
    position_table,
    attn_gain,
    attn_bias,
    joint_weight,
    query_bias,
    value_bias,
    mix_weight,
    mix_bias,
    mlp_gain,
    mlp_bias,
    expand_weight,
    expand_bias,
    shrink_weight,
    shrink_bias,
    cotangent,
):
    sections = lax.axis_size("section")
    devices = sections * lax.axis_size("batch")
    staged = (devices, sections) == (2 * PAIRS, 4)
    index = lax.axis_index(BOTH)
    images, cells, channels = stem_input.shape
    middle = conv_in_weight.shape[1]
    width = embed_weight.shape[1]
    inner = expand_weight.shape[1]
    section_index = lax.axis_index("section")
    mine = lax.dynamic_index_in_dim(owner.reshape(sections, images), section_index, 0, keepdims=False)
    core = ((index % 2) if staged else jnp.zeros((), jnp.int32)).astype(jnp.int32).reshape(1)
    received = lax.all_to_all(cotangent[0], "section", split_axis=0, concat_axis=0, tiled=True)
    norms = (first_gain, first_bias, second_gain, second_bias, third_gain, third_bias)
    weights = (conv_in_weight, conv_mid_weight.reshape(-1, middle), conv_out_weight)
    std_in, std_mid, std_out, first, second, third, stat1, stat2, stat3, stem, tokens = stem_forward(
        image_class, stem_input, *weights, norms, embed_weight, embed_bias, position_table
    )
    normed, query, key, value, log_total, mixed, resid, normed_two = attend_forward(
        image_class,
        tokens,
        attn_gain,
        attn_bias,
        joint_weight,
        query_bias,
        value_bias,
        mix_weight,
        mix_bias,
        mlp_gain,
        mlp_bias,
    )
    (
        outgoing,
        grad_resid,
        grad_mixed,
        shrink_mine,
        shrink_other,
        expand_mine,
        expand_other,
        sums_expand,
        sums_shrink,
        sums_mix,
    ) = feed(
        image_class,
        mine,
        core,
        normed_two,
        resid,
        received,
        expand_weight,
        expand_bias,
        shrink_weight,
        shrink_bias,
        mlp_gain,
        mix_weight,
    )
    sums = Sums(index, devices)
    if staged:
        feed_core = sums.start_core([shrink_mine, expand_mine], [shrink_other, expand_other])
    arrived = lax.all_to_all(outgoing, "section", split_axis=0, concat_axis=0, tiled=True)
    grad_joint0, sums_attend0 = attend_backward(
        0, image_class, query, key, value, log_total, grad_mixed
    )
    if staged:
        feed_core = ahead(grad_joint0, feed_core)
        feed_half = sums.halves(
            list(zip(*feed_core)), ((2, 0), (1, 1)), (4, 2), 4
        )
        grad_mixed = after(grad_mixed, feed_half[0][0])
    grad_joint1, sums_attend1 = attend_backward(
        1, image_class, query, key, value, log_total, grad_mixed
    )
    grad_tokens, joint_mine, joint_other, sums_attn = joint_backward(
        core,
        tokens,
        normed,
        mixed,
        grad_resid,
        grad_joint0,
        grad_joint1,
        attn_gain,
        joint_weight,
    )
    if staged:
        feed_half, arrived, joint_other = ahead(grad_tokens, (feed_half, arrived, joint_other))
        joint_other = after(joint_other, *feed_half[0], *feed_half[1], arrived)
        joint_core = sums.start_core([joint_mine], [joint_other])
        feed_quarter = sums.halves(feed_half, ((1, 1), (1, 0)), (2, 4), 4)
        grad_tokens = after(grad_tokens, feed_quarter[0][0])
    embed_blocks, sums_embed = embed_weights(image_class, grad_tokens, stem)
    if staged:
        embed_own = lax.psum_scatter(embed_blocks, BOTH, scatter_dimension=0, tiled=True)
    if staged:
        joint_core, feed_quarter, grad_tokens = (
            ahead(embed_blocks, joint_core),
            feed_quarter,
            ahead(embed_blocks, grad_tokens),
        )
        joint_parts = sums.end_core(joint_core)
        feed_quarter = ahead(joint_parts[0], feed_quarter)
        joint_plane = sums.start_plane(joint_parts)
        feed_eighth = sums.merged(feed_quarter, 2, 8)
        grad_tokens = after(grad_tokens, joint_plane[0], feed_eighth[0])
    grad_inner, grad_third, sums3 = embed_backward(
        image_class,
        grad_tokens,
        stem_input,
        third,
        stat3,
        third_gain,
        third_bias,
        embed_weight,
    )
    if staged:
        feed_eighth = ahead(grad_third, feed_eighth)
        feed_last = sums.merged([feed_eighth], 3, 16)
        joint_plane = ahead(feed_last[0], joint_plane)
        joint_depth = sums.start_depth(sums.end_plane(joint_plane))
        grad_third = after(grad_third, joint_depth[0], feed_last[0])
    grad_first, conv_mine, conv_other, block_output = convs_backward(
        image_class,
        core,
        grad_third,
        stem_input,
        first,
        second,
        stat1,
        stat2,
        (std_in, std_mid, std_out),
        weights,
        norms,
        sums_embed,
        sums3,
        sums_attn,
        (sums_expand, sums_shrink, sums_mix, sums_attend0, sums_attend1),
        arrived,
    )
    block_output = block_output[None]
    if staged:
        feed_last, joint_depth = ahead(grad_first, (feed_last, joint_depth))
        conv_other = after(conv_other, *feed_last, *joint_depth)
        conv_core = sums.start_core([conv_mine], [conv_other])
    input_grad = input_backward(image_class, grad_inner, grad_first, std_in)

    parts = 2 * PAIRS
    shrink_places = octets(0, inner // parts, width, width)
    expand_places = octets(1, width // parts, inner, width)
    feed_sizes = [inner // parts * width] * 2
    joint_places = octets(0, width // parts, 3 * width, width) + octets(1, width // parts, width, width)
    joint_sizes = [3 * width * width // parts, width * width // parts]
    embed_places = octets(0, channels // parts, width, width) + octets(1, cells // parts, width, width)
    embed_sizes = [channels * width // parts, cells * width // parts]
    conv_places = (
        octets(0, channels // parts, middle, middle)
        + octets(1, 9 * middle // parts, middle, middle)
        + octets(2, middle // parts, channels, middle)
    )
    conv_sizes = [
        channels * middle // parts,
        9 * middle * middle // parts,
        middle * channels // parts,
    ]
    stem_lines = []
    row = 0
    for size in [width] * 3 + [middle] * 4 + [channels] * 2 + [inner] + [width] * 6:
        stem_lines.append([(row + k, middle) for k in range(size // middle)])
        row += size // middle
    if staged:
        conv_plane = sums.start_plane(sums.end_core(conv_core, 1))
        grad_shrink, grad_expand, grad_joint, grad_mix = combine_depth(
            [
                ([item[0] for item in feed_last], shrink_places + expand_places, feed_sizes, []),
                (joint_depth, joint_places, joint_sizes, []),
            ]
        )
        conv_plane = ahead((input_grad, grad_shrink), conv_plane)
        last_depth = sums.start_depth(sums.end_plane(conv_plane, 1))
        grad_embed, grad_position, *grads = combine_depth(
            [
                ([embed_own[0]], embed_places, embed_sizes, []),
                (last_depth, conv_places + [None] * (2 * VECTORS), conv_sizes, stem_lines),
            ]
        )
        grad_in, grad_mid, grad_out = grads[:3]
        stem_vectors = grads[3:]
    else:
        (grad_shrink,) = scattered(
            shrink_mine, shrink_other, shrink_places, [(0, feed_sizes[0])], devices
        )
        (grad_expand,) = scattered(
            expand_mine, expand_other, expand_places, [(1, feed_sizes[1])], devices
        )
        grad_joint, grad_mix = scattered(
            joint_mine, joint_other, joint_places, list(enumerate(joint_sizes)), devices
        )
        grad_embed, grad_position = scattered_blocks(
            embed_blocks, embed_places, list(enumerate(embed_sizes)), devices
        )
        rows = conv_mine[PAIRS, :VECTORS].astype(f32) + conv_mine[PAIRS, VECTORS : 2 * VECTORS].astype(f32)
        rows = lax.psum(rows.reshape(-1, middle), BOTH)
        stem_vectors = [rows[pieces[0][0] : pieces[-1][0] + 1].reshape(-1) for pieces in stem_lines]
        conv_mine, conv_other = conv_mine[:PAIRS], conv_other[:PAIRS]
        grad_in, grad_mid, grad_out = scattered(
            conv_mine, conv_other, conv_places, list(enumerate(conv_sizes)), devices
        )
    (
        grad_embed_bias,
        grad_attn_gain,
        grad_attn_bias,
        grad_first_gain,
        grad_first_bias,
        grad_second_gain,
        grad_second_bias,
        grad_third_gain,
        grad_third_bias,
        grad_expand_bias,
        grad_shrink_bias,
        grad_mlp_gain,
        grad_mlp_bias,
        grad_mix_bias,
        grad_query_bias,
        grad_value_bias,
    ) = stem_vectors
    return (
        block_output,
        input_grad,
        grad_in,
        grad_first_gain,
        grad_first_bias,
        grad_mid,
        grad_second_gain,
        grad_second_bias,
        grad_out,
        grad_third_gain,
        grad_third_bias,
        grad_embed,
        grad_embed_bias,
        grad_position,
        grad_attn_gain,
        grad_attn_bias,
        grad_joint,
        grad_query_bias,
        grad_value_bias,
        grad_mix,
        grad_mix_bias,
        grad_mlp_gain,
        grad_mlp_bias,
        grad_expand,
        grad_expand_bias,
        grad_shrink,
        grad_shrink_bias,
    )


def solution(mesh):
    split = P(BOTH)
    images = P(BOTH, None, None)
    slots = P(BOTH, None, None, None)
    full = P()
    in_specs = (images, split, P("batch")) + (full,) * 25 + (slots,)
    out_specs = (
        slots,
        images,
        split,
        full,
        full,
        split,
        full,
        full,
        split,
        full,
        full,
        split,
        full,
        split,
        full,
        full,
        split,
        full,
        full,
        split,
        full,
        full,
        full,
        split,
        full,
        split,
        full,
    )
    return jax.shard_map(shards, mesh=mesh, in_specs=in_specs, out_specs=out_specs, check_vma=False)
```
